32 devices in a mesh: groups: 2 (over x), img: 16 (over z, y, core).
Axes of the slice: x: 2, y: 2, z: 4, core: 2. Of those that a mesh axis runs over, the one named last changes fastest.
Arguments:
- images: bfloat16 [256, 4608], P(('groups', 'img')), parts along dimension 0, may hold values from -64 to 64
- class_refs: bfloat16 [96, 4608], P('groups', 'img'), parts along dimension 0, may hold values from -0.6 to 0.6
- sigma2: float32 [32, 16], P('groups'), parts along dimension 0, may hold values from 0.5 to 18
- ctf_group: int32 [256], P(('groups', 'img')), parts along dimension 0, may hold values from 0 to 15, as said below
- defocus_bin: int32 [256], P(('groups', 'img')), parts along dimension 0, may hold values from 0 to 31
Outputs:
- new_refs: float32 [96, 4608], P('groups', 'img'), parts along dimension 0
The draws below stay inside these ranges and needn't reach their ends.
There are 2 independent parts, one for each index of `groups`. The reference program is written for one: setup_inputs(seed, part) draws one part's arguments, and reference() takes and returns one part's arrays. A program takes and returns all parts, laid end to end along the dimension named above; each array names one. Nothing has to cross between parts.
Inputs may be any that keep to these rules, and one draw needn't show every extreme that they name: `ctf_group`: never falls from one image to the next; every group appears.
All inputs are finite; a program needn't handle non-finite values.
Results may differ from the reference program's by a relative error of at most 0.0084.
Values may be sent and summed in bfloat16 or wider, within the bound.
No kernel may reach another device: no remote copies, remote signals or barrier semaphores. Data moves between devices by JAX's collectives and lax.ppermute only.
A program may use at most 128 MiB of HBM per device.

```python
import math
import jax
import jax.numpy as jnp
from jax import lax

CLASSES = 48
ROT = 36
SHELLS = 16
ANG = 144
REACH = 3
SHIFTS = 49
BINS = 32
NGROUP = 16
IMAGES = 128


def group_ids(key):
    extra = jax.random.randint(jax.random.fold_in(key, 11), (IMAGES - NGROUP,), 0, NGROUP)
    joined = jnp.concatenate([jnp.arange(NGROUP, dtype=jnp.int32), extra.astype(jnp.int32)])
    return jnp.sort(joined)


def bin_ids(key):
    return jax.random.randint(jax.random.fold_in(key, 13), (IMAGES,), 0, BINS).astype(jnp.int32)


def noise_table(key, rise):
    level = jnp.arange(NGROUP, dtype=jnp.float32) / max(NGROUP - 1, 1)
    base = jnp.exp(jax.random.uniform(jax.random.fold_in(key, 17), (NGROUP, SHELLS), jnp.float32, math.log(0.5), math.log(2.0)))
    return base * rise ** level[:, None]


def reference_table(key):
    values = jax.random.normal(jax.random.fold_in(key, 21), (CLASSES, 2, SHELLS, ANG), jnp.float32)
    return 0.1 * jnp.clip(values, -6.0, 6.0)


def draw_ctf_group(key, part):
    return group_ids(key)


def draw_defocus_bin(key, part):
    return bin_ids(key)


def draw_sigma2(key, part):
    return noise_table(key, 3.0)


def draw_class_refs(key, part):
    table = reference_table(key)
    return table.reshape(CLASSES, 2 * SHELLS * ANG).astype(jnp.bfloat16)


def draw_images(key, part):
    values = jax.random.normal(jax.random.fold_in(key, 31), (IMAGES, 2 * SHELLS * ANG), jnp.float32)
    return jnp.clip(values, -6.0, 6.0).astype(jnp.bfloat16)


def setup_inputs(seed: int = 0, part: int = 0) -> dict:
    keys = jax.random.split(jax.random.key(seed), 6)
    part_keys = jax.random.split(jax.random.fold_in(keys[5], part), 6)
    images = draw_images(jax.random.fold_in(jax.random.fold_in(keys[5], part), 71), part)
    class_refs = draw_class_refs(jax.random.fold_in(jax.random.fold_in(keys[5], part), 71), part)
    sigma2 = draw_sigma2(jax.random.fold_in(jax.random.fold_in(keys[5], part), 71), part)
    ctf_group = draw_ctf_group(jax.random.fold_in(jax.random.fold_in(keys[5], part), 71), part)
    defocus_bin = draw_defocus_bin(jax.random.fold_in(jax.random.fold_in(keys[5], part), 71), part)
    return dict(images=images, class_refs=class_refs, sigma2=sigma2, ctf_group=ctf_group, defocus_bin=defocus_bin)


def shell_radius():
    return (jnp.arange(SHELLS, dtype=jnp.float32) + 1.0) / (2.0 * SHELLS)


def ctf_table():
    defocus = 1.0 + jnp.arange(BINS, dtype=jnp.float32) / BINS
    radius = shell_radius()
    return -jnp.sin(80.0 * defocus[:, None] * radius[None, :] ** 2 + 0.1)


def phase_tables():
    offsets = jnp.arange(2 * REACH + 1, dtype=jnp.float32) - REACH
    shift_x = jnp.repeat(offsets, 2 * REACH + 1)
    shift_y = jnp.tile(offsets, 2 * REACH + 1)
    angles = 2.0 * math.pi * jnp.arange(ANG, dtype=jnp.float32) / ANG
    radius = shell_radius()
    phase = 2.0 * math.pi * radius[None, :, None] * (
        jnp.cos(angles)[None, None, :] * shift_x[:, None, None]
        + jnp.sin(angles)[None, None, :] * shift_y[:, None, None])
    return jnp.cos(phase), jnp.sin(phase)


def image_weights(ctf_group, defocus_bin, sigma2):
    bin_hot = (defocus_bin[:, None] == jnp.arange(BINS, dtype=jnp.int32)[None, :]).astype(jnp.float32)
    group_hot = (ctf_group[:, None] == jnp.arange(NGROUP, dtype=jnp.int32)[None, :]).astype(jnp.float32)
    ctf_sel = jnp.dot(bin_hot, ctf_table(), precision=lax.Precision.HIGHEST)
    noise_sel = jnp.dot(group_hot, sigma2, precision=lax.Precision.HIGHEST)
    return ctf_sel / noise_sel, ctf_sel * ctf_sel / noise_sel


def shifted_features(images, filter_weight):
    count_img = images.shape[0]
    pixels = images.astype(jnp.float32).reshape(count_img, 2, SHELLS, ANG)
    real_part = pixels[:, 0] * filter_weight[:, :, None]
    imag_part = pixels[:, 1] * filter_weight[:, :, None]
    cosine, sine_table = phase_tables()
    shifted_real = real_part[:, None] * cosine[None] - imag_part[:, None] * sine_table[None]
    shifted_imag = real_part[:, None] * sine_table[None] + imag_part[:, None] * cosine[None]
    stacked = jnp.stack([shifted_real, shifted_imag], axis=2)
    return stacked.reshape(count_img * SHIFTS, 2 * SHELLS * ANG).astype(jnp.bfloat16)


def reference(images, class_refs, sigma2, ctf_group, defocus_bin):
    count_img = images.shape[0]
    angle_step = ANG // ROT
    filter_weight, shell_weight = image_weights(ctf_group, defocus_bin, sigma2)
    features = shifted_features(images, filter_weight)
    refs_four = class_refs.reshape(CLASSES, 2, SHELLS, ANG)
    rotated = jnp.concatenate([jnp.roll(refs_four, turn_index * angle_step, axis=3) for turn_index in range(ROT)], axis=0)
    rotated = rotated.reshape(ROT * CLASSES, 2 * SHELLS * ANG)
    cross = jnp.dot(features, rotated.T, preferred_element_type=jnp.float32)
    shell_power = jnp.sum(jnp.square(refs_four.astype(jnp.float32)), axis=(1, 3))
    quadratic = 0.5 * jnp.dot(shell_weight, shell_power.T, precision=lax.Precision.HIGHEST)
    scores = cross.reshape(count_img, SHIFTS, ROT, CLASSES) - quadratic[:, None, None, :]
    highest = jnp.max(scores, axis=(1, 2, 3), keepdims=True)
    expanded = jnp.exp(scores - highest)
    normalizer = jnp.sum(expanded, axis=(1, 2, 3), keepdims=True)
    posterior = expanded / normalizer
    occupancy = jnp.sum(posterior, axis=(1, 2))
    posterior_b = posterior.astype(jnp.bfloat16).reshape(count_img * SHIFTS, ROT * CLASSES)
    oriented = jnp.dot(posterior_b.T, features, preferred_element_type=jnp.float32)
    oriented = oriented.reshape(ROT, CLASSES, 2, SHELLS, ANG)
    numerator = jnp.zeros((CLASSES, 2, SHELLS, ANG), jnp.float32)
    for turn_index in range(ROT):
        numerator = numerator + jnp.roll(oriented[turn_index], -turn_index * angle_step, axis=3)
    weights = jnp.dot(occupancy.T, shell_weight, precision=lax.Precision.HIGHEST)
    new_refs = numerator / (weights[:, None, :, None] + 1.0)
    return new_refs.reshape(CLASSES, 2 * SHELLS * ANG)
```

```python
import functools
import math

import jax
import jax.numpy as jnp
import numpy as np
from jax import lax
from jax.experimental import pallas as pl
from jax.experimental.pallas import tpu as pltpu
from jax.sharding import PartitionSpec as P

CLASSES = 48
ROT = 36
SHELLS = 16
ANG = 144
REACH = 3
SHIFTS = 49
BINS = 32
NGROUP = 16

STEP = ANG // ROT
CHANS = 2 * SHELLS
BLOCKS = CHANS // 2
BLOCK_COLS = 2 * ANG
LANES = CHANS * STEP
FREQS = ROT // 2 + 1
ROWS8 = 8
S_PAD = SHIFTS + 1
ROWS = S_PAD * ROWS8
LIVE = SHIFTS * ROWS8
COLS = 512
KPAD = 64
PAY = (FREQS + 1) * ROWS8
BF = jnp.bfloat16
F32 = jnp.float32
VMEM_LIMIT = 56 * 1024 * 1024


def block_order():
    return [m for m in range(0, BLOCKS, 2)] + [m for m in range(1, BLOCKS, 2)]


def lane_channel():
    chan, off = [], []
    for m in block_order():
        for cc in range(2):
            for d in range(STEP):
                chan.append(2 * m + cc)
                off.append(d)
    return np.array(chan), np.array(off)


def radius_of():
    return (np.arange(SHELLS, dtype=np.float64) + 1.0) / (2.0 * SHELLS)


def ctf_lanes():
    chan, _ = lane_channel()
    radius = (jnp.arange(SHELLS, dtype=F32) + 1.0) / (2.0 * SHELLS)
    defocus = 1.0 + jnp.arange(BINS, dtype=F32) / BINS
    table = -jnp.sin(80.0 * defocus[:, None] * radius[None, :] ** 2 + 0.1)
    return table[:, chan % SHELLS]


def shell_expand():
    chan, _ = lane_channel()
    return (np.arange(SHELLS)[:, None] == (chan % SHELLS)[None, :]).astype(np.float32)


def pixel_perm():
    table = np.zeros((BLOCK_COLS, BLOCK_COLS), np.float32)
    for b in range(ROT):
        for cc in range(2):
            for d in range(STEP):
                table[b * 8 + cc * STEP + d, cc * ANG + STEP * b + d] = 1.0
    return table


def phase_lanes():
    chan, off = lane_channel()
    shell = chan % SHELLS
    sign = np.where(chan < SHELLS, -1.0, 1.0)
    offsets = np.arange(2 * REACH + 1, dtype=np.float64) - REACH
    sx = np.repeat(offsets, 2 * REACH + 1)
    sy = np.tile(offsets, 2 * REACH + 1)
    angle = 2.0 * math.pi * (STEP * np.arange(ROT)[:, None] + off[None, :]) / ANG
    phase = (
        2.0
        * math.pi
        * radius_of()[shell][None, None, :]
        * (np.cos(angle)[None] * sx[:, None, None] + np.sin(angle)[None] * sy[:, None, None])
    )
    cos_t = np.zeros((S_PAD, ROT, LANES), np.float32)
    sin_t = np.zeros((S_PAD, ROT, LANES), np.float32)
    cos_t[:SHIFTS] = np.cos(phase)
    sin_t[:SHIFTS] = np.sin(phase) * sign[None, None, :]
    return cos_t, sin_t


def refs_transform():
    table = np.zeros((FREQS, 2, 2, STEP, 2, ANG), np.float64)
    for q in range(FREQS):
        scale = (1.0 if q in (0, ROT // 2) else 2.0) / ROT
        for d in range(STEP):
            b = np.arange(ROT)
            turn = 2.0 * math.pi * ((q * b) % ROT) / ROT
            for cc in range(2):
                table[q, 0, cc, d, cc, STEP * b + d] = scale * np.cos(turn)
                if q not in (0, ROT // 2):
                    table[q, 1, cc, d, cc, STEP * b + d] = -scale * np.sin(turn)
    return table.reshape(FREQS * 16, BLOCK_COLS)


def power_rows():
    table = np.zeros((2, STEP, 2, ANG), np.float32)
    for cc in range(2):
        table[cc, 0, cc, :] = -0.5
    return table.reshape(8, BLOCK_COLS)


def inverse_transform():
    real = np.zeros((FREQS + 1, 2, STEP, 2, ANG), np.float64)
    imag = np.zeros((FREQS + 1, 2, STEP, 2, ANG), np.float64)
    pick = np.zeros((FREQS + 1, 2, STEP, 2, ANG), np.float64)
    b = np.arange(ROT)
    for q in range(FREQS):
        scale = (1.0 if q in (0, ROT // 2) else 2.0) / ROT
        turn = 2.0 * math.pi * ((q * b) % ROT) / ROT
        for cc in range(2):
            for d in range(STEP):
                real[q, cc, d, cc, STEP * b + d] = scale * np.cos(turn)
                if q not in (0, ROT // 2):
                    imag[q, cc, d, cc, STEP * b + d] = -scale * np.sin(turn)
    for cc in range(2):
        for d in range(2):
            pick[0, cc, d, cc, :] = 1.0
    shape = (PAY, BLOCK_COLS)
    return [t.reshape(shape).astype(np.float32) for t in (real, imag, pick)]


C1, C2 = math.cos(2 * math.pi / 9), math.cos(4 * math.pi / 9)
S1, S3, S4 = math.sin(2 * math.pi / 9), math.sin(6 * math.pi / 9), math.sin(8 * math.pi / 9)


def nine_cos(x0, s1, s2, s3, s4):
    u = s1 + s2 + s4
    v = x0 + s3
    base = x0 - 0.5 * s3
    a, b, c = s1 - s4, s2 - s4, s1 - s2
    p1 = C1 * a + C2 * b
    p2 = C2 * c - C1 * b
    return u + v, base + p1, base + p2, v - 0.5 * u, base - (p1 + p2)


def nine_sin(d1, d2, d3, d4):
    p, q, r = d1 + d2, d2 + d4, d1 - d4
    h = S3 * d3
    e1 = S1 * p + S4 * q
    e2 = S1 * r + S4 * p
    return e1 + h, e2 - h, S3 * (d1 - d2 + d4), (e2 - e1) + h


def nine_real(x):
    r = nine_cos(x[0], x[1] + x[8], x[2] + x[7], x[3] + x[6], x[4] + x[5])
    i = nine_sin(x[1] - x[8], x[2] - x[7], x[3] - x[6], x[4] - x[5])
    return r, (None,) + i


def crt(k1, k2):
    for k in range(ROT):
        if k % 4 == k1 and k % 9 == k2:
            return k
    return None


def forward36(x):
    re, im = [None] * FREQS, [None] * FREQS
    y0, y2, ya, yb = [], [], [], []
    for n2 in range(9):
        v = [x[(9 * n1 + 4 * n2) % ROT] for n1 in range(4)]
        t0, t1 = v[0] + v[2], v[1] + v[3]
        y0.append(t0 + t1)
        y2.append(t0 - t1)
        ya.append(v[0] - v[2])
        yb.append(v[3] - v[1])

    def put(k, real, imag):
        if k <= ROT // 2:
            re[k], im[k] = real, imag
        else:
            re[ROT - k], im[ROT - k] = real, -imag

    for k1, y in ((0, y0), (2, y2)):
        r, i = nine_real(y)
        k = crt(k1, 0)
        re[k] = r[0]
        for k2 in range(1, 5):
            k = crt(k1, k2)
            if k <= ROT // 2:
                re[k], im[k] = r[k2], -i[k2]
            else:
                re[ROT - k], im[ROT - k] = r[k2], i[k2]
    ra, ia = nine_real(ya)
    rb, ib = nine_real(yb)
    put(crt(1, 0), ra[0], rb[0])
    for k2 in range(1, 5):
        put(crt(1, k2), ra[k2] + ib[k2], rb[k2] - ia[k2])
        put(crt(1, 9 - k2), ra[k2] - ib[k2], rb[k2] + ia[k2])
    return re, im


def inverse36(re, im):
    def entry(k):
        if k <= ROT // 2:
            return re[k], im[k], 1
        return re[ROT - k], im[ROT - k], -1

    ys = []
    for k1 in (0, 2):
        real, imag = [entry(crt(k1, 0))[0]], [None]
        for k2 in range(1, 5):
            a, b, sign = entry(crt(k1, k2))
            real.append(a)
            imag.append(b if sign > 0 else -b)
        r = nine_cos(*real)
        i = (None,) + nine_sin(*imag[1:])
        y = [None] * 9
        y[0] = r[0]
        for n in range(1, 5):
            y[n], y[9 - n] = r[n] - i[n], r[n] + i[n]
        ys.append(y)
    xr, xi = [], []
    for k2 in range(9):
        a, b, sign = entry(crt(1, k2))
        xr.append(a)
        xi.append(b if sign > 0 else -b)
    rr, ir = nine_real(xr)
    ri, ii = nine_real(xi)
    ya, yb = [None] * 9, [None] * 9
    ya[0], yb[0] = rr[0], ri[0]
    for n in range(1, 5):
        ya[n], ya[9 - n] = rr[n] - ii[n], rr[n] + ii[n]
        yb[n], yb[9 - n] = ri[n] + ir[n], ri[n] - ir[n]
    x = [None] * ROT
    for n2 in range(9):
        t0, t1 = ys[0][n2] + ys[1][n2], ys[0][n2] - ys[1][n2]
        for n1, value in enumerate((t0 + ya[n2], t1 - yb[n2], t0 - ya[n2], t1 + yb[n2])):
            x[(9 * n1 + 4 * n2) % ROT] = value
    return x


def features_kernel(
    grp_ref, bin_ref, img_ref, sig_ref, ctf_ref, exp_ref, perm_ref, cos_ref, sin_ref,
    fh_ref, fl_ref, noise_ref, pix_ref, swp_ref,
):
    noise_ref[...] = jnp.dot(
        sig_ref[...], exp_ref[...], precision=lax.Precision.HIGHEST, preferred_element_type=F32
    )
    ctf = jnp.concatenate([ctf_ref[pl.ds(bin_ref[i], 1), :] for i in range(ROWS8)], axis=0)
    noise = jnp.concatenate([noise_ref[pl.ds(grp_ref[i], 1), :] for i in range(ROWS8)], axis=0)
    filt = ctf / noise
    weight = ctf * ctf / noise

    img = img_ref[...].astype(F32)
    stack = jnp.concatenate(
        [img[:, BLOCK_COLS * m : BLOCK_COLS * (m + 1)] for m in block_order()], axis=0
    ).astype(BF)
    turned = lax.dot_general(
        perm_ref[...], stack, (((1,), (1,)), ((), ())), preferred_element_type=F32
    )
    sub = lax.broadcasted_iota(jnp.int32, (ROWS8, LANES), 0)
    lane = lax.broadcasted_iota(jnp.int32, (ROWS8, LANES), 1)
    for b in range(ROT):
        y = turned[b * 8 : (b + 1) * 8]
        for t in (1, 2, 4):
            up = pltpu.roll(pltpu.roll(y, t, 0), LANES - t, 1)
            down = pltpu.roll(pltpu.roll(y, 8 - t, 0), t, 1)
            row_bit, lane_bit = (sub & t) != 0, (lane & t) != 0
            y = jnp.where(row_bit == lane_bit, y, jnp.where(row_bit, up, down))
        y = y * filt
        pix_ref[b] = y
        swp_ref[b] = jnp.where(
            (lane & 32) == 0, pltpu.roll(y, LANES - 32, 1), pltpu.roll(y, 32, 1)
        )

    off = lane & (STEP - 1)
    weight_hi = weight.astype(BF).astype(F32)
    slot = jnp.where(off == 0, weight, jnp.where(off == 1, weight - weight_hi, 0.0))
    slot = jnp.concatenate([slot, slot], axis=0)
    nothing = jnp.zeros_like(slot)

    def pair(sp, _):
        x = []
        for b in range(ROT):
            halves = []
            for h in range(2):
                c = cos_ref[2 * sp + h, b : b + 1, :]
                s = sin_ref[2 * sp + h, b : b + 1, :]
                halves.append(pix_ref[b] * c + swp_ref[b] * s)
            x.append(jnp.concatenate(halves, axis=0).astype(BF).astype(F32))
        re, im = forward36(x)
        im[0], im[ROT // 2] = slot, nothing
        rows = pl.ds(pl.multiple_of(sp * 16, 16), 16)
        for q in range(FREQS):
            for part, value in ((0, re[q]), (1, im[q])):
                hi = value.astype(BF)
                fh_ref[q, rows, part * LANES : (part + 1) * LANES] = hi
                fl_ref[q, rows, part * LANES : (part + 1) * LANES] = (
                    value - hi.astype(F32)
                ).astype(BF)
        return 0

    lax.fori_loop(0, S_PAD // 2, pair, 0)


def make_features(images, sigma2, ctf_group, defocus_bin):
    cos_t, sin_t = phase_lanes()
    vm = pl.BlockSpec(memory_space=pltpu.VMEM)
    sm = pl.BlockSpec(memory_space=pltpu.SMEM)
    shape = jax.ShapeDtypeStruct((FREQS, ROWS, 2 * LANES), BF)
    return pl.pallas_call(
        features_kernel,
        out_shape=(shape, shape),
        in_specs=[sm, sm] + [vm] * 7,
        out_specs=(vm, vm),
        scratch_shapes=[
            pltpu.VMEM((NGROUP, LANES), F32),
            pltpu.VMEM((ROT, ROWS8, LANES), F32),
            pltpu.VMEM((ROT, ROWS8, LANES), F32),
        ],
        compiler_params=pltpu.CompilerParams(vmem_limit_bytes=VMEM_LIMIT),
        name="features",
    )(
        ctf_group, defocus_bin, images, sigma2, ctf_lanes(), jnp.asarray(shell_expand()),
        jnp.asarray(pixel_perm(), BF), jnp.asarray(cos_t), jnp.asarray(sin_t),
    )


def nt(left, right):
    return lax.dot_general(left, right, (((1,), (1,)), ((), ())), preferred_element_type=F32)


def posterior_kernel(
    ref_ref, fh_ref, fl_ref, mth_ref, mtl_ref, pow_ref, out_ref, x_ref, d_ref, c_ref, p_ref, num_ref
):
    lane = lax.broadcasted_iota(jnp.int32, (CLASSES, LANES), 1)
    lane8 = lax.broadcasted_iota(jnp.int32, (8, LANES), 1)

    for m in range(BLOCKS):
        x_ref[m * KPAD : m * KPAD + CLASSES, :] = ref_ref[m]
        x_ref[m * KPAD + CLASSES : (m + 1) * KPAD, :] = jnp.zeros((KPAD - CLASSES, BLOCK_COLS), BF)
    x = x_ref[...]
    d_ref[...] = nt(mth_ref[...], x) + nt(mtl_ref[...], x)
    square = jnp.square(x.astype(F32))
    square_hi = square.astype(BF)
    square_lo = (square - square_hi.astype(F32)).astype(BF)
    d_ref[8:16, :] = nt(pow_ref[...], square_hi) + nt(pow_ref[...], square_lo)

    c_ref[:, :, COLS - LANES :] = jnp.zeros((2 * FREQS, CLASSES, LANES), F32)
    for q in range(FREQS):
        tile = jnp.concatenate(
            [
                d_ref[q * 16 + part * 8 : q * 16 + part * 8 + 8, t * LANES : (t + 1) * LANES]
                for part in range(2)
                for t in range(BLOCKS // 2)
            ],
            axis=0,
        )
        tile = tile.T
        even, odd = tile[:CLASSES], tile[KPAD : KPAD + CLASSES]
        real = jnp.where(lane < 64, even, pltpu.roll(odd, 64, 1))
        imag = jnp.where(lane < 64, pltpu.roll(even, 64, 1), odd)
        left = jnp.concatenate(
            [jnp.concatenate([real, imag], axis=1), jnp.concatenate([-imag, real], axis=1)], axis=0
        )
        hi = left.astype(BF)
        lo = (left - hi.astype(F32)).astype(BF)
        first = nt(jnp.concatenate([hi, lo], axis=0), fh_ref[q])
        second = nt(hi, fl_ref[q])
        total = first[: 2 * CLASSES] + first[2 * CLASSES :] + second
        c_ref[2 * q, :, :ROWS] = total[:CLASSES]
        c_ref[2 * q + 1, :, :ROWS] = total[CLASSES:]

    tiles_k = CLASSES // 8

    def where_of(i):
        col = pl.multiple_of((i // tiles_k) * LANES, LANES)
        row = pl.multiple_of((i % tiles_k) * 8, 8)
        return pl.ds(row, 8), pl.ds(col, LANES), col

    def to_scores(i, top):
        rows, cols, col = where_of(i)
        re = [c_ref[2 * q, rows, cols] for q in range(FREQS)]
        im = [None] + [c_ref[2 * q + 1, rows, cols] for q in range(1, FREQS - 1)] + [None]
        re[0] = jnp.where(lane8 + col < LIVE, re[0], -1e30)
        x = inverse36(re, im)
        for r in range(ROT):
            c_ref[r, rows, cols] = x[r]
        peak = x[0]
        for r in range(1, ROT):
            peak = jnp.maximum(peak, x[r])
        return jnp.maximum(top, peak)

    count = tiles_k * (COLS // LANES)
    top = lax.fori_loop(0, count, to_scores, jnp.full((8, LANES), -1e30, F32))

    def fold(v, op):
        for t in (4, 2, 1):
            v = op(v, pltpu.roll(v, t, 0))
        for t in (64, 32, 16, 8):
            v = op(v, pltpu.roll(v, t, 1))
        return v

    top = fold(top, jnp.maximum)

    def to_posterior(i, total):
        rows, cols, _ = where_of(i)
        x = [jnp.exp(c_ref[r, rows, cols] - top) for r in range(ROT)]
        re, im = forward36(x)
        for q in range(FREQS):
            c_ref[2 * q, rows, cols] = re[q]
            if im[q] is not None:
                c_ref[2 * q + 1, rows, cols] = im[q]
            else:
                c_ref[2 * q + 1, rows, cols] = jnp.zeros_like(re[q])
        return total + re[0]

    total = lax.fori_loop(0, count, to_posterior, jnp.zeros((8, LANES), F32))
    inverse = 1.0 / fold(total, jnp.add)
    scale = jnp.concatenate([inverse[:1]] * (COLS // LANES), axis=1)

    num_ref[FREQS] = jnp.zeros((LANES, LANES), F32)
    empty = jnp.zeros((KPAD - CLASSES, LANES), F32)
    for q in range(FREQS):
        p_ref[:CLASSES, :] = (c_ref[2 * q] * scale).astype(BF)
        p_ref[CLASSES:, :] = (c_ref[2 * q + 1] * scale).astype(BF)
        o = jnp.dot(p_ref[:, :ROWS], fh_ref[q], preferred_element_type=F32)
        real = o[:CLASSES, :LANES] + o[CLASSES:, LANES:]
        imag = o[:CLASSES, LANES:] - o[CLASSES:, :LANES]
        num_ref[q] = jnp.concatenate([real, empty, imag, empty], axis=0).T
    for pos, m in enumerate(block_order()):
        block = num_ref[:, pos * 8 : (pos + 1) * 8, :]
        out_ref[m] = block.reshape(PAY, LANES).astype(BF)


def make_payload(refs, feat_hi, feat_lo):
    mt = refs_transform()
    mt_hi = mt.astype(np.float32).astype(jnp.bfloat16)
    mt_lo = (mt - mt_hi.astype(np.float64)).astype(np.float32).astype(jnp.bfloat16)
    vm = pl.BlockSpec(memory_space=pltpu.VMEM)
    return pl.pallas_call(
        posterior_kernel,
        out_shape=jax.ShapeDtypeStruct((BLOCKS, PAY, LANES), BF),
        in_specs=[vm] * 6,
        out_specs=vm,
        scratch_shapes=[
            pltpu.VMEM((BLOCKS * KPAD, BLOCK_COLS), BF),
            pltpu.VMEM((FREQS * 16, BLOCKS * KPAD), F32),
            pltpu.VMEM((2 * FREQS, CLASSES, COLS), F32),
            pltpu.VMEM((2 * CLASSES, COLS), BF),
            pltpu.VMEM((FREQS + 1, LANES, LANES), F32),
        ],
        compiler_params=pltpu.CompilerParams(vmem_limit_bytes=VMEM_LIMIT),
        name="posterior",
    )(refs, feat_hi, feat_lo, jnp.asarray(mt_hi), jnp.asarray(mt_lo), jnp.asarray(power_rows(), BF))


def final_kernel(pay_ref, re_ref, im_ref, pick_ref, out_ref):
    total = jnp.sum(pay_ref[...].astype(F32), axis=0)
    turned = total.T
    real, imag = turned[:CLASSES], turned[KPAD : KPAD + CLASSES]
    dot = functools.partial(
        jnp.dot, precision=lax.Precision.HIGHEST, preferred_element_type=F32
    )
    numer = dot(real, re_ref[...]) + dot(imag, im_ref[...])
    out_ref[...] = numer / (dot(imag, pick_ref[...]) + 1.0)


def finish(pieces):
    re_t, im_t, pick = inverse_transform()
    vm = pl.BlockSpec(memory_space=pltpu.VMEM)
    return pl.pallas_call(
        final_kernel,
        out_shape=jax.ShapeDtypeStruct((CLASSES, BLOCK_COLS), F32),
        in_specs=[vm] * 4,
        out_specs=vm,
        compiler_params=pltpu.CompilerParams(vmem_limit_bytes=VMEM_LIMIT),
        name="finish",
    )(pieces, jnp.asarray(re_t), jnp.asarray(im_t), jnp.asarray(pick))


def on_device(images, class_refs, sigma2, ctf_group, defocus_bin):
    devices = lax.axis_size("img")
    share = class_refs.shape[1]
    me = lax.axis_index("img")
    direct = devices == BLOCKS and share == BLOCK_COLS
    if direct:
        own = jnp.broadcast_to(class_refs[None], (devices,) + class_refs.shape)
        refs = lax.all_to_all(own, "img", 0, 0)
    else:
        whole = lax.all_gather(class_refs, "img", axis=1, tiled=True)
        refs = whole.reshape(CLASSES, BLOCKS, BLOCK_COLS).transpose(1, 0, 2)
    pay = None
    for first in range(0, images.shape[0], ROWS8):
        part = slice(first, first + ROWS8)
        hi, lo = make_features(images[part], sigma2, ctf_group[part], defocus_bin[part])
        one = make_payload(refs, hi, lo)
        pay = one if pay is None else pay + one
    if direct:
        return finish(lax.all_to_all(pay, "img", 0, 0))
    summed = lax.psum(pay.astype(F32), "img")
    start = me * share
    block = lax.dynamic_index_in_dim(summed, start // BLOCK_COLS, 0, keepdims=True)
    return lax.dynamic_slice_in_dim(finish(block), start % BLOCK_COLS, share, 1)


def solution(mesh):
    in_specs = (
        P(("groups", "img"), None),
        P("groups", "img"),
        P("groups", None),
        P(("groups", "img")),
        P(("groups", "img")),
    )
    out_specs = P("groups", "img")
    return jax.shard_map(
        on_device, mesh=mesh, in_specs=in_specs, out_specs=out_specs, check_vma=False
    )
```

```python
import functools
import math

import jax
import jax.numpy as jnp
import numpy as np
from jax import lax
from jax.experimental import pallas as pl
from jax.experimental.pallas import tpu as pltpu
from jax.sharding import PartitionSpec as P

CLASSES = 48
ROT = 36
SHELLS = 16
ANG = 144
REACH = 3
SHIFTS = 49
BINS = 32
NGROUP = 16

STEP = ANG // ROT
CHANS = 2 * SHELLS
BLOCKS = CHANS // 2
BLOCK_COLS = 2 * ANG
LANES = CHANS * STEP
FREQS = ROT // 2 + 1
ROWS8 = 8
S_PAD = SHIFTS + 1
ROWS = S_PAD * ROWS8
LIVE = SHIFTS * ROWS8
COLS = 512
PAIRS_A = 16
ROWS_A = 16 * PAIRS_A
ROWS_B = ROWS - ROWS_A
KPAD = 64
QUADS = (FREQS + 1) // 4
TILES = 3 * QUADS
PAY = TILES * ROWS8
BF = jnp.bfloat16
F32 = jnp.float32
MIB = 1024 * 1024


def block_order():
    return [m for m in range(0, BLOCKS, 2)] + [m for m in range(1, BLOCKS, 2)]


def lane_channel():
    chan, off = [], []
    for m in block_order():
        for cc in range(2):
            for d in range(STEP):
                chan.append(2 * m + cc)
                off.append(d)
    return np.array(chan), np.array(off)


def radius_of():
    return (np.arange(SHELLS, dtype=np.float64) + 1.0) / (2.0 * SHELLS)


def ctf_lanes():
    chan, _ = lane_channel()
    defocus = 1.0 + np.arange(BINS, dtype=np.float64) / BINS
    table = -np.sin(80.0 * defocus[:, None] * radius_of()[None, :] ** 2 + 0.1)
    return table[:, chan % SHELLS].astype(np.float32)


def shell_expand():
    chan, _ = lane_channel()
    return (np.arange(SHELLS)[:, None] == (chan % SHELLS)[None, :]).astype(np.float32)


def pixel_perm():
    table = np.zeros((BLOCK_COLS, BLOCK_COLS), np.float32)
    for b in range(ROT):
        for cc in range(2):
            for d in range(STEP):
                table[b * 8 + cc * STEP + d, cc * ANG + STEP * b + d] = 1.0
    return table


def phase_lanes():
    chan, off = lane_channel()
    shell = chan % SHELLS
    sign = np.where(chan < SHELLS, -1.0, 1.0)
    offsets = np.arange(2 * REACH + 1, dtype=np.float64) - REACH
    sx = np.repeat(offsets, 2 * REACH + 1)
    sy = np.tile(offsets, 2 * REACH + 1)
    angle = 2.0 * math.pi * (STEP * np.arange(ROT)[:, None] + off[None, :]) / ANG
    phase = (
        2.0
        * math.pi
        * radius_of()[shell][None, None, :]
        * (np.cos(angle)[None] * sx[:, None, None] + np.sin(angle)[None] * sy[:, None, None])
    )
    cos_t = np.zeros((S_PAD, ROT, LANES), np.float32)
    sin_t = np.zeros((S_PAD, ROT, LANES), np.float32)
    cos_t[:SHIFTS] = np.cos(phase)
    sin_t[:SHIFTS] = np.sin(phase) * sign[None, None, :]
    return np.concatenate([cos_t, sin_t], axis=1)


def refs_transform():
    table = np.zeros((FREQS, 2, 2, STEP, 2, ANG), np.float64)
    for q in range(FREQS):
        scale = (1.0 if q in (0, ROT // 2) else 2.0) / ROT
        for d in range(STEP):
            b = np.arange(ROT)
            turn = 2.0 * math.pi * ((q * b) % ROT) / ROT
            for cc in range(2):
                table[q, 0, cc, d, cc, STEP * b + d] = scale * np.cos(turn)
                if q not in (0, ROT // 2):
                    table[q, 1, cc, d, cc, STEP * b + d] = -scale * np.sin(turn)
    return table.reshape(FREQS * 16, BLOCK_COLS)


def inverse_transform():
    real = np.zeros((FREQS + 1, 2, STEP, 2, ANG), np.float64)
    imag = np.zeros((FREQS + 1, 2, STEP, 2, ANG), np.float64)
    b = np.arange(ROT)
    for q in range(FREQS):
        scale = (1.0 if q in (0, ROT // 2) else 2.0) / ROT
        turn = 2.0 * math.pi * ((q * b) % ROT) / ROT
        for cc in range(2):
            for d in range(STEP):
                real[q, cc, d, cc, STEP * b + d] = scale * np.cos(turn)
                if q not in (0, ROT // 2):
                    imag[q, cc, d, cc, STEP * b + d] = -scale * np.sin(turn)
    shape = (QUADS, 4, ROWS8, BLOCK_COLS)
    return [t.reshape(shape).transpose(1, 0, 2, 3).reshape(4 * QUADS * ROWS8, BLOCK_COLS) for t in (real, imag)]


def split(table):
    hi = table.astype(np.float32).astype(jnp.bfloat16)
    lo = (table - hi.astype(np.float64)).astype(np.float32).astype(jnp.bfloat16)
    return hi, lo


C1, C2 = math.cos(2 * math.pi / 9), math.cos(4 * math.pi / 9)
S1, S3, S4 = math.sin(2 * math.pi / 9), math.sin(6 * math.pi / 9), math.sin(8 * math.pi / 9)


def nine_cos(x0, s1, s2, s3, s4):
    u = s1 + s2 + s4
    v = x0 + s3
    base = x0 - 0.5 * s3
    a, b, c = s1 - s4, s2 - s4, s1 - s2
    p1 = C1 * a + C2 * b
    p2 = C2 * c - C1 * b
    return u + v, base + p1, base + p2, v - 0.5 * u, base - (p1 + p2)


def nine_sin(d1, d2, d3, d4):
    p, q, r = d1 + d2, d2 + d4, d1 - d4
    h = S3 * d3
    e1 = S1 * p + S4 * q
    e2 = S1 * r + S4 * p
    return e1 + h, e2 - h, S3 * (d1 - d2 + d4), (e2 - e1) + h


def nine_real(x):
    r = nine_cos(x[0], x[1] + x[8], x[2] + x[7], x[3] + x[6], x[4] + x[5])
    i = nine_sin(x[1] - x[8], x[2] - x[7], x[3] - x[6], x[4] - x[5])
    return r, (None,) + i


def crt(k1, k2):
    for k in range(ROT):
        if k % 4 == k1 and k % 9 == k2:
            return k
    return None


def forward36(x):
    re, im = [None] * FREQS, [None] * FREQS
    y0, y2, ya, yb = [], [], [], []
    for n2 in range(9):
        v = [x[(9 * n1 + 4 * n2) % ROT] for n1 in range(4)]
        t0, t1 = v[0] + v[2], v[1] + v[3]
        y0.append(t0 + t1)
        y2.append(t0 - t1)
        ya.append(v[0] - v[2])
        yb.append(v[3] - v[1])

    def put(k, real, imag):
        if k <= ROT // 2:
            re[k], im[k] = real, imag
        else:
            re[ROT - k], im[ROT - k] = real, -imag

    for k1, y in ((0, y0), (2, y2)):
        r, i = nine_real(y)
        k = crt(k1, 0)
        re[k] = r[0]
        for k2 in range(1, 5):
            k = crt(k1, k2)
            if k <= ROT // 2:
                re[k], im[k] = r[k2], -i[k2]
            else:
                re[ROT - k], im[ROT - k] = r[k2], i[k2]
    ra, ia = nine_real(ya)
    rb, ib = nine_real(yb)
    put(crt(1, 0), ra[0], rb[0])
    for k2 in range(1, 5):
        put(crt(1, k2), ra[k2] + ib[k2], rb[k2] - ia[k2])
        put(crt(1, 9 - k2), ra[k2] - ib[k2], rb[k2] + ia[k2])
    return re, im


def inverse36(re, im):
    def entry(k):
        if k <= ROT // 2:
            return re[k], im[k], 1
        return re[ROT - k], im[ROT - k], -1

    ys = []
    for k1 in (0, 2):
        real, imag = [entry(crt(k1, 0))[0]], [None]
        for k2 in range(1, 5):
            a, b, sign = entry(crt(k1, k2))
            real.append(a)
            imag.append(b if sign > 0 else -b)
        r = nine_cos(*real)
        i = (None,) + nine_sin(*imag[1:])
        y = [None] * 9
        y[0] = r[0]
        for n in range(1, 5):
            y[n], y[9 - n] = r[n] - i[n], r[n] + i[n]
        ys.append(y)
    xr, xi = [], []
    for k2 in range(9):
        a, b, sign = entry(crt(1, k2))
        xr.append(a)
        xi.append(b if sign > 0 else -b)
    rr, ir = nine_real(xr)
    ri, ii = nine_real(xi)
    ya, yb = [None] * 9, [None] * 9
    ya[0], yb[0] = rr[0], ri[0]
    for n in range(1, 5):
        ya[n], ya[9 - n] = rr[n] - ii[n], rr[n] + ii[n]
        yb[n], yb[9 - n] = ri[n] + ir[n], ri[n] - ir[n]
    x = [None] * ROT
    for n2 in range(9):
        t0, t1 = ys[0][n2] + ys[1][n2], ys[0][n2] - ys[1][n2]
        for n1, value in enumerate((t0 + ya[n2], t1 - yb[n2], t0 - ya[n2], t1 + yb[n2])):
            x[(9 * n1 + 4 * n2) % ROT] = value
    return x


def transform_pairs(table_ref, pix_ref, slot_ref, fh_ref, fl_ref, count):
    slot = jnp.concatenate([slot_ref[...]] * 2, axis=0)
    nothing = jnp.zeros_like(slot)

    def pair(sp, _):
        x = []
        for b in range(ROT):
            halves = []
            for h in range(2):
                c = table_ref[2 * sp + h, b : b + 1, :]
                s = table_ref[2 * sp + h, ROT + b : ROT + b + 1, :]
                halves.append(pix_ref[0, b] * c + pix_ref[1, b] * s)
            x.append(jnp.concatenate(halves, axis=0).astype(BF).astype(F32))
        re, im = forward36(x)
        im[0], im[ROT // 2] = slot, nothing
        rows = pl.ds(pl.multiple_of(sp * 16, 16), 16)
        for q in range(FREQS):
            for part, value in ((0, re[q]), (1, im[q])):
                hi = value.astype(BF)
                fh_ref[q, rows, part * LANES : (part + 1) * LANES] = hi
                fl_ref[q, rows, part * LANES : (part + 1) * LANES] = (
                    value - hi.astype(F32)
                ).astype(BF)
        return 0

    lax.fori_loop(0, count, pair, 0)


def first_kernel(
    grp_hbm, bin_hbm, img_hbm, sig_hbm, ctf_hbm, exp_hbm, perm_hbm, table_hbm,
    fh_ref, fl_ref, pix_ref, slot_ref, rest_ref,
    grp_ref, bin_ref, img_ref, sig_ref, ctf_ref, exp_ref, perm_ref, table_ref, noise_ref, sems,
):
    moves = [
        (grp_hbm, grp_ref), (bin_hbm, bin_ref), (img_hbm, img_ref), (sig_hbm, sig_ref),
        (ctf_hbm, ctf_ref), (exp_hbm, exp_ref), (perm_hbm, perm_ref),
        (table_hbm.at[pl.ds(0, 2 * PAIRS_A)], table_ref),
        (table_hbm.at[pl.ds(2 * PAIRS_A, S_PAD - 2 * PAIRS_A)], rest_ref),
    ]
    copies = [pltpu.make_async_copy(a, b, sems.at[i]) for i, (a, b) in enumerate(moves)]
    for copy in copies:
        copy.start()
    for copy in copies[:7]:
        copy.wait()
    noise_ref[...] = jnp.dot(
        sig_ref[...], exp_ref[...], precision=lax.Precision.HIGHEST, preferred_element_type=F32
    )
    ctf = jnp.concatenate([ctf_ref[pl.ds(bin_ref[i], 1), :] for i in range(ROWS8)], axis=0)
    noise = jnp.concatenate([noise_ref[pl.ds(grp_ref[i], 1), :] for i in range(ROWS8)], axis=0)
    filt = ctf / noise
    weight = ctf * ctf / noise

    img = img_ref[...].astype(F32)
    stack = jnp.concatenate(
        [img[:, BLOCK_COLS * m : BLOCK_COLS * (m + 1)] for m in block_order()], axis=0
    ).astype(BF)
    turned = lax.dot_general(
        perm_ref[...], stack, (((1,), (1,)), ((), ())), preferred_element_type=F32
    )
    sub = lax.broadcasted_iota(jnp.int32, (ROWS8, LANES), 0)
    lane = lax.broadcasted_iota(jnp.int32, (ROWS8, LANES), 1)
    for b in range(ROT):
        y = turned[b * 8 : (b + 1) * 8]
        for t in (1, 2, 4):
            up = pltpu.roll(pltpu.roll(y, t, 0), LANES - t, 1)
            down = pltpu.roll(pltpu.roll(y, 8 - t, 0), t, 1)
            row_bit, lane_bit = (sub & t) != 0, (lane & t) != 0
            y = jnp.where(row_bit == lane_bit, y, jnp.where(row_bit, up, down))
        y = y * filt
        pix_ref[0, b] = y
        pix_ref[1, b] = jnp.where(
            (lane & 32) == 0, pltpu.roll(y, LANES - 32, 1), pltpu.roll(y, 32, 1)
        )

    off = lane & (STEP - 1)
    weight_hi = weight.astype(BF).astype(F32)
    slot_ref[...] = jnp.where(off == 0, weight, jnp.where(off == 1, weight - weight_hi, 0.0))
    copies[7].wait()
    transform_pairs(table_ref, pix_ref, slot_ref, fh_ref, fl_ref, PAIRS_A)
    copies[8].wait()


def second_kernel(
    table_ref, pix_ref, slot_ref, mt_hbm, back_hbm, fh_ref, fl_ref, mt_ref, back_ref, sems
):
    copies = [
        pltpu.make_async_copy(mt_hbm, mt_ref, sems.at[0]),
        pltpu.make_async_copy(back_hbm, back_ref, sems.at[1]),
    ]
    for copy in copies:
        copy.start()
    transform_pairs(table_ref, pix_ref, slot_ref, fh_ref, fl_ref, S_PAD // 2 - PAIRS_A)
    for copy in copies:
        copy.wait()


VM = pl.BlockSpec(memory_space=pltpu.VMEM)
HB = pl.BlockSpec(memory_space=pltpu.HBM)


def in_hbm(*arrays):
    return [pltpu.with_memory_space_constraint(a, pltpu.HBM) for a in arrays]


def cost(micros):
    return pl.CostEstimate(flops=int(micros * 1e9), bytes_accessed=int(micros * 3e6), transcendentals=0)


def first_features(images, sigma2, ctf_group, defocus_bin):
    feat = jax.ShapeDtypeStruct((FREQS, ROWS_A, 2 * LANES), BF)
    tail = S_PAD - 2 * PAIRS_A
    return pl.pallas_call(
        first_kernel,
        out_shape=(
            feat,
            feat,
            jax.ShapeDtypeStruct((2, ROT, ROWS8, LANES), F32),
            jax.ShapeDtypeStruct((ROWS8, LANES), F32),
            jax.ShapeDtypeStruct((tail, 2 * ROT, LANES), F32),
        ),
        in_specs=[HB] * 8,
        out_specs=[VM] * 5,
        scratch_shapes=[
            pltpu.SMEM((ROWS8,), jnp.int32),
            pltpu.SMEM((ROWS8,), jnp.int32),
            pltpu.VMEM(images.shape, BF),
            pltpu.VMEM(sigma2.shape, F32),
            pltpu.VMEM((BINS, LANES), F32),
            pltpu.VMEM((NGROUP, LANES), F32),
            pltpu.VMEM((BLOCK_COLS, BLOCK_COLS), BF),
            pltpu.VMEM((2 * PAIRS_A, 2 * ROT, LANES), F32),
            pltpu.VMEM((NGROUP, LANES), F32),
            pltpu.SemaphoreType.DMA((9,)),
        ],
        compiler_params=pltpu.CompilerParams(vmem_limit_bytes=20 * MIB),
        cost_estimate=cost(4.5),
        name="features_first",
    )(*in_hbm(
        ctf_group, defocus_bin, images, sigma2, jnp.asarray(ctf_lanes()),
        jnp.asarray(shell_expand()), jnp.asarray(pixel_perm(), BF), jnp.asarray(phase_lanes()),
    ))


def second_features(table, pix, slot):
    feat = jax.ShapeDtypeStruct((FREQS, ROWS_B, 2 * LANES), BF)
    mt = np.stack(split(refs_transform()))
    back = np.stack([half for part in inverse_transform() for half in split(part)])
    return pl.pallas_call(
        second_kernel,
        out_shape=(
            feat,
            feat,
            jax.ShapeDtypeStruct(mt.shape, BF),
            jax.ShapeDtypeStruct(back.shape, BF),
        ),
        in_specs=[VM] * 3 + [HB] * 2,
        out_specs=[VM] * 4,
        scratch_shapes=[pltpu.SemaphoreType.DMA((2,))],
        compiler_params=pltpu.CompilerParams(vmem_limit_bytes=16 * MIB),
        cost_estimate=cost(2.5),
        name="features_second",
    )(table, pix, slot, *in_hbm(jnp.asarray(mt), jnp.asarray(back)))


def nt(left, right):
    return lax.dot_general(left, right, (((1,), (1,)), ((), ())), preferred_element_type=F32)


def posterior_kernel(
    direct, r0_ref, r1_ref, r2_ref, r3_ref, fha_ref, fla_ref, fhb_ref, flb_ref, mt_ref,
    out_ref, x_ref, d_ref, c_ref, p_ref, num_ref,
):
    lane = lax.broadcasted_iota(jnp.int32, (CLASSES, LANES), 1)
    lane8 = lax.broadcasted_iota(jnp.int32, (8, LANES), 1)

    me = lax.axis_index("img") if direct else 0
    blank = jnp.zeros((KPAD - CLASSES, BLOCK_COLS), BF)
    for group, ref in enumerate((r0_ref, r1_ref, r2_ref, r3_ref)):
        for f in range(BLOCKS // 4):
            row = pl.multiple_of((me ^ (4 * f + group)) * KPAD, KPAD)
            x_ref[pl.ds(row, KPAD), :] = jnp.concatenate([ref[f], blank], axis=0)
    x = x_ref[...]
    d_ref[...] = nt(mt_ref[0], x) + nt(mt_ref[1], x)
    square = jnp.square(x.astype(F32))
    square_hi = square.astype(BF)
    square_lo = (square - square_hi.astype(F32)).astype(BF)
    e = lax.broadcasted_iota(jnp.int32, (8, BLOCK_COLS), 0)
    col = lax.broadcasted_iota(jnp.int32, (8, BLOCK_COLS), 1)
    power = jnp.where(e == jnp.where(col < ANG, 0, STEP), -0.5, 0.0).astype(BF)
    d_ref[8:16, :] = nt(power, square_hi) + nt(power, square_lo)

    c_ref[:, :, COLS - LANES :] = jnp.zeros((2 * FREQS, CLASSES, LANES), F32)
    for q in range(FREQS):
        tile = jnp.concatenate(
            [
                d_ref[q * 16 + part * 8 : q * 16 + part * 8 + 8, t * LANES : (t + 1) * LANES]
                for part in range(2)
                for t in range(BLOCKS // 2)
            ],
            axis=0,
        )
        tile = tile.T
        even, odd = tile[:CLASSES], tile[KPAD : KPAD + CLASSES]
        real = jnp.where(lane < 64, even, pltpu.roll(odd, 64, 1))
        imag = jnp.where(lane < 64, pltpu.roll(even, 64, 1), odd)
        left = jnp.concatenate(
            [jnp.concatenate([real, imag], axis=1), jnp.concatenate([-imag, real], axis=1)], axis=0
        )
        hi = left.astype(BF)
        lo = (left - hi.astype(F32)).astype(BF)
        both = jnp.concatenate([hi, lo], axis=0)
        for fh, fl, span in ((fha_ref, fla_ref, slice(0, ROWS_A)), (fhb_ref, flb_ref, slice(ROWS_A, ROWS))):
            first = nt(both, fh[q])
            total = first[: 2 * CLASSES] + first[2 * CLASSES :] + nt(hi, fl[q])
            c_ref[2 * q, :, span] = total[:CLASSES]
            c_ref[2 * q + 1, :, span] = total[CLASSES:]

    tiles_k = CLASSES // 8

    def where_of(i):
        col = pl.multiple_of((i // tiles_k) * LANES, LANES)
        row = pl.multiple_of((i % tiles_k) * 8, 8)
        return pl.ds(row, 8), pl.ds(col, LANES), col

    def to_scores(i, top):
        rows, cols, col = where_of(i)
        re = [c_ref[2 * q, rows, cols] for q in range(FREQS)]
        im = [None] + [c_ref[2 * q + 1, rows, cols] for q in range(1, FREQS - 1)] + [None]
        re[0] = jnp.where(lane8 + col < LIVE, re[0], -1e30)
        x = inverse36(re, im)
        for r in range(ROT):
            c_ref[r, rows, cols] = x[r]
        peak = x[0]
        for r in range(1, ROT):
            peak = jnp.maximum(peak, x[r])
        return jnp.maximum(top, peak)

    count = tiles_k * (COLS // LANES)
    top = lax.fori_loop(0, count, to_scores, jnp.full((8, LANES), -1e30, F32))

    def fold(v, op):
        for t in (4, 2, 1):
            v = op(v, pltpu.roll(v, t, 0))
        for t in (64, 32, 16, 8):
            v = op(v, pltpu.roll(v, t, 1))
        return v

    top = fold(top, jnp.maximum)

    def to_posterior(i, total):
        rows, cols, _ = where_of(i)
        x = [jnp.exp(c_ref[r, rows, cols] - top) for r in range(ROT)]
        re, im = forward36(x)
        for q in range(FREQS):
            c_ref[2 * q, rows, cols] = re[q]
            if im[q] is not None:
                c_ref[2 * q + 1, rows, cols] = im[q]
            else:
                c_ref[2 * q + 1, rows, cols] = jnp.zeros_like(re[q])
        return total + re[0]

    total = lax.fori_loop(0, count, to_posterior, jnp.zeros((8, LANES), F32))
    inverse = 1.0 / fold(total, jnp.add)
    scale = jnp.concatenate([inverse[:1]] * (COLS // LANES), axis=1)

    def product(q):
        p_ref[:CLASSES, :] = (c_ref[2 * q] * scale).astype(BF)
        p_ref[CLASSES:, :] = (c_ref[2 * q + 1] * scale).astype(BF)
        o = jnp.dot(p_ref[:, :ROWS_A], fha_ref[q], preferred_element_type=F32)
        o += jnp.dot(p_ref[:, ROWS_A:ROWS], fhb_ref[q], preferred_element_type=F32)
        real = o[:CLASSES, :LANES] + o[CLASSES:, LANES:]
        imag = o[:CLASSES, LANES:] - o[CLASSES:, :LANES]
        return jnp.concatenate([real, imag], axis=0)

    third = 2 * CLASSES // 3
    for quad in range(QUADS):
        if 4 * quad + 3 < FREQS:
            extra = product(4 * quad + 3)
        else:
            extra = jnp.zeros((2 * CLASSES, LANES), F32)
        for slot in range(3):
            tile = [product(4 * quad + slot), extra[slot * third : (slot + 1) * third]]
            num_ref[slot * QUADS + quad] = jnp.concatenate(tile, axis=0).T
    core, chip = me % 2, me // 2
    for half in range(2):
        side = (1 - core) if half == 0 else core
        for e in range(BLOCKS // 2):
            row = pl.multiple_of(side * (LANES // 2) + (chip ^ e) * ROWS8, ROWS8)
            out_ref[half, e] = num_ref[:, pl.ds(row, 8), :].reshape(PAY, LANES).astype(BF)


def make_payload(direct, refs, feat_a, feat_b, mt):
    return pl.pallas_call(
        functools.partial(posterior_kernel, direct),
        out_shape=jax.ShapeDtypeStruct((2, BLOCKS // 2, PAY, LANES), BF),
        in_specs=[VM] * 9,
        out_specs=VM,
        scratch_shapes=[
            pltpu.VMEM((BLOCKS * KPAD, BLOCK_COLS), BF),
            pltpu.VMEM((FREQS * 16, BLOCKS * KPAD), F32),
            pltpu.VMEM((2 * FREQS, CLASSES, COLS), F32),
            pltpu.VMEM((2 * CLASSES, COLS), BF),
            pltpu.VMEM((TILES, LANES, LANES), F32),
        ],
        compiler_params=pltpu.CompilerParams(vmem_limit_bytes=24 * MIB),
        cost_estimate=cost(10.0),
        name="posterior",
    )(*refs, *feat_a, *feat_b, mt)


def final_kernel(keep_ref, got_ref, back_ref, out_ref):
    total = keep_ref[...] + got_ref[...].astype(F32)
    turned = total.T
    width = QUADS * ROWS8
    third = 2 * CLASSES // 3
    last = jnp.concatenate(
        [turned[2 * CLASSES :, slot * width : (slot + 1) * width] for slot in range(3)], axis=0
    )
    numer = jnp.zeros((CLASSES, BLOCK_COLS), F32)
    for part in range(2):
        rows = slice(part * CLASSES, (part + 1) * CLASSES)
        for value, first in ((turned[rows], 0), (last[rows], 3 * width)):
            span = slice(first, first + value.shape[1])
            hi = value.astype(BF)
            lo = (value - hi.astype(F32)).astype(BF)
            dot = functools.partial(jnp.dot, preferred_element_type=F32)
            table_hi, table_lo = back_ref[2 * part, span], back_ref[2 * part + 1, span]
            numer += dot(hi, table_hi) + dot(lo, table_hi) + dot(hi, table_lo)
    weights = turned[CLASSES : 2 * CLASSES]
    column = lax.broadcasted_iota(jnp.int32, (CLASSES, BLOCK_COLS), 1)
    first = weights[:, 0:1] + weights[:, 1:2]
    second = weights[:, STEP : STEP + 1] + weights[:, STEP + 1 : STEP + 2]
    out_ref[...] = numer / (jnp.where(column < ANG, first, second) + 1.0)


def finish(keep, got, back):
    return pl.pallas_call(
        final_kernel,
        out_shape=jax.ShapeDtypeStruct((CLASSES, BLOCK_COLS), F32),
        in_specs=[VM] * 3,
        out_specs=VM,
        compiler_params=pltpu.CompilerParams(vmem_limit_bytes=8 * MIB),
        cost_estimate=cost(1.0),
        name="finish",
    )(keep, got, back)


def swap(value, distance):
    pairs = [(i, i ^ distance) for i in range(lax.axis_size("img"))]
    return lax.ppermute(value, "img", pairs)


def reduce_direct(pay):
    pairs = pay[1].astype(F32) + swap(pay[0], 1).astype(F32)
    pairs = pairs.reshape((BLOCKS // 4, 2) + pairs.shape[1:])
    parts = [swap(pairs[f].astype(BF), 4 * f) for f in range(1, BLOCKS // 4)]
    total = pairs[0]
    for part in parts:
        total = total + part.astype(F32)
    return total[0], swap(total[1].astype(BF), 2)


def on_device(images, class_refs, sigma2, ctf_group, defocus_bin):
    devices = lax.axis_size("img")
    share = class_refs.shape[1]
    me = lax.axis_index("img")
    direct = devices == BLOCKS and share == BLOCK_COLS
    if direct:
        line = [swap(class_refs, 4 * f) for f in range(1, BLOCKS // 4)]
    else:
        whole = lax.all_gather(class_refs, "img", axis=1, tiled=True)
        blocks = whole.reshape(CLASSES, BLOCKS // 4, 4, BLOCK_COLS).transpose(2, 1, 0, 3)
        refs = [blocks[g] for g in range(4)]
    pay = None
    for first in range(0, images.shape[0], ROWS8):
        part = slice(first, first + ROWS8)
        fha, fla, pix, slot, rest = first_features(
            images[part], sigma2, ctf_group[part], defocus_bin[part]
        )
        if direct and first == 0:
            line, fha = lax.optimization_barrier((line, fha))
            line = jnp.stack([class_refs] + line)
            across = swap(line, 2)
        fhb, flb, mt, back = second_features(rest, pix, slot)
        if direct and first == 0:
            across, fhb = lax.optimization_barrier((across, fhb))
            refs = [line, swap(line, 1), across, swap(across, 1)]
        one = make_payload(direct, refs, (fha, fla), (fhb, flb), mt)
        pay = one if pay is None else pay + one
    if direct:
        return finish(*reduce_direct(pay), back)
    summed = lax.psum(pay.astype(F32), "img")
    start = me * share
    block = start // BLOCK_COLS
    mine = summed[1 - block % 2, block // 2]
    return lax.dynamic_slice_in_dim(
        finish(mine, jnp.zeros_like(mine, BF), back), start % BLOCK_COLS, share, 1
    )


def solution(mesh):
    in_specs = (
        P(("groups", "img"), None),
        P("groups", "img"),
        P("groups", None),
        P(("groups", "img")),
        P(("groups", "img")),
    )
    out_specs = P("groups", "img")
    return jax.shard_map(
        on_device, mesh=mesh, in_specs=in_specs, out_specs=out_specs, check_vma=False
    )
```

```python
import functools
import math

import jax
import jax.numpy as jnp
import numpy as np
from jax import lax
from jax.experimental import pallas as pl
from jax.experimental.pallas import tpu as pltpu
from jax.sharding import PartitionSpec as P

CLASSES = 48
ROT = 36
SHELLS = 16
ANG = 144
REACH = 3
SHIFTS = 49
BINS = 32
NGROUP = 16

STEP = ANG // ROT
CHANS = 2 * SHELLS
BLOCKS = CHANS // 2
BLOCK_COLS = 2 * ANG
LANES = CHANS * STEP
FREQS = ROT // 2 + 1
ROWS8 = 8
S_STEP = 4
S_PAD = -(-SHIFTS // S_STEP) * S_STEP
ROWS = S_PAD * ROWS8
LIVE = SHIFTS * ROWS8
COLS = 512
STEPS_A = 3
GROUP = 256
TAIL = 3 * LANES
TAIL_ROWS = 16
KPAD = 64
QUADS = (FREQS + 1) // 4
TILES = 3 * QUADS
PAY = TILES * ROWS8
BF = jnp.bfloat16
F8 = jnp.float8_e5m2
F32 = jnp.float32
MIB = 1024 * 1024


def block_order():
    return [m for m in range(0, BLOCKS, 2)] + [m for m in range(1, BLOCKS, 2)]


def lane_channel():
    chan, off = [], []
    for m in block_order():
        for cc in range(2):
            for d in range(STEP):
                chan.append(2 * m + cc)
                off.append(d)
    return np.array(chan), np.array(off)


def radius_of():
    return (np.arange(SHELLS, dtype=np.float64) + 1.0) / (2.0 * SHELLS)


def ctf_lanes():
    chan, _ = lane_channel()
    defocus = 1.0 + np.arange(BINS, dtype=np.float64) / BINS
    table = -np.sin(80.0 * defocus[:, None] * radius_of()[None, :] ** 2 + 0.1)
    return table[:, chan % SHELLS].astype(np.float32)


def shell_expand():
    chan, _ = lane_channel()
    return (np.arange(SHELLS)[:, None] == (chan % SHELLS)[None, :]).astype(np.float32)


def pixel_perm():
    table = np.zeros((BLOCK_COLS, BLOCK_COLS), np.float32)
    for b in range(ROT):
        for cc in range(2):
            for d in range(STEP):
                table[b * 8 + cc * STEP + d, cc * ANG + STEP * b + d] = 1.0
    return table


def phase_lanes():
    chan, off = lane_channel()
    shell = chan % SHELLS
    sign = np.where(chan < SHELLS, -1.0, 1.0)
    offsets = np.arange(2 * REACH + 1, dtype=np.float64) - REACH
    sx = np.repeat(offsets, 2 * REACH + 1)
    sy = np.tile(offsets, 2 * REACH + 1)
    angle = 2.0 * math.pi * (STEP * np.arange(ROT)[:, None] + off[None, :]) / ANG
    phase = (
        2.0
        * math.pi
        * radius_of()[shell][None, None, :]
        * (np.cos(angle)[None] * sx[:, None, None] + np.sin(angle)[None] * sy[:, None, None])
    )
    cos_t = np.zeros((S_PAD, ROT, LANES), np.float32)
    sin_t = np.zeros((S_PAD, ROT, LANES), np.float32)
    cos_t[:SHIFTS] = np.cos(phase)
    sin_t[:SHIFTS] = np.sin(phase) * sign[None, None, :]
    return np.concatenate([cos_t, sin_t], axis=1)


def refs_transform():
    table = np.zeros((FREQS, 2, 2, STEP, 2, ANG), np.float64)
    for q in range(FREQS):
        scale = (1.0 if q in (0, ROT // 2) else 2.0) / ROT
        for d in range(STEP):
            b = np.arange(ROT)
            turn = 2.0 * math.pi * ((q * b) % ROT) / ROT
            for cc in range(2):
                table[q, 0, cc, d, cc, STEP * b + d] = scale * np.cos(turn)
                if q not in (0, ROT // 2):
                    table[q, 1, cc, d, cc, STEP * b + d] = -scale * np.sin(turn)
    return table.reshape(FREQS * 16, BLOCK_COLS)


def inverse_transform():
    real = np.zeros((FREQS + 1, 2, STEP, 2, ANG), np.float64)
    imag = np.zeros((FREQS + 1, 2, STEP, 2, ANG), np.float64)
    b = np.arange(ROT)
    for q in range(FREQS):
        scale = (1.0 if q in (0, ROT // 2) else 2.0) / ROT
        turn = 2.0 * math.pi * ((q * b) % ROT) / ROT
        for cc in range(2):
            for d in range(STEP):
                real[q, cc, d, cc, STEP * b + d] = scale * np.cos(turn)
                if q not in (0, ROT // 2):
                    imag[q, cc, d, cc, STEP * b + d] = -scale * np.sin(turn)
    shape = (QUADS, 4, ROWS8, BLOCK_COLS)
    return [t.reshape(shape).transpose(1, 0, 2, 3).reshape(4 * QUADS * ROWS8, BLOCK_COLS) for t in (real, imag)]


def split(table):
    hi = table.astype(np.float32).astype(jnp.bfloat16)
    lo = (table - hi.astype(np.float64)).astype(np.float32).astype(jnp.bfloat16)
    return hi, lo


C1, C2 = math.cos(2 * math.pi / 9), math.cos(4 * math.pi / 9)
S1, S3, S4 = math.sin(2 * math.pi / 9), math.sin(6 * math.pi / 9), math.sin(8 * math.pi / 9)


def nine_cos(x0, s1, s2, s3, s4):
    u = s1 + s2 + s4
    v = x0 + s3
    base = x0 - 0.5 * s3
    a, b, c = s1 - s4, s2 - s4, s1 - s2
    p1 = C1 * a + C2 * b
    p2 = C2 * c - C1 * b
    return u + v, base + p1, base + p2, v - 0.5 * u, base - (p1 + p2)


def nine_sin(d1, d2, d3, d4):
    p, q, r = d1 + d2, d2 + d4, d1 - d4
    h = S3 * d3
    e1 = S1 * p + S4 * q
    e2 = S1 * r + S4 * p
    return e1 + h, e2 - h, S3 * (d1 - d2 + d4), (e2 - e1) + h


def nine_real(x):
    r = nine_cos(x[0], x[1] + x[8], x[2] + x[7], x[3] + x[6], x[4] + x[5])
    i = nine_sin(x[1] - x[8], x[2] - x[7], x[3] - x[6], x[4] - x[5])
    return r, (None,) + i


def crt(k1, k2):
    for k in range(ROT):
        if k % 4 == k1 and k % 9 == k2:
            return k
    return None


def forward36(x):
    re, im = [None] * FREQS, [None] * FREQS
    y0, y2, ya, yb = [], [], [], []
    for n2 in range(9):
        v = [x[(9 * n1 + 4 * n2) % ROT] for n1 in range(4)]
        t0, t1 = v[0] + v[2], v[1] + v[3]
        y0.append(t0 + t1)
        y2.append(t0 - t1)
        ya.append(v[0] - v[2])
        yb.append(v[3] - v[1])

    def put(k, real, imag):
        if k <= ROT // 2:
            re[k], im[k] = real, imag
        else:
            re[ROT - k], im[ROT - k] = real, -imag

    for k1, y in ((0, y0), (2, y2)):
        r, i = nine_real(y)
        k = crt(k1, 0)
        re[k] = r[0]
        for k2 in range(1, 5):
            k = crt(k1, k2)
            if k <= ROT // 2:
                re[k], im[k] = r[k2], -i[k2]
            else:
                re[ROT - k], im[ROT - k] = r[k2], i[k2]
    ra, ia = nine_real(ya)
    rb, ib = nine_real(yb)
    put(crt(1, 0), ra[0], rb[0])
    for k2 in range(1, 5):
        put(crt(1, k2), ra[k2] + ib[k2], rb[k2] - ia[k2])
        put(crt(1, 9 - k2), ra[k2] - ib[k2], rb[k2] + ia[k2])
    return re, im


def inverse36(re, im):
    def entry(k):
        if k <= ROT // 2:
            return re[k], im[k], 1
        return re[ROT - k], im[ROT - k], -1

    ys = []
    for k1 in (0, 2):
        real, imag = [entry(crt(k1, 0))[0]], [None]
        for k2 in range(1, 5):
            a, b, sign = entry(crt(k1, k2))
            real.append(a)
            imag.append(b if sign > 0 else -b)
        r = nine_cos(*real)
        i = (None,) + nine_sin(*imag[1:])
        y = [None] * 9
        y[0] = r[0]
        for n in range(1, 5):
            y[n], y[9 - n] = r[n] - i[n], r[n] + i[n]
        ys.append(y)
    xr, xi = [], []
    for k2 in range(9):
        a, b, sign = entry(crt(1, k2))
        xr.append(a)
        xi.append(b if sign > 0 else -b)
    rr, ir = nine_real(xr)
    ri, ii = nine_real(xi)
    ya, yb = [None] * 9, [None] * 9
    ya[0], yb[0] = rr[0], ri[0]
    for n in range(1, 5):
        ya[n], ya[9 - n] = rr[n] - ii[n], rr[n] + ii[n]
        yb[n], yb[9 - n] = ri[n] + ir[n], ri[n] - ir[n]
    x = [None] * ROT
    for n2 in range(9):
        t0, t1 = ys[0][n2] + ys[1][n2], ys[0][n2] - ys[1][n2]
        for n1, value in enumerate((t0 + ya[n2], t1 - yb[n2], t0 - ya[n2], t1 + yb[n2])):
            x[(9 * n1 + 4 * n2) % ROT] = value
    return x


def transform_steps(table_ref, pix_ref, slot_ref, fh_ref, fl_ref, first, count):
    slot = jnp.concatenate([slot_ref[...]] * 2, axis=0)
    nothing = jnp.zeros_like(slot)

    def step(i, _):
        parts = []
        for pair in range(S_STEP // 2):
            x = []
            for b in range(ROT):
                halves = []
                for h in range(2):
                    at = S_STEP * i + 2 * pair + h
                    c = table_ref[at, b : b + 1, :]
                    s = table_ref[at, ROT + b : ROT + b + 1, :]
                    halves.append(pix_ref[0, b] * c + pix_ref[1, b] * s)
                x.append(jnp.concatenate(halves, axis=0).astype(BF).astype(F32))
            re, im = forward36(x)
            im[0], im[ROT // 2] = slot, nothing
            row = pl.multiple_of((first + i) * S_STEP * ROWS8 + 16 * pair, 16)
            low = []
            for q in range(FREQS):
                for part, value in ((0, re[q]), (1, im[q])):
                    hi = value.astype(BF)
                    fh_ref[q, pl.ds(row, 16), part * LANES : (part + 1) * LANES] = hi
                    low.append(value - hi.astype(F32))
            parts.append(low)
        rows = pl.ds(pl.multiple_of((first + i) * S_STEP * ROWS8, S_STEP * ROWS8), S_STEP * ROWS8)
        for n, low in enumerate(zip(*parts)):
            cols = slice((n % 2) * LANES, (n % 2 + 1) * LANES)
            fl_ref[n // 2, rows, cols] = jnp.concatenate(low, axis=0).astype(F8)
        return 0

    lax.fori_loop(0, count, step, 0)


def first_kernel(
    grp_hbm, bin_hbm, img_hbm, sig_hbm, ctf_hbm, exp_hbm, perm_hbm, table_hbm,
    fh_ref, fl_ref, pix_ref, slot_ref, rest_ref,
    grp_ref, bin_ref, img_ref, sig_ref, ctf_ref, exp_ref, perm_ref, table_ref, noise_ref, sems,
):
    moves = [
        (grp_hbm, grp_ref), (bin_hbm, bin_ref), (img_hbm, img_ref), (sig_hbm, sig_ref),
        (ctf_hbm, ctf_ref), (exp_hbm, exp_ref), (perm_hbm, perm_ref),
        (table_hbm.at[pl.ds(0, S_STEP * STEPS_A)], table_ref),
        (table_hbm.at[pl.ds(S_STEP * STEPS_A, S_PAD - S_STEP * STEPS_A)], rest_ref),
    ]
    copies = [pltpu.make_async_copy(a, b, sems.at[i]) for i, (a, b) in enumerate(moves)]
    for copy in copies:
        copy.start()
    for copy in copies[:7]:
        copy.wait()
    noise_ref[...] = jnp.dot(
        sig_ref[...], exp_ref[...], precision=lax.Precision.HIGHEST, preferred_element_type=F32
    )
    ctf = jnp.concatenate([ctf_ref[pl.ds(bin_ref[i], 1), :] for i in range(ROWS8)], axis=0)
    noise = jnp.concatenate([noise_ref[pl.ds(grp_ref[i], 1), :] for i in range(ROWS8)], axis=0)
    filt = ctf / noise
    weight = ctf * ctf / noise

    img = img_ref[...].astype(F32)
    stack = jnp.concatenate(
        [img[:, BLOCK_COLS * m : BLOCK_COLS * (m + 1)] for m in block_order()], axis=0
    ).astype(BF)
    turned = lax.dot_general(
        perm_ref[...], stack, (((1,), (1,)), ((), ())), preferred_element_type=F32
    )
    sub = lax.broadcasted_iota(jnp.int32, (ROWS8, LANES), 0)
    lane = lax.broadcasted_iota(jnp.int32, (ROWS8, LANES), 1)
    for b in range(ROT):
        y = turned[b * 8 : (b + 1) * 8]
        for t in (1, 2, 4):
            up = pltpu.roll(pltpu.roll(y, t, 0), LANES - t, 1)
            down = pltpu.roll(pltpu.roll(y, 8 - t, 0), t, 1)
            row_bit, lane_bit = (sub & t) != 0, (lane & t) != 0
            y = jnp.where(row_bit == lane_bit, y, jnp.where(row_bit, up, down))
        y = y * filt
        pix_ref[0, b] = y
        pix_ref[1, b] = jnp.where(
            (lane & 32) == 0, pltpu.roll(y, LANES - 32, 1), pltpu.roll(y, 32, 1)
        )

    off = lane & (STEP - 1)
    weight_hi = weight.astype(BF).astype(F32)
    slot_ref[...] = jnp.where(off == 0, weight_hi, jnp.where(off == 1, weight - weight_hi, 0.0))
    copies[7].wait()
    transform_steps(table_ref, pix_ref, slot_ref, fh_ref, fl_ref, 0, STEPS_A)
    copies[8].wait()


def second_kernel(
    fh_in, fl_in, table_ref, pix_ref, slot_ref, mt_hbm, back_hbm,
    fh_ref, fl_ref, mt_ref, back_ref, sems,
):
    del fh_in, fl_in
    copies = [
        pltpu.make_async_copy(mt_hbm, mt_ref, sems.at[0]),
        pltpu.make_async_copy(back_hbm, back_ref, sems.at[1]),
    ]
    for copy in copies:
        copy.start()
    transform_steps(
        table_ref, pix_ref, slot_ref, fh_ref, fl_ref, STEPS_A, S_PAD // S_STEP - STEPS_A
    )
    for copy in copies:
        copy.wait()


VM = pl.BlockSpec(memory_space=pltpu.VMEM)
HB = pl.BlockSpec(memory_space=pltpu.HBM)


def in_hbm(*arrays):
    return [pltpu.with_memory_space_constraint(a, pltpu.HBM) for a in arrays]


def cost(micros):
    return pl.CostEstimate(flops=int(micros * 1e9), bytes_accessed=int(micros * 3e6), transcendentals=0)


def first_features(images, sigma2, ctf_group, defocus_bin):
    feat = (FREQS, ROWS, 2 * LANES)
    tail = S_PAD - S_STEP * STEPS_A
    return pl.pallas_call(
        first_kernel,
        out_shape=(
            jax.ShapeDtypeStruct(feat, BF),
            jax.ShapeDtypeStruct(feat, F8),
            jax.ShapeDtypeStruct((2, ROT, ROWS8, LANES), F32),
            jax.ShapeDtypeStruct((ROWS8, LANES), F32),
            jax.ShapeDtypeStruct((tail, 2 * ROT, LANES), F32),
        ),
        in_specs=[HB] * 8,
        out_specs=[VM] * 5,
        scratch_shapes=[
            pltpu.SMEM((ROWS8,), jnp.int32),
            pltpu.SMEM((ROWS8,), jnp.int32),
            pltpu.VMEM(images.shape, BF),
            pltpu.VMEM(sigma2.shape, F32),
            pltpu.VMEM((BINS, LANES), F32),
            pltpu.VMEM((NGROUP, LANES), F32),
            pltpu.VMEM((BLOCK_COLS, BLOCK_COLS), BF),
            pltpu.VMEM((S_STEP * STEPS_A, 2 * ROT, LANES), F32),
            pltpu.VMEM((NGROUP, LANES), F32),
            pltpu.SemaphoreType.DMA((9,)),
        ],
        compiler_params=pltpu.CompilerParams(vmem_limit_bytes=20 * MIB),
        cost_estimate=cost(4.5),
        name="features_first",
    )(*in_hbm(
        ctf_group, defocus_bin, images, sigma2, jnp.asarray(ctf_lanes()),
        jnp.asarray(shell_expand()), jnp.asarray(pixel_perm(), BF), jnp.asarray(phase_lanes()),
    ))


def second_features(hi, lo, table, pix, slot):
    mt = np.stack(split(refs_transform()))
    back = np.stack([half for part in inverse_transform() for half in split(part)])
    return pl.pallas_call(
        second_kernel,
        out_shape=(
            jax.ShapeDtypeStruct(hi.shape, BF),
            jax.ShapeDtypeStruct(lo.shape, F8),
            jax.ShapeDtypeStruct(mt.shape, BF),
            jax.ShapeDtypeStruct(back.shape, BF),
        ),
        in_specs=[VM] * 5 + [HB] * 2,
        out_specs=[VM] * 4,
        scratch_shapes=[pltpu.SemaphoreType.DMA((2,))],
        input_output_aliases={0: 0, 1: 1},
        compiler_params=pltpu.CompilerParams(vmem_limit_bytes=16 * MIB),
        cost_estimate=cost(2.5),
        name="features_second",
    )(hi, lo, table, pix, slot, *in_hbm(jnp.asarray(mt), jnp.asarray(back)))


def nt(left, right):
    return lax.dot_general(left, right, (((1,), (1,)), ((), ())), preferred_element_type=F32)


def posterior_kernel(
    direct, near_ref, rest_ref, near1_ref, rest1_ref, fh_ref, fl_ref, mt_ref,
    out_ref, x_ref, d_ref, a_ref, e_ref, ca_ref, cb_ref, ct_ref, sa_ref, sb_ref, st_ref,
    pa_ref, pb_ref, pt_ref, q_ref, num_ref,
):
    lane = lax.broadcasted_iota(jnp.int32, (CLASSES, LANES), 1)
    lane8 = lax.broadcasted_iota(jnp.int32, (8, LANES), 1)
    row8 = lax.broadcasted_iota(jnp.int32, (8, LANES), 0)

    me = lax.axis_index("img") if direct else 0
    blank = jnp.zeros((KPAD - CLASSES, BLOCK_COLS), BF)
    for side, refs in enumerate(((near_ref, rest_ref), (near1_ref, rest1_ref))):
        for entry in range(BLOCKS // 2):
            values = refs[0][entry] if entry < 2 else refs[1][entry - 2]
            block = me ^ (2 * (entry // 2) + 8 * (entry % 2) + side)
            row = pl.multiple_of(block * KPAD, KPAD)
            x_ref[pl.ds(row, KPAD), :] = jnp.concatenate([values, blank], axis=0)
    x = x_ref[...]
    d_ref[...] = nt(mt_ref[0], x) + nt(mt_ref[1], x)

    for t in range(BLOCKS // 2):
        cols = slice(t * LANES, (t + 1) * LANES)
        edge = jnp.zeros((8, LANES), F32)
        inner = jnp.zeros((8, LANES), F32)
        for q in range(FREQS):
            re = d_ref[q * 16 : q * 16 + 8, cols]
            if q in (0, ROT // 2):
                edge += re * re
            else:
                im = d_ref[q * 16 + 8 : q * 16 + 16, cols]
                inner += re * re + im * im
        power = -0.5 * (ROT * edge + (ROT // 2) * inner)
        power += pltpu.roll(power, 7, 0)
        power += pltpu.roll(power, 6, 0)
        power = jnp.where((row8 & (STEP - 1)) == 0, power, 0.0)
        d_ref[8:16, cols] = power + pltpu.roll(power, 1, 0)

    def operand(q):
        tile = jnp.concatenate(
            [
                d_ref[q * 16 + part * 8 : q * 16 + part * 8 + 8, t * LANES : (t + 1) * LANES]
                for part in range(2)
                for t in range(BLOCKS // 2)
            ],
            axis=0,
        )
        tile = tile.T
        even, odd = tile[:CLASSES], tile[KPAD : KPAD + CLASSES]
        real = jnp.where(lane < 64, even, pltpu.roll(odd, 64, 1))
        imag = jnp.where(lane < 64, pltpu.roll(even, 64, 1), odd)
        real_hi, imag_hi = real.astype(BF), imag.astype(BF)
        real_lo = (real - real_hi.astype(F32)).astype(BF)
        imag_lo = (imag - imag_hi.astype(F32)).astype(BF)
        for first, re, im in ((0, real_hi, imag_hi), (2 * CLASSES, real_lo, imag_lo)):
            a_ref[q, first : first + CLASSES, :LANES] = re
            a_ref[q, first : first + CLASSES, LANES:] = im
            a_ref[q, first + CLASSES : first + 2 * CLASSES, :LANES] = -im
            a_ref[q, first + CLASSES : first + 2 * CLASSES, LANES:] = re
        left = [jnp.concatenate([real, imag], axis=1), jnp.concatenate([-imag, real], axis=1)]
        e_ref[q] = jnp.concatenate(left, axis=0).astype(F8)

    tiles_k = CLASSES // 8

    def cross(q, rows):
        both = a_ref[q]
        first = nt(both, fh_ref[q, rows])
        return first[: 2 * CLASSES] + first[2 * CLASSES :] + nt(e_ref[q], fl_ref[q, rows])

    def cross_first(q):
        total = cross(q, slice(0, GROUP))
        if q + 1 < FREQS:
            operand(q + 1)
        ca_ref[2 * q] = total[:CLASSES]
        ca_ref[2 * q + 1] = total[CLASSES:]

    def cross_second(q):
        total = cross(q, slice(GROUP, ROWS))
        cb_ref[2 * q] = total[:CLASSES, : TAIL - GROUP]
        cb_ref[2 * q + 1] = total[CLASSES:, : TAIL - GROUP]
        last = total[:, TAIL - GROUP : TAIL - GROUP + TAIL_ROWS]
        last = jnp.concatenate([last, jnp.zeros((2 * CLASSES, LANES - TAIL_ROWS), F32)], axis=1)
        for part in range(2):
            packed = last[part * CLASSES : part * CLASSES + 8]
            for kt in range(1, tiles_k):
                row = part * CLASSES + kt * 8
                packed += pltpu.roll(last[row : row + 8], kt * TAIL_ROWS, 1)
            ct_ref[2 * q + part] = packed

    def tiles_of(c_ref, s_ref, p_ref):
        return [
            (c_ref, s_ref, p_ref, slice(row, row + 8), slice(col, col + LANES))
            for col in range(0, c_ref.shape[2], LANES)
            for row in range(0, c_ref.shape[1], 8)
        ]

    packed_live = ((lane8 & (TAIL_ROWS - 1)) < LIVE - TAIL) & (lane8 < tiles_k * TAIL_ROWS)

    def to_scores(where, top):
        c_ref, s_ref, _, rows, cols = where
        re = [c_ref[2 * q, rows, cols] for q in range(FREQS)]
        im = [None] + [c_ref[2 * q + 1, rows, cols] for q in range(1, FREQS - 1)] + [None]
        if c_ref is ct_ref:
            re[0] = jnp.where(packed_live, re[0], -1e30)
        x = inverse36(re, im)
        for r in range(ROT):
            s_ref[r, rows, cols] = x[r]
        while len(x) > 1:
            x = [jnp.maximum(*x[i : i + 2]) if i + 1 < len(x) else x[i] for i in range(0, len(x), 2)]
        return x[0] if top is None else jnp.maximum(top, x[0])

    def fold(v, op):
        for t in (4, 2, 1):
            v = op(v, pltpu.roll(v, t, 0))
        for t in (64, 32, 16, 8):
            v = op(v, pltpu.roll(v, t, 1))
        return v

    def to_posterior(where, top, total):
        _, s_ref, p_ref, rows, cols = where
        x = [jnp.exp(s_ref[r, rows, cols] - top) for r in range(ROT)]
        re, im = forward36(x)
        for q in range(FREQS):
            p_ref[2 * q, rows, cols] = re[q]
            if im[q] is not None:
                p_ref[2 * q + 1, rows, cols] = im[q]
        return re[0] if total is None else total + re[0]

    operand(0)
    for q in range(FREQS):
        cross_first(q)
    tiles_a = tiles_of(ca_ref, sa_ref, pa_ref)
    top_a = total_a = None
    todo = list(range(FREQS))
    for step, where in enumerate(tiles_a):
        top_a = to_scores(where, top_a)
        while todo and todo[0] * 2 * len(tiles_a) < (step + 1) * FREQS:
            cross_second(todo.pop(0))
    top_a = fold(top_a, jnp.maximum)
    for step, where in enumerate(tiles_a):
        total_a = to_posterior(where, top_a, total_a)
        while todo and todo[0] * 2 * len(tiles_a) < (len(tiles_a) + step + 1) * FREQS:
            cross_second(todo.pop(0))
    for q in todo:
        cross_second(q)
    tiles_b = tiles_of(cb_ref, sb_ref, pb_ref) + tiles_of(ct_ref, st_ref, pt_ref)
    top_b = total_b = None
    for where in tiles_b:
        top_b = to_scores(where, top_b)
    top_b = fold(top_b, jnp.maximum)
    for where in tiles_b:
        total_b = to_posterior(where, top_b, total_b)
    top = jnp.maximum(top_a, top_b)
    part_a, part_b = jnp.exp(top_a - top), jnp.exp(top_b - top)
    inverse = 1.0 / (part_a * fold(total_a, jnp.add) + part_b * fold(total_b, jnp.add))
    scale_a, scale_b = (part_a * inverse)[:1], (part_b * inverse)[:1]

    def scaled(q):
        for part in range(2):
            rows = slice(part * CLASSES, (part + 1) * CLASSES)
            if part == 1 and q in (0, ROT // 2):
                q_ref[q, rows, :] = jnp.zeros((CLASSES, COLS), BF)
                continue
            slot = 2 * q + part
            for col in range(0, GROUP, LANES):
                value = pa_ref[slot, :, col : col + LANES] * scale_a
                q_ref[q, rows, col : col + LANES] = value.astype(BF)
            q_ref[q, rows, GROUP:TAIL] = (pb_ref[slot] * scale_b).astype(BF)
            packed = jnp.where(packed_live, pt_ref[slot] * scale_b, 0.0)
            last = [packed] + [
                pltpu.roll(packed, LANES - kt * TAIL_ROWS, 1) for kt in range(1, tiles_k)
            ]
            last = jnp.where(lane < TAIL_ROWS, jnp.concatenate(last, axis=0), 0.0)
            q_ref[q, rows, TAIL:] = last.astype(BF)

    third = 2 * CLASSES // 3
    order = [4 * quad + slot for quad in range(QUADS) for slot in (3, 0, 1, 2)]
    order = [q for q in order if q < FREQS]
    extra = jnp.zeros((2 * CLASSES, LANES), F32)
    scaled(order[0])
    for n, q in enumerate(order):
        o = jnp.dot(q_ref[q, :, :ROWS], fh_ref[q], preferred_element_type=F32)
        if n + 1 < len(order):
            scaled(order[n + 1])
        real = o[:CLASSES, :LANES] + o[CLASSES:, LANES:]
        imag = o[:CLASSES, LANES:] - o[CLASSES:, :LANES]
        both = jnp.concatenate([real, imag], axis=0)
        quad, slot = q // 4, q % 4
        if slot == 3:
            extra = both
            continue
        if 4 * quad + 3 >= FREQS:
            extra = jnp.zeros((2 * CLASSES, LANES), F32)
        tile = [both, extra[slot * third : (slot + 1) * third]]
        num_ref[slot * QUADS + quad] = jnp.concatenate(tile, axis=0).T
    core, chip = me % 2, me // 2
    for half in range(2):
        side = (1 - core) if half == 0 else core
        for e in range(BLOCKS // 2):
            row = side * (LANES // 2) + (chip ^ (e // 2 + 4 * (e % 2))) * ROWS8
            row = pl.multiple_of(row, ROWS8)
            out_ref[half, e] = num_ref[:, pl.ds(row, 8), :].reshape(PAY, LANES).astype(BF)


def make_payload(direct, refs, feat_hi, feat_lo, mt):
    return pl.pallas_call(
        functools.partial(posterior_kernel, direct),
        out_shape=jax.ShapeDtypeStruct((2, BLOCKS // 2, PAY, LANES), BF),
        in_specs=[VM] * 7,
        out_specs=VM,
        scratch_shapes=[
            pltpu.VMEM((BLOCKS * KPAD, BLOCK_COLS), BF),
            pltpu.VMEM((FREQS * 16, BLOCKS * KPAD), F32),
            pltpu.VMEM((FREQS, 4 * CLASSES, 2 * LANES), BF),
            pltpu.VMEM((FREQS, 2 * CLASSES, 2 * LANES), F8),
            pltpu.VMEM((2 * FREQS, CLASSES, GROUP), F32),
            pltpu.VMEM((2 * FREQS, CLASSES, TAIL - GROUP), F32),
            pltpu.VMEM((2 * FREQS, 8, LANES), F32),
            pltpu.VMEM((ROT, CLASSES, GROUP), F32),
            pltpu.VMEM((ROT, CLASSES, TAIL - GROUP), F32),
            pltpu.VMEM((ROT, 8, LANES), F32),
            pltpu.VMEM((2 * FREQS, CLASSES, GROUP), F32),
            pltpu.VMEM((2 * FREQS, CLASSES, TAIL - GROUP), F32),
            pltpu.VMEM((2 * FREQS, 8, LANES), F32),
            pltpu.VMEM((FREQS, 2 * CLASSES, COLS), BF),
            pltpu.VMEM((TILES, LANES, LANES), F32),
        ],
        compiler_params=pltpu.CompilerParams(vmem_limit_bytes=28 * MIB),
        cost_estimate=cost(10.0),
        name="posterior",
    )(*refs, feat_hi, feat_lo, mt)


def final_kernel(keep_ref, got_ref, back_ref, out_ref):
    total = keep_ref[...] + got_ref[...].astype(F32)
    turned = total.T
    width = QUADS * ROWS8
    third = 2 * CLASSES // 3
    last = jnp.concatenate(
        [turned[2 * CLASSES :, slot * width : (slot + 1) * width] for slot in range(3)], axis=0
    )
    numer = jnp.zeros((CLASSES, BLOCK_COLS), F32)
    for part in range(2):
        rows = slice(part * CLASSES, (part + 1) * CLASSES)
        for value, first in ((turned[rows], 0), (last[rows], 3 * width)):
            span = slice(first, first + value.shape[1])
            hi = value.astype(BF)
            lo = (value - hi.astype(F32)).astype(BF)
            dot = functools.partial(jnp.dot, preferred_element_type=F32)
            table_hi, table_lo = back_ref[2 * part, span], back_ref[2 * part + 1, span]
            numer += dot(hi, table_hi) + dot(lo, table_hi) + dot(hi, table_lo)
    weights = turned[CLASSES : 2 * CLASSES]
    column = lax.broadcasted_iota(jnp.int32, (CLASSES, BLOCK_COLS), 1)
    first = weights[:, 0:1] + weights[:, 1:2]
    second = weights[:, STEP : STEP + 1] + weights[:, STEP + 1 : STEP + 2]
    out_ref[...] = numer / (jnp.where(column < ANG, first, second) + 1.0)


def finish(keep, got, back):
    return pl.pallas_call(
        final_kernel,
        out_shape=jax.ShapeDtypeStruct((CLASSES, BLOCK_COLS), F32),
        in_specs=[VM] * 3,
        out_specs=VM,
        compiler_params=pltpu.CompilerParams(vmem_limit_bytes=8 * MIB),
        cost_estimate=cost(1.0),
        name="finish",
    )(keep, got, back)


def swap(value, distance):
    pairs = [(i, i ^ distance) for i in range(lax.axis_size("img"))]
    return lax.ppermute(value, "img", pairs)


def reduce_direct(pay):
    pairs = pay[1].astype(F32) + swap(pay[0], 1).astype(F32)
    pairs = pairs.reshape((4, BLOCKS // 8) + pairs.shape[1:])
    parts = [swap(pairs[g].astype(BF), 2 * g) for g in (1, 2, 3)]
    total = pairs[0]
    for part in parts:
        total = total + part.astype(F32)
    return total[0], swap(total[1].astype(BF), 8)


def on_device(images, class_refs, sigma2, ctf_group, defocus_bin):
    devices = lax.axis_size("img")
    share = class_refs.shape[1]
    me = lax.axis_index("img")
    direct = devices == BLOCKS and share == BLOCK_COLS
    if direct:
        near = swap(class_refs, 8)
    else:
        whole = lax.all_gather(class_refs, "img", axis=1, tiled=True)
        blocks = whole.reshape(CLASSES, BLOCKS, BLOCK_COLS).transpose(1, 0, 2)
        order = [2 * (e // 2) + 8 * (e % 2) for e in range(BLOCKS // 2)]
        sides = [jnp.stack([blocks[m + side] for m in order]) for side in range(2)]
        refs = [part for side in sides for part in (side[:2], side[2:])]
    pay = None
    for first in range(0, images.shape[0], ROWS8):
        part = slice(first, first + ROWS8)
        hi, lo, pix, slot, table = first_features(
            images[part], sigma2, ctf_group[part], defocus_bin[part]
        )
        if direct and first == 0:
            near, hi = lax.optimization_barrier((near, hi))
            near = jnp.stack([class_refs, near])
            rest = [swap(near, 2 * g) for g in (1, 2, 3)]
        hi, lo, mt, back = second_features(hi, lo, table, pix, slot)
        if direct and first == 0:
            rest, hi = lax.optimization_barrier((rest, hi))
            rest = jnp.concatenate(rest)
            refs = [near, rest, swap(near, 1), swap(rest, 1)]
        one = make_payload(direct, refs, hi, lo, mt)
        pay = one if pay is None else pay + one
    if direct:
        return finish(*reduce_direct(pay), back)
    summed = lax.psum(pay.astype(F32), "img")
    start = me * share
    block = start // BLOCK_COLS
    chip = block // 2
    mine = summed[1 - block % 2, 2 * (chip % 4) + chip // 4]
    return lax.dynamic_slice_in_dim(
        finish(mine, jnp.zeros_like(mine, BF), back), start % BLOCK_COLS, share, 1
    )


def solution(mesh):
    in_specs = (
        P(("groups", "img"), None),
        P("groups", "img"),
        P("groups", None),
        P(("groups", "img")),
        P(("groups", "img")),
    )
    out_specs = P("groups", "img")
    return jax.shard_map(
        on_device, mesh=mesh, in_specs=in_specs, out_specs=out_specs, check_vma=False
    )
```

```python
import functools
import math

import jax
import jax.numpy as jnp
import numpy as np
from jax import lax
from jax.experimental import pallas as pl
from jax.experimental.pallas import tpu as pltpu
from jax.sharding import PartitionSpec as P

CLASSES = 48
ROT = 36
SHELLS = 16
ANG = 144
REACH = 3
SHIFTS = 49
BINS = 32
NGROUP = 16

STEP = ANG // ROT
CHANS = 2 * SHELLS
BLOCKS = CHANS // 2
BLOCK_COLS = 2 * ANG
LANES = CHANS * STEP
FREQS = ROT // 2 + 1
ROWS8 = 8
S_STEP = 4
S_PAD = -(-SHIFTS // S_STEP) * S_STEP
ROWS = S_PAD * ROWS8
LIVE = SHIFTS * ROWS8
COLS = 512
STEPS_A = 3
GROUP = 256
TAIL = 3 * LANES
TAIL_ROWS = 16
KPAD = 64
QUADS = (FREQS + 1) // 4
TILES = 3 * QUADS
PAY = TILES * ROWS8
BF = jnp.bfloat16
F8 = jnp.float8_e5m2
F32 = jnp.float32
MIB = 1024 * 1024


def block_order():
    return [m for m in range(0, BLOCKS, 2)] + [m for m in range(1, BLOCKS, 2)]


def lane_channel():
    chan, off = [], []
    for m in block_order():
        for cc in range(2):
            for d in range(STEP):
                chan.append(2 * m + cc)
                off.append(d)
    return np.array(chan), np.array(off)


def radius_of():
    return (np.arange(SHELLS, dtype=np.float64) + 1.0) / (2.0 * SHELLS)


def ctf_lanes():
    chan, _ = lane_channel()
    defocus = 1.0 + np.arange(BINS, dtype=np.float64) / BINS
    table = -np.sin(80.0 * defocus[:, None] * radius_of()[None, :] ** 2 + 0.1)
    return table[:, chan % SHELLS].astype(np.float32)


def shell_expand():
    chan, _ = lane_channel()
    return (np.arange(SHELLS)[:, None] == (chan % SHELLS)[None, :]).astype(np.float32)


def pixel_perm():
    table = np.zeros((BLOCK_COLS, BLOCK_COLS), np.float32)
    for b in range(ROT):
        for cc in range(2):
            for d in range(STEP):
                table[b * 8 + cc * STEP + d, cc * ANG + STEP * b + d] = 1.0
    return table


def phase_lanes():
    chan, off = lane_channel()
    shell = chan % SHELLS
    sign = np.where(chan < SHELLS, -1.0, 1.0)
    offsets = np.arange(2 * REACH + 1, dtype=np.float64) - REACH
    sx = np.repeat(offsets, 2 * REACH + 1)
    sy = np.tile(offsets, 2 * REACH + 1)
    angle = 2.0 * math.pi * (STEP * np.arange(ROT)[:, None] + off[None, :]) / ANG
    phase = (
        2.0
        * math.pi
        * radius_of()[shell][None, None, :]
        * (np.cos(angle)[None] * sx[:, None, None] + np.sin(angle)[None] * sy[:, None, None])
    )
    cos_t = np.zeros((S_PAD, ROT, LANES), np.float32)
    sin_t = np.zeros((S_PAD, ROT, LANES), np.float32)
    cos_t[:SHIFTS] = np.cos(phase)
    sin_t[:SHIFTS] = np.sin(phase) * sign[None, None, :]
    return np.concatenate([cos_t, sin_t], axis=1)


def refs_transform():
    table = np.zeros((FREQS, 2, 2, STEP, 2, ANG), np.float64)
    for q in range(FREQS):
        scale = (1.0 if q in (0, ROT // 2) else 2.0) / ROT
        for d in range(STEP):
            b = np.arange(ROT)
            turn = 2.0 * math.pi * ((q * b) % ROT) / ROT
            for cc in range(2):
                table[q, 0, cc, d, cc, STEP * b + d] = scale * np.cos(turn)
                if q not in (0, ROT // 2):
                    table[q, 1, cc, d, cc, STEP * b + d] = -scale * np.sin(turn)
    return table.reshape(FREQS * 16, BLOCK_COLS)


def inverse_transform():
    real = np.zeros((FREQS + 1, 2, STEP, 2, ANG), np.float64)
    imag = np.zeros((FREQS + 1, 2, STEP, 2, ANG), np.float64)
    b = np.arange(ROT)
    for q in range(FREQS):
        scale = (1.0 if q in (0, ROT // 2) else 2.0) / ROT
        turn = 2.0 * math.pi * ((q * b) % ROT) / ROT
        for cc in range(2):
            for d in range(STEP):
                real[q, cc, d, cc, STEP * b + d] = scale * np.cos(turn)
                if q not in (0, ROT // 2):
                    imag[q, cc, d, cc, STEP * b + d] = -scale * np.sin(turn)
    shape = (QUADS, 4, ROWS8, BLOCK_COLS)
    return [t.reshape(shape).transpose(1, 0, 2, 3).reshape(4 * QUADS * ROWS8, BLOCK_COLS) for t in (real, imag)]


def split(table):
    hi = table.astype(np.float32).astype(jnp.bfloat16)
    lo = (table - hi.astype(np.float64)).astype(np.float32).astype(jnp.bfloat16)
    return hi, lo


C1, C2 = math.cos(2 * math.pi / 9), math.cos(4 * math.pi / 9)
S1, S3, S4 = math.sin(2 * math.pi / 9), math.sin(6 * math.pi / 9), math.sin(8 * math.pi / 9)


def nine_cos(x0, s1, s2, s3, s4):
    u = s1 + s2 + s4
    v = x0 + s3
    base = x0 - 0.5 * s3
    a, b, c = s1 - s4, s2 - s4, s1 - s2
    p1 = C1 * a + C2 * b
    p2 = C2 * c - C1 * b
    return u + v, base + p1, base + p2, v - 0.5 * u, base - (p1 + p2)


def nine_sin(d1, d2, d3, d4):
    p, q, r = d1 + d2, d2 + d4, d1 - d4
    h = S3 * d3
    e1 = S1 * p + S4 * q
    e2 = S1 * r + S4 * p
    return e1 + h, e2 - h, S3 * (d1 - d2 + d4), (e2 - e1) + h


def nine_real(x):
    r = nine_cos(x[0], x[1] + x[8], x[2] + x[7], x[3] + x[6], x[4] + x[5])
    i = nine_sin(x[1] - x[8], x[2] - x[7], x[3] - x[6], x[4] - x[5])
    return r, (None,) + i


def crt(k1, k2):
    for k in range(ROT):
        if k % 4 == k1 and k % 9 == k2:
            return k
    return None


def forward36(x):
    re, im = [None] * FREQS, [None] * FREQS
    y0, y2, ya, yb = [], [], [], []
    for n2 in range(9):
        v = [x[(9 * n1 + 4 * n2) % ROT] for n1 in range(4)]
        t0, t1 = v[0] + v[2], v[1] + v[3]
        y0.append(t0 + t1)
        y2.append(t0 - t1)
        ya.append(v[0] - v[2])
        yb.append(v[3] - v[1])

    def put(k, real, imag):
        if k <= ROT // 2:
            re[k], im[k] = real, imag
        else:
            re[ROT - k], im[ROT - k] = real, -imag

    for k1, y in ((0, y0), (2, y2)):
        r, i = nine_real(y)
        k = crt(k1, 0)
        re[k] = r[0]
        for k2 in range(1, 5):
            k = crt(k1, k2)
            if k <= ROT // 2:
                re[k], im[k] = r[k2], -i[k2]
            else:
                re[ROT - k], im[ROT - k] = r[k2], i[k2]
    ra, ia = nine_real(ya)
    rb, ib = nine_real(yb)
    put(crt(1, 0), ra[0], rb[0])
    for k2 in range(1, 5):
        put(crt(1, k2), ra[k2] + ib[k2], rb[k2] - ia[k2])
        put(crt(1, 9 - k2), ra[k2] - ib[k2], rb[k2] + ia[k2])
    return re, im


def inverse36(re, im):
    def entry(k):
        if k <= ROT // 2:
            return re[k], im[k], 1
        return re[ROT - k], im[ROT - k], -1

    ys = []
    for k1 in (0, 2):
        real, imag = [entry(crt(k1, 0))[0]], [None]
        for k2 in range(1, 5):
            a, b, sign = entry(crt(k1, k2))
            real.append(a)
            imag.append(b if sign > 0 else -b)
        r = nine_cos(*real)
        i = (None,) + nine_sin(*imag[1:])
        y = [None] * 9
        y[0] = r[0]
        for n in range(1, 5):
            y[n], y[9 - n] = r[n] - i[n], r[n] + i[n]
        ys.append(y)
    xr, xi = [], []
    for k2 in range(9):
        a, b, sign = entry(crt(1, k2))
        xr.append(a)
        xi.append(b if sign > 0 else -b)
    rr, ir = nine_real(xr)
    ri, ii = nine_real(xi)
    ya, yb = [None] * 9, [None] * 9
    ya[0], yb[0] = rr[0], ri[0]
    for n in range(1, 5):
        ya[n], ya[9 - n] = rr[n] - ii[n], rr[n] + ii[n]
        yb[n], yb[9 - n] = ri[n] + ir[n], ri[n] - ir[n]
    x = [None] * ROT
    for n2 in range(9):
        t0, t1 = ys[0][n2] + ys[1][n2], ys[0][n2] - ys[1][n2]
        for n1, value in enumerate((t0 + ya[n2], t1 - yb[n2], t0 - ya[n2], t1 + yb[n2])):
            x[(9 * n1 + 4 * n2) % ROT] = value
    return x


def transform_steps(table_ref, pix_ref, slot_ref, fh_ref, fl_ref, first, count):
    slot = jnp.concatenate([slot_ref[...]] * 2, axis=0)
    nothing = jnp.zeros_like(slot)

    def step(i, _):
        parts = []
        for pair in range(S_STEP // 2):
            x = []
            for b in range(ROT):
                halves = []
                for h in range(2):
                    at = S_STEP * i + 2 * pair + h
                    c = table_ref[at, b : b + 1, :]
                    s = table_ref[at, ROT + b : ROT + b + 1, :]
                    halves.append(pix_ref[0, b] * c + pix_ref[1, b] * s)
                x.append(jnp.concatenate(halves, axis=0).astype(BF).astype(F32))
            re, im = forward36(x)
            im[0], im[ROT // 2] = slot, nothing
            row = pl.multiple_of((first + i) * S_STEP * ROWS8 + 16 * pair, 16)
            low = []
            for q in range(FREQS):
                for part, value in ((0, re[q]), (1, im[q])):
                    hi = value.astype(BF)
                    fh_ref[q, pl.ds(row, 16), part * LANES : (part + 1) * LANES] = hi
                    low.append(value - hi.astype(F32))
            parts.append(low)
        rows = pl.ds(pl.multiple_of((first + i) * S_STEP * ROWS8, S_STEP * ROWS8), S_STEP * ROWS8)
        for n, low in enumerate(zip(*parts)):
            cols = slice((n % 2) * LANES, (n % 2 + 1) * LANES)
            fl_ref[n // 2, rows, cols] = jnp.concatenate(low, axis=0).astype(F8)
        return 0

    lax.fori_loop(0, count, step, 0)


def first_kernel(
    grp_hbm, bin_hbm, img_hbm, sig_hbm, ctf_hbm, exp_hbm, perm_hbm, table_hbm,
    fh_ref, fl_ref, pix_ref, slot_ref, rest_ref,
    grp_ref, bin_ref, img_ref, sig_ref, ctf_ref, exp_ref, perm_ref, table_ref, noise_ref, sems,
):
    moves = [
        (grp_hbm, grp_ref), (bin_hbm, bin_ref), (img_hbm, img_ref), (sig_hbm, sig_ref),
        (ctf_hbm, ctf_ref), (exp_hbm, exp_ref), (perm_hbm, perm_ref),
        (table_hbm.at[pl.ds(0, S_STEP * STEPS_A)], table_ref),
        (table_hbm.at[pl.ds(S_STEP * STEPS_A, S_PAD - S_STEP * STEPS_A)], rest_ref),
    ]
    copies = [pltpu.make_async_copy(a, b, sems.at[i]) for i, (a, b) in enumerate(moves)]
    for copy in copies[:8]:
        copy.start()
    for copy in copies[:7]:
        copy.wait()
    copies[8].start()
    noise_ref[...] = jnp.dot(
        sig_ref[...], exp_ref[...], precision=lax.Precision.HIGHEST, preferred_element_type=F32
    )
    ctf = jnp.concatenate([ctf_ref[pl.ds(bin_ref[i], 1), :] for i in range(ROWS8)], axis=0)
    noise = jnp.concatenate([noise_ref[pl.ds(grp_ref[i], 1), :] for i in range(ROWS8)], axis=0)
    filt = ctf / noise
    weight = ctf * ctf / noise

    img = img_ref[...].astype(F32)
    stack = jnp.concatenate(
        [img[:, BLOCK_COLS * m : BLOCK_COLS * (m + 1)] for m in block_order()], axis=0
    ).astype(BF)
    turned = lax.dot_general(
        perm_ref[...], stack, (((1,), (1,)), ((), ())), preferred_element_type=F32
    )
    sub = lax.broadcasted_iota(jnp.int32, (ROWS8, LANES), 0)
    lane = lax.broadcasted_iota(jnp.int32, (ROWS8, LANES), 1)
    for b in range(ROT):
        y = turned[b * 8 : (b + 1) * 8]
        for t in (1, 2, 4):
            up = pltpu.roll(pltpu.roll(y, t, 0), LANES - t, 1)
            down = pltpu.roll(pltpu.roll(y, 8 - t, 0), t, 1)
            row_bit, lane_bit = (sub & t) != 0, (lane & t) != 0
            y = jnp.where(row_bit == lane_bit, y, jnp.where(row_bit, up, down))
        y = y * filt
        pix_ref[0, b] = y
        pix_ref[1, b] = jnp.where(
            (lane & 32) == 0, pltpu.roll(y, LANES - 32, 1), pltpu.roll(y, 32, 1)
        )

    off = lane & (STEP - 1)
    weight_hi = weight.astype(BF).astype(F32)
    slot_ref[...] = jnp.where(off == 0, weight_hi, jnp.where(off == 1, weight - weight_hi, 0.0))
    copies[7].wait()
    transform_steps(table_ref, pix_ref, slot_ref, fh_ref, fl_ref, 0, STEPS_A)
    copies[8].wait()


def second_kernel(
    fh_in, fl_in, table_ref, pix_ref, slot_ref, mt_hbm, back_hbm,
    fh_ref, fl_ref, mt_ref, back_ref, sems,
):
    del fh_in, fl_in
    copies = [
        pltpu.make_async_copy(mt_hbm, mt_ref, sems.at[0]),
        pltpu.make_async_copy(back_hbm, back_ref, sems.at[1]),
    ]
    for copy in copies:
        copy.start()
    transform_steps(
        table_ref, pix_ref, slot_ref, fh_ref, fl_ref, STEPS_A, S_PAD // S_STEP - STEPS_A
    )
    for copy in copies:
        copy.wait()


VM = pl.BlockSpec(memory_space=pltpu.VMEM)
HB = pl.BlockSpec(memory_space=pltpu.HBM)


def in_hbm(*arrays):
    return [pltpu.with_memory_space_constraint(a, pltpu.HBM) for a in arrays]


def cost(micros):
    return pl.CostEstimate(flops=int(micros * 1e9), bytes_accessed=int(micros * 3e6), transcendentals=0)


def first_features(images, sigma2, ctf_group, defocus_bin):
    feat = (FREQS, ROWS, 2 * LANES)
    tail = S_PAD - S_STEP * STEPS_A
    return pl.pallas_call(
        first_kernel,
        out_shape=(
            jax.ShapeDtypeStruct(feat, BF),
            jax.ShapeDtypeStruct(feat, F8),
            jax.ShapeDtypeStruct((2, ROT, ROWS8, LANES), F32),
            jax.ShapeDtypeStruct((ROWS8, LANES), F32),
            jax.ShapeDtypeStruct((tail, 2 * ROT, LANES), F32),
        ),
        in_specs=[HB] * 8,
        out_specs=[VM] * 5,
        scratch_shapes=[
            pltpu.SMEM((ROWS8,), jnp.int32),
            pltpu.SMEM((ROWS8,), jnp.int32),
            pltpu.VMEM(images.shape, BF),
            pltpu.VMEM(sigma2.shape, F32),
            pltpu.VMEM((BINS, LANES), F32),
            pltpu.VMEM((NGROUP, LANES), F32),
            pltpu.VMEM((BLOCK_COLS, BLOCK_COLS), BF),
            pltpu.VMEM((S_STEP * STEPS_A, 2 * ROT, LANES), F32),
            pltpu.VMEM((NGROUP, LANES), F32),
            pltpu.SemaphoreType.DMA((9,)),
        ],
        compiler_params=pltpu.CompilerParams(vmem_limit_bytes=20 * MIB),
        cost_estimate=cost(4.5),
        name="features_first",
    )(*in_hbm(
        ctf_group, defocus_bin, images, sigma2, jnp.asarray(ctf_lanes()),
        jnp.asarray(shell_expand()), jnp.asarray(pixel_perm(), BF), jnp.asarray(phase_lanes()),
    ))


def second_features(hi, lo, table, pix, slot):
    mt = np.stack(split(refs_transform()))
    back = np.stack([half for part in inverse_transform() for half in split(part)])
    return pl.pallas_call(
        second_kernel,
        out_shape=(
            jax.ShapeDtypeStruct(hi.shape, BF),
            jax.ShapeDtypeStruct(lo.shape, F8),
            jax.ShapeDtypeStruct(mt.shape, BF),
            jax.ShapeDtypeStruct(back.shape, BF),
        ),
        in_specs=[VM] * 5 + [HB] * 2,
        out_specs=[VM] * 4,
        scratch_shapes=[pltpu.SemaphoreType.DMA((2,))],
        input_output_aliases={0: 0, 1: 1},
        compiler_params=pltpu.CompilerParams(vmem_limit_bytes=16 * MIB),
        cost_estimate=cost(2.5),
        name="features_second",
    )(hi, lo, table, pix, slot, *in_hbm(jnp.asarray(mt), jnp.asarray(back)))


def nt(left, right):
    return lax.dot_general(left, right, (((1,), (1,)), ((), ())), preferred_element_type=F32)


def posterior_kernel(
    direct, r0_ref, r1_ref, r2_ref, r3_ref, s0_ref, s1_ref, s2_ref, s3_ref, fh_ref, fl_ref, mt_ref,
    out_ref, x_ref, d_ref, a_ref, e_ref, ca_ref, cb_ref, ct_ref, sa_ref, sb_ref, st_ref,
    pa_ref, pb_ref, pt_ref, q_ref, num_ref,
):
    lane = lax.broadcasted_iota(jnp.int32, (CLASSES, LANES), 1)
    lane8 = lax.broadcasted_iota(jnp.int32, (8, LANES), 1)
    row8 = lax.broadcasted_iota(jnp.int32, (8, LANES), 0)

    me = lax.axis_index("img") if direct else 0
    blank = jnp.zeros((KPAD - CLASSES, BLOCK_COLS), BF)
    for side, refs in enumerate(((r0_ref, r1_ref, r2_ref, r3_ref), (s0_ref, s1_ref, s2_ref, s3_ref))):
        for g, pair in enumerate(refs):
            for h in range(2):
                row = pl.multiple_of((me ^ (2 * g + 8 * h + side)) * KPAD, KPAD)
                x_ref[pl.ds(row, KPAD), :] = jnp.concatenate([pair[h], blank], axis=0)
    x = x_ref[...]
    d_ref[...] = nt(mt_ref[0], x) + nt(mt_ref[1], x)

    for t in range(BLOCKS // 2):
        cols = slice(t * LANES, (t + 1) * LANES)
        edge = jnp.zeros((8, LANES), F32)
        inner = jnp.zeros((8, LANES), F32)
        for q in range(FREQS):
            re = d_ref[q * 16 : q * 16 + 8, cols]
            if q in (0, ROT // 2):
                edge += re * re
            else:
                im = d_ref[q * 16 + 8 : q * 16 + 16, cols]
                inner += re * re + im * im
        power = -0.5 * (ROT * edge + (ROT // 2) * inner)
        power += pltpu.roll(power, 7, 0)
        power += pltpu.roll(power, 6, 0)
        power = jnp.where((row8 & (STEP - 1)) == 0, power, 0.0)
        d_ref[8:16, cols] = power + pltpu.roll(power, 1, 0)

    def operand(q):
        tile = jnp.concatenate(
            [
                d_ref[q * 16 + part * 8 : q * 16 + part * 8 + 8, t * LANES : (t + 1) * LANES]
                for part in range(2)
                for t in range(BLOCKS // 2)
            ],
            axis=0,
        )
        tile = tile.T
        even, odd = tile[:CLASSES], tile[KPAD : KPAD + CLASSES]
        real = jnp.where(lane < 64, even, pltpu.roll(odd, 64, 1))
        imag = jnp.where(lane < 64, pltpu.roll(even, 64, 1), odd)
        real_hi, imag_hi = real.astype(BF), imag.astype(BF)
        real_lo = (real - real_hi.astype(F32)).astype(BF)
        imag_lo = (imag - imag_hi.astype(F32)).astype(BF)
        for first, re, im in ((0, real_hi, imag_hi), (2 * CLASSES, real_lo, imag_lo)):
            a_ref[q, first : first + CLASSES, :LANES] = re
            a_ref[q, first : first + CLASSES, LANES:] = im
            a_ref[q, first + CLASSES : first + 2 * CLASSES, :LANES] = -im
            a_ref[q, first + CLASSES : first + 2 * CLASSES, LANES:] = re
        left = [jnp.concatenate([real, imag], axis=1), jnp.concatenate([-imag, real], axis=1)]
        e_ref[q] = jnp.concatenate(left, axis=0).astype(F8)

    tiles_k = CLASSES // 8

    def cross(q, rows):
        both = a_ref[q]
        first = nt(both, fh_ref[q, rows])
        return first[: 2 * CLASSES] + first[2 * CLASSES :] + nt(e_ref[q], fl_ref[q, rows])

    def cross_first(q):
        total = cross(q, slice(0, GROUP))
        if q + 1 < FREQS:
            operand(q + 1)
        ca_ref[2 * q] = total[:CLASSES]
        ca_ref[2 * q + 1] = total[CLASSES:]

    def cross_second(q):
        total = cross(q, slice(GROUP, ROWS))
        cb_ref[2 * q] = total[:CLASSES, : TAIL - GROUP]
        cb_ref[2 * q + 1] = total[CLASSES:, : TAIL - GROUP]
        last = total[:, TAIL - GROUP : TAIL - GROUP + TAIL_ROWS]
        last = jnp.concatenate([last, jnp.zeros((2 * CLASSES, LANES - TAIL_ROWS), F32)], axis=1)
        for part in range(2):
            packed = last[part * CLASSES : part * CLASSES + 8]
            for kt in range(1, tiles_k):
                row = part * CLASSES + kt * 8
                packed += pltpu.roll(last[row : row + 8], kt * TAIL_ROWS, 1)
            ct_ref[2 * q + part] = packed

    def tiles_of(c_ref, s_ref, p_ref):
        return [
            (c_ref, s_ref, p_ref, slice(row, row + 8), slice(col, col + LANES))
            for col in range(0, c_ref.shape[2], LANES)
            for row in range(0, c_ref.shape[1], 8)
        ]

    packed_live = ((lane8 & (TAIL_ROWS - 1)) < LIVE - TAIL) & (lane8 < tiles_k * TAIL_ROWS)

    def to_scores(where, top):
        c_ref, s_ref, _, rows, cols = where
        re = [c_ref[2 * q, rows, cols] for q in range(FREQS)]
        im = [None] + [c_ref[2 * q + 1, rows, cols] for q in range(1, FREQS - 1)] + [None]
        if c_ref is ct_ref:
            re[0] = jnp.where(packed_live, re[0], -1e30)
        x = inverse36(re, im)
        for r in range(ROT):
            s_ref[r, rows, cols] = x[r]
        while len(x) > 1:
            x = [jnp.maximum(*x[i : i + 2]) if i + 1 < len(x) else x[i] for i in range(0, len(x), 2)]
        return x[0] if top is None else jnp.maximum(top, x[0])

    def fold(v, op):
        for t in (4, 2, 1):
            v = op(v, pltpu.roll(v, t, 0))
        for t in (64, 32, 16, 8):
            v = op(v, pltpu.roll(v, t, 1))
        return v

    def to_posterior(where, top, total):
        _, s_ref, p_ref, rows, cols = where
        x = [jnp.exp(s_ref[r, rows, cols] - top) for r in range(ROT)]
        re, im = forward36(x)
        for q in range(FREQS):
            p_ref[2 * q, rows, cols] = re[q]
            if im[q] is not None:
                p_ref[2 * q + 1, rows, cols] = im[q]
        return re[0] if total is None else total + re[0]

    operand(0)
    for q in range(FREQS):
        cross_first(q)
    tiles_a = tiles_of(ca_ref, sa_ref, pa_ref)
    top_a = total_a = None
    todo = list(range(FREQS))
    for step, where in enumerate(tiles_a):
        top_a = to_scores(where, top_a)
        while todo and todo[0] * 2 * len(tiles_a) < (step + 1) * FREQS:
            cross_second(todo.pop(0))
    top_a = fold(top_a, jnp.maximum)
    for step, where in enumerate(tiles_a):
        total_a = to_posterior(where, top_a, total_a)
        while todo and todo[0] * 2 * len(tiles_a) < (len(tiles_a) + step + 1) * FREQS:
            cross_second(todo.pop(0))
    for q in todo:
        cross_second(q)
    tiles_b = tiles_of(cb_ref, sb_ref, pb_ref) + tiles_of(ct_ref, st_ref, pt_ref)
    top_b = total_b = None
    for where in tiles_b:
        top_b = to_scores(where, top_b)
    top_b = fold(top_b, jnp.maximum)
    for where in tiles_b:
        total_b = to_posterior(where, top_b, total_b)
    top = jnp.maximum(top_a, top_b)
    part_a, part_b = jnp.exp(top_a - top), jnp.exp(top_b - top)
    inverse = 1.0 / (part_a * fold(total_a, jnp.add) + part_b * fold(total_b, jnp.add))
    scale_a, scale_b = (part_a * inverse)[:1], (part_b * inverse)[:1]

    def scaled(q):
        for part in range(2):
            rows = slice(part * CLASSES, (part + 1) * CLASSES)
            if part == 1 and q in (0, ROT // 2):
                q_ref[q, rows, :] = jnp.zeros((CLASSES, COLS), BF)
                continue
            slot = 2 * q + part
            for col in range(0, GROUP, LANES):
                value = pa_ref[slot, :, col : col + LANES] * scale_a
                q_ref[q, rows, col : col + LANES] = value.astype(BF)
            q_ref[q, rows, GROUP:TAIL] = (pb_ref[slot] * scale_b).astype(BF)
            packed = jnp.where(packed_live, pt_ref[slot] * scale_b, 0.0)
            last = [packed] + [
                pltpu.roll(packed, LANES - kt * TAIL_ROWS, 1) for kt in range(1, tiles_k)
            ]
            last = jnp.where(lane < TAIL_ROWS, jnp.concatenate(last, axis=0), 0.0)
            q_ref[q, rows, TAIL:] = last.astype(BF)

    third = 2 * CLASSES // 3
    order = [4 * quad + slot for quad in range(QUADS) for slot in (3, 0, 1, 2)]
    order = [q for q in order if q < FREQS]
    extra = jnp.zeros((2 * CLASSES, LANES), F32)
    scaled(order[0])
    for n, q in enumerate(order):
        o = jnp.dot(q_ref[q, :, :ROWS], fh_ref[q], preferred_element_type=F32)
        if n + 1 < len(order):
            scaled(order[n + 1])
        real = o[:CLASSES, :LANES] + o[CLASSES:, LANES:]
        imag = o[:CLASSES, LANES:] - o[CLASSES:, :LANES]
        both = jnp.concatenate([real, imag], axis=0)
        quad, slot = q // 4, q % 4
        if slot == 3:
            extra = both
            continue
        if 4 * quad + 3 >= FREQS:
            extra = jnp.zeros((2 * CLASSES, LANES), F32)
        tile = [both, extra[slot * third : (slot + 1) * third]]
        num_ref[slot * QUADS + quad] = jnp.concatenate(tile, axis=0).T
    core, chip = me % 2, me // 2
    for half in range(2):
        side = (1 - core) if half == 0 else core
        for e in range(BLOCKS // 2):
            row = side * (LANES // 2) + (chip ^ (e // 2 + 4 * (e % 2))) * ROWS8
            row = pl.multiple_of(row, ROWS8)
            out_ref[half, e] = num_ref[:, pl.ds(row, 8), :].reshape(PAY, LANES).astype(BF)


def make_payload(direct, refs, feat_hi, feat_lo, mt):
    return pl.pallas_call(
        functools.partial(posterior_kernel, direct),
        out_shape=jax.ShapeDtypeStruct((2, BLOCKS // 2, PAY, LANES), BF),
        in_specs=[VM] * 11,
        out_specs=VM,
        scratch_shapes=[
            pltpu.VMEM((BLOCKS * KPAD, BLOCK_COLS), BF),
            pltpu.VMEM((FREQS * 16, BLOCKS * KPAD), F32),
            pltpu.VMEM((FREQS, 4 * CLASSES, 2 * LANES), BF),
            pltpu.VMEM((FREQS, 2 * CLASSES, 2 * LANES), F8),
            pltpu.VMEM((2 * FREQS, CLASSES, GROUP), F32),
            pltpu.VMEM((2 * FREQS, CLASSES, TAIL - GROUP), F32),
            pltpu.VMEM((2 * FREQS, 8, LANES), F32),
            pltpu.VMEM((ROT, CLASSES, GROUP), F32),
            pltpu.VMEM((ROT, CLASSES, TAIL - GROUP), F32),
            pltpu.VMEM((ROT, 8, LANES), F32),
            pltpu.VMEM((2 * FREQS, CLASSES, GROUP), F32),
            pltpu.VMEM((2 * FREQS, CLASSES, TAIL - GROUP), F32),
            pltpu.VMEM((2 * FREQS, 8, LANES), F32),
            pltpu.VMEM((FREQS, 2 * CLASSES, COLS), BF),
            pltpu.VMEM((TILES, LANES, LANES), F32),
        ],
        compiler_params=pltpu.CompilerParams(vmem_limit_bytes=28 * MIB),
        cost_estimate=cost(10.0),
        name="posterior",
    )(*refs, feat_hi, feat_lo, mt)


def final_kernel(keep_ref, got_ref, back_ref, out_ref):
    total = keep_ref[...] + got_ref[...].astype(F32)
    turned = total.T
    width = QUADS * ROWS8
    third = 2 * CLASSES // 3
    last = jnp.concatenate(
        [turned[2 * CLASSES :, slot * width : (slot + 1) * width] for slot in range(3)], axis=0
    )
    numer = jnp.zeros((CLASSES, BLOCK_COLS), F32)
    for part in range(2):
        rows = slice(part * CLASSES, (part + 1) * CLASSES)
        for value, first in ((turned[rows], 0), (last[rows], 3 * width)):
            span = slice(first, first + value.shape[1])
            hi = value.astype(BF)
            lo = (value - hi.astype(F32)).astype(BF)
            dot = functools.partial(jnp.dot, preferred_element_type=F32)
            table_hi, table_lo = back_ref[2 * part, span], back_ref[2 * part + 1, span]
            numer += dot(hi, table_hi) + dot(lo, table_hi) + dot(hi, table_lo)
    weights = turned[CLASSES : 2 * CLASSES]
    column = lax.broadcasted_iota(jnp.int32, (CLASSES, BLOCK_COLS), 1)
    first = weights[:, 0:1] + weights[:, 1:2]
    second = weights[:, STEP : STEP + 1] + weights[:, STEP + 1 : STEP + 2]
    out_ref[...] = numer / (jnp.where(column < ANG, first, second) + 1.0)


def finish(keep, got, back):
    return pl.pallas_call(
        final_kernel,
        out_shape=jax.ShapeDtypeStruct((CLASSES, BLOCK_COLS), F32),
        in_specs=[VM] * 3,
        out_specs=VM,
        compiler_params=pltpu.CompilerParams(vmem_limit_bytes=8 * MIB),
        cost_estimate=cost(1.0),
        name="finish",
    )(keep, got, back)


def swap(value, distance):
    pairs = [(i, i ^ distance) for i in range(lax.axis_size("img"))]
    return lax.ppermute(value, "img", pairs)


def reduce_direct(pay):
    pairs = pay[1].astype(F32) + swap(pay[0], 1).astype(F32)
    pairs = pairs.reshape((4, BLOCKS // 8) + pairs.shape[1:])
    parts = [swap(pairs[g].astype(BF), 2 * g) for g in (1, 2, 3)]
    total = pairs[0]
    for part in parts:
        total = total + part.astype(F32)
    return total[0], swap(total[1].astype(BF), 8)


def on_device(images, class_refs, sigma2, ctf_group, defocus_bin):
    devices = lax.axis_size("img")
    share = class_refs.shape[1]
    me = lax.axis_index("img")
    direct = devices == BLOCKS and share == BLOCK_COLS
    if direct:
        near = swap(class_refs, 8)
    else:
        whole = lax.all_gather(class_refs, "img", axis=1, tiled=True)
        blocks = whole.reshape(CLASSES, BLOCKS, BLOCK_COLS).transpose(1, 0, 2)
        refs = [jnp.stack([blocks[2 * g + s], blocks[2 * g + s + 8]]) for s in range(2) for g in range(4)]
    pay = None
    for first in range(0, images.shape[0], ROWS8):
        part = slice(first, first + ROWS8)
        hi, lo, pix, slot, table = first_features(
            images[part], sigma2, ctf_group[part], defocus_bin[part]
        )
        if direct and first == 0:
            near, hi = lax.optimization_barrier((near, hi))
            near = jnp.stack([class_refs, near])
            rest = [swap(near, 2 * g) for g in (1, 2, 3)]
        hi, lo, mt, back = second_features(hi, lo, table, pix, slot)
        if direct and first == 0:
            other = [swap(near, 1)]
            other[0], hi = lax.optimization_barrier((other[0], hi))
            for g in range(3):
                rest[g], hi = lax.optimization_barrier((rest[g], hi))
                other.append(swap(rest[g], 1))
            refs = [near] + rest + other
        one = make_payload(direct, refs, hi, lo, mt)
        pay = one if pay is None else pay + one
    if direct:
        return finish(*reduce_direct(pay), back)
    summed = lax.psum(pay.astype(F32), "img")
    start = me * share
    block = start // BLOCK_COLS
    chip = block // 2
    mine = summed[1 - block % 2, 2 * (chip % 4) + chip // 4]
    return lax.dynamic_slice_in_dim(
        finish(mine, jnp.zeros_like(mine, BF), back), start % BLOCK_COLS, share, 1
    )


def solution(mesh):
    in_specs = (
        P(("groups", "img"), None),
        P("groups", "img"),
        P("groups", None),
        P(("groups", "img")),
        P(("groups", "img")),
    )
    out_specs = P("groups", "img")
    return jax.shard_map(
        on_device, mesh=mesh, in_specs=in_specs, out_specs=out_specs, check_vma=False
    )
```

```python
import functools
import math

import jax
import jax.numpy as jnp
import numpy as np
from jax import lax
from jax.experimental import pallas as pl
from jax.experimental.pallas import tpu as pltpu
from jax.sharding import PartitionSpec as P

CLASSES = 48
ROT = 36
SHELLS = 16
ANG = 144
REACH = 3
SHIFTS = 49
BINS = 32
NGROUP = 16

STEP = ANG // ROT
CHANS = 2 * SHELLS
BLOCKS = CHANS // 2
BLOCK_COLS = 2 * ANG
LANES = CHANS * STEP
FREQS = ROT // 2 + 1
ROWS8 = 8
S_STEP = 4
S_PAD = -(-SHIFTS // S_STEP) * S_STEP
ROWS = S_PAD * ROWS8
LIVE = SHIFTS * ROWS8
COLS = 512
STEPS_A = 3
GROUP = 256
TAIL = 3 * LANES
TAIL_ROWS = 16
KPAD = 64
QUADS = (FREQS + 1) // 4
TILES = 3 * QUADS
PAY = TILES * ROWS8
BF = jnp.bfloat16
F8 = jnp.float8_e5m2
F32 = jnp.float32
MIB = 1024 * 1024


def block_order():
    return [m for m in range(0, BLOCKS, 2)] + [m for m in range(1, BLOCKS, 2)]


def lane_channel():
    chan, off = [], []
    for m in block_order():
        for cc in range(2):
            for d in range(STEP):
                chan.append(2 * m + cc)
                off.append(d)
    return np.array(chan), np.array(off)


def radius_of():
    return (np.arange(SHELLS, dtype=np.float64) + 1.0) / (2.0 * SHELLS)


def ctf_lanes():
    chan, _ = lane_channel()
    defocus = 1.0 + np.arange(BINS, dtype=np.float64) / BINS
    table = -np.sin(80.0 * defocus[:, None] * radius_of()[None, :] ** 2 + 0.1)
    return table[:, chan % SHELLS].astype(np.float32)


def shell_expand():
    chan, _ = lane_channel()
    return (np.arange(SHELLS)[:, None] == (chan % SHELLS)[None, :]).astype(np.float32)


def pixel_perm():
    table = np.zeros((BLOCK_COLS, BLOCK_COLS), np.float32)
    for b in range(ROT):
        for cc in range(2):
            for d in range(STEP):
                table[b * 8 + cc * STEP + d, cc * ANG + STEP * b + d] = 1.0
    return table


def phase_lanes():
    chan, off = lane_channel()
    shell = chan % SHELLS
    sign = np.where(chan < SHELLS, -1.0, 1.0)
    offsets = np.arange(2 * REACH + 1, dtype=np.float64) - REACH
    sx = np.repeat(offsets, 2 * REACH + 1)
    sy = np.tile(offsets, 2 * REACH + 1)
    angle = 2.0 * math.pi * (STEP * np.arange(ROT)[:, None] + off[None, :]) / ANG
    phase = (
        2.0
        * math.pi
        * radius_of()[shell][None, None, :]
        * (np.cos(angle)[None] * sx[:, None, None] + np.sin(angle)[None] * sy[:, None, None])
    )
    cos_t = np.zeros((S_PAD, ROT, LANES), np.float32)
    sin_t = np.zeros((S_PAD, ROT, LANES), np.float32)
    cos_t[:SHIFTS] = np.cos(phase)
    sin_t[:SHIFTS] = np.sin(phase) * sign[None, None, :]
    return np.concatenate([cos_t, sin_t], axis=1)


def refs_transform():
    table = np.zeros((FREQS, 2, 2, STEP, 2, ANG), np.float64)
    for q in range(FREQS):
        scale = (1.0 if q in (0, ROT // 2) else 2.0) / ROT
        for d in range(STEP):
            b = np.arange(ROT)
            turn = 2.0 * math.pi * ((q * b) % ROT) / ROT
            for cc in range(2):
                table[q, 0, cc, d, cc, STEP * b + d] = scale * np.cos(turn)
                if q not in (0, ROT // 2):
                    table[q, 1, cc, d, cc, STEP * b + d] = -scale * np.sin(turn)
    return table.reshape(FREQS * 16, BLOCK_COLS)


def inverse_transform():
    real = np.zeros((FREQS + 1, 2, STEP, 2, ANG), np.float64)
    imag = np.zeros((FREQS + 1, 2, STEP, 2, ANG), np.float64)
    b = np.arange(ROT)
    for q in range(FREQS):
        scale = (1.0 if q in (0, ROT // 2) else 2.0) / ROT
        turn = 2.0 * math.pi * ((q * b) % ROT) / ROT
        for cc in range(2):
            for d in range(STEP):
                real[q, cc, d, cc, STEP * b + d] = scale * np.cos(turn)
                if q not in (0, ROT // 2):
                    imag[q, cc, d, cc, STEP * b + d] = -scale * np.sin(turn)
    shape = (QUADS, 4, ROWS8, BLOCK_COLS)
    return [t.reshape(shape).transpose(1, 0, 2, 3).reshape(4 * QUADS * ROWS8, BLOCK_COLS) for t in (real, imag)]


def split(table):
    hi = table.astype(np.float32).astype(jnp.bfloat16)
    lo = (table - hi.astype(np.float64)).astype(np.float32).astype(jnp.bfloat16)
    return hi, lo


C1, C2 = math.cos(2 * math.pi / 9), math.cos(4 * math.pi / 9)
S1, S3, S4 = math.sin(2 * math.pi / 9), math.sin(6 * math.pi / 9), math.sin(8 * math.pi / 9)


def nine_cos(x0, s1, s2, s3, s4):
    u = s1 + s2 + s4
    v = x0 + s3
    base = x0 - 0.5 * s3
    a, b, c = s1 - s4, s2 - s4, s1 - s2
    p1 = C1 * a + C2 * b
    p2 = C2 * c - C1 * b
    return u + v, base + p1, base + p2, v - 0.5 * u, base - (p1 + p2)


def nine_sin(d1, d2, d3, d4):
    p, q, r = d1 + d2, d2 + d4, d1 - d4
    h = S3 * d3
    e1 = S1 * p + S4 * q
    e2 = S1 * r + S4 * p
    return e1 + h, e2 - h, S3 * (d1 - d2 + d4), (e2 - e1) + h


def nine_real(x):
    r = nine_cos(x[0], x[1] + x[8], x[2] + x[7], x[3] + x[6], x[4] + x[5])
    i = nine_sin(x[1] - x[8], x[2] - x[7], x[3] - x[6], x[4] - x[5])
    return r, (None,) + i


def crt(k1, k2):
    for k in range(ROT):
        if k % 4 == k1 and k % 9 == k2:
            return k
    return None


def forward36(x):
    re, im = [None] * FREQS, [None] * FREQS
    y0, y2, ya, yb = [], [], [], []
    for n2 in range(9):
        v = [x[(9 * n1 + 4 * n2) % ROT] for n1 in range(4)]
        t0, t1 = v[0] + v[2], v[1] + v[3]
        y0.append(t0 + t1)
        y2.append(t0 - t1)
        ya.append(v[0] - v[2])
        yb.append(v[3] - v[1])

    def put(k, real, imag):
        if k <= ROT // 2:
            re[k], im[k] = real, imag
        else:
            re[ROT - k], im[ROT - k] = real, -imag

    for k1, y in ((0, y0), (2, y2)):
        r, i = nine_real(y)
        k = crt(k1, 0)
        re[k] = r[0]
        for k2 in range(1, 5):
            k = crt(k1, k2)
            if k <= ROT // 2:
                re[k], im[k] = r[k2], -i[k2]
            else:
                re[ROT - k], im[ROT - k] = r[k2], i[k2]
    ra, ia = nine_real(ya)
    rb, ib = nine_real(yb)
    put(crt(1, 0), ra[0], rb[0])
    for k2 in range(1, 5):
        put(crt(1, k2), ra[k2] + ib[k2], rb[k2] - ia[k2])
        put(crt(1, 9 - k2), ra[k2] - ib[k2], rb[k2] + ia[k2])
    return re, im


def inverse36(re, im):
    def entry(k):
        if k <= ROT // 2:
            return re[k], im[k], 1
        return re[ROT - k], im[ROT - k], -1

    ys = []
    for k1 in (0, 2):
        real, imag = [entry(crt(k1, 0))[0]], [None]
        for k2 in range(1, 5):
            a, b, sign = entry(crt(k1, k2))
            real.append(a)
            imag.append(b if sign > 0 else -b)
        r = nine_cos(*real)
        i = (None,) + nine_sin(*imag[1:])
        y = [None] * 9
        y[0] = r[0]
        for n in range(1, 5):
            y[n], y[9 - n] = r[n] - i[n], r[n] + i[n]
        ys.append(y)
    xr, xi = [], []
    for k2 in range(9):
        a, b, sign = entry(crt(1, k2))
        xr.append(a)
        xi.append(b if sign > 0 else -b)
    rr, ir = nine_real(xr)
    ri, ii = nine_real(xi)
    ya, yb = [None] * 9, [None] * 9
    ya[0], yb[0] = rr[0], ri[0]
    for n in range(1, 5):
        ya[n], ya[9 - n] = rr[n] - ii[n], rr[n] + ii[n]
        yb[n], yb[9 - n] = ri[n] + ir[n], ri[n] - ir[n]
    x = [None] * ROT
    for n2 in range(9):
        t0, t1 = ys[0][n2] + ys[1][n2], ys[0][n2] - ys[1][n2]
        for n1, value in enumerate((t0 + ya[n2], t1 - yb[n2], t0 - ya[n2], t1 + yb[n2])):
            x[(9 * n1 + 4 * n2) % ROT] = value
    return x


def transform_steps(table_ref, pix_ref, slot_ref, fh_ref, fl_ref, first, count):
    slot = jnp.concatenate([slot_ref[...]] * 2, axis=0)
    nothing = jnp.zeros_like(slot)

    def step(i, _):
        parts = []
        for pair in range(S_STEP // 2):
            x = []
            for b in range(ROT):
                halves = []
                for h in range(2):
                    at = S_STEP * i + 2 * pair + h
                    c = table_ref[at, b : b + 1, :]
                    s = table_ref[at, ROT + b : ROT + b + 1, :]
                    halves.append(pix_ref[0, b] * c + pix_ref[1, b] * s)
                x.append(jnp.concatenate(halves, axis=0).astype(BF).astype(F32))
            re, im = forward36(x)
            im[0], im[ROT // 2] = slot, nothing
            row = pl.multiple_of((first + i) * S_STEP * ROWS8 + 16 * pair, 16)
            low = []
            for q in range(FREQS):
                for part, value in ((0, re[q]), (1, im[q])):
                    hi = value.astype(BF)
                    fh_ref[q, pl.ds(row, 16), part * LANES : (part + 1) * LANES] = hi
                    low.append(value - hi.astype(F32))
            parts.append(low)
        rows = pl.ds(pl.multiple_of((first + i) * S_STEP * ROWS8, S_STEP * ROWS8), S_STEP * ROWS8)
        for n, low in enumerate(zip(*parts)):
            cols = slice((n % 2) * LANES, (n % 2 + 1) * LANES)
            fl_ref[n // 2, rows, cols] = jnp.concatenate(low, axis=0).astype(F8)
        return 0

    lax.fori_loop(0, count, step, 0)


def first_kernel(
    grp_hbm, bin_hbm, img_hbm, sig_hbm, ctf_hbm, exp_hbm, perm_hbm, table_hbm,
    fh_ref, fl_ref, pix_ref, slot_ref, rest_ref,
    grp_ref, bin_ref, img_ref, sig_ref, ctf_ref, exp_ref, perm_ref, table_ref, noise_ref, sems,
):
    moves = [
        (grp_hbm, grp_ref), (bin_hbm, bin_ref), (img_hbm, img_ref), (sig_hbm, sig_ref),
        (ctf_hbm, ctf_ref), (exp_hbm, exp_ref), (perm_hbm, perm_ref),
        (table_hbm.at[pl.ds(0, S_STEP * STEPS_A)], table_ref),
        (table_hbm.at[pl.ds(S_STEP * STEPS_A, S_PAD - S_STEP * STEPS_A)], rest_ref),
    ]
    copies = [pltpu.make_async_copy(a, b, sems.at[i]) for i, (a, b) in enumerate(moves)]
    for copy in copies[:8]:
        copy.start()
    for copy in copies[:7]:
        copy.wait()
    copies[8].start()
    noise_ref[...] = jnp.dot(
        sig_ref[...], exp_ref[...], precision=lax.Precision.HIGHEST, preferred_element_type=F32
    )
    ctf = jnp.concatenate([ctf_ref[pl.ds(bin_ref[i], 1), :] for i in range(ROWS8)], axis=0)
    noise = jnp.concatenate([noise_ref[pl.ds(grp_ref[i], 1), :] for i in range(ROWS8)], axis=0)
    filt = ctf / noise
    weight = ctf * ctf / noise

    img = img_ref[...].astype(F32)
    stack = jnp.concatenate(
        [img[:, BLOCK_COLS * m : BLOCK_COLS * (m + 1)] for m in block_order()], axis=0
    ).astype(BF)
    turned = lax.dot_general(
        perm_ref[...], stack, (((1,), (1,)), ((), ())), preferred_element_type=F32
    )
    sub = lax.broadcasted_iota(jnp.int32, (ROWS8, LANES), 0)
    lane = lax.broadcasted_iota(jnp.int32, (ROWS8, LANES), 1)
    for b in range(ROT):
        y = turned[b * 8 : (b + 1) * 8]
        for t in (1, 2, 4):
            up = pltpu.roll(pltpu.roll(y, t, 0), LANES - t, 1)
            down = pltpu.roll(pltpu.roll(y, 8 - t, 0), t, 1)
            row_bit, lane_bit = (sub & t) != 0, (lane & t) != 0
            y = jnp.where(row_bit == lane_bit, y, jnp.where(row_bit, up, down))
        y = y * filt
        pix_ref[0, b] = y
        pix_ref[1, b] = jnp.where(
            (lane & 32) == 0, pltpu.roll(y, LANES - 32, 1), pltpu.roll(y, 32, 1)
        )

    off = lane & (STEP - 1)
    weight_hi = weight.astype(BF).astype(F32)
    slot_ref[...] = jnp.where(off == 0, weight_hi, jnp.where(off == 1, weight - weight_hi, 0.0))
    copies[7].wait()
    transform_steps(table_ref, pix_ref, slot_ref, fh_ref, fl_ref, 0, STEPS_A)
    copies[8].wait()


def second_kernel(
    fh_in, fl_in, table_ref, pix_ref, slot_ref, mt_hbm, back_hbm,
    fh_ref, fl_ref, mt_ref, back_ref, sems,
):
    del fh_in, fl_in
    copies = [
        pltpu.make_async_copy(mt_hbm, mt_ref, sems.at[0]),
        pltpu.make_async_copy(back_hbm, back_ref, sems.at[1]),
    ]
    for copy in copies:
        copy.start()
    transform_steps(
        table_ref, pix_ref, slot_ref, fh_ref, fl_ref, STEPS_A, S_PAD // S_STEP - STEPS_A
    )
    for copy in copies:
        copy.wait()


VM = pl.BlockSpec(memory_space=pltpu.VMEM)
HB = pl.BlockSpec(memory_space=pltpu.HBM)


def in_hbm(*arrays):
    return [pltpu.with_memory_space_constraint(a, pltpu.HBM) for a in arrays]


def cost(micros):
    return pl.CostEstimate(flops=int(micros * 1e9), bytes_accessed=int(micros * 3e6), transcendentals=0)


def first_features(images, sigma2, ctf_group, defocus_bin):
    feat = (FREQS, ROWS, 2 * LANES)
    tail = S_PAD - S_STEP * STEPS_A
    return pl.pallas_call(
        first_kernel,
        out_shape=(
            jax.ShapeDtypeStruct(feat, BF),
            jax.ShapeDtypeStruct(feat, F8),
            jax.ShapeDtypeStruct((2, ROT, ROWS8, LANES), F32),
            jax.ShapeDtypeStruct((ROWS8, LANES), F32),
            jax.ShapeDtypeStruct((tail, 2 * ROT, LANES), F32),
        ),
        in_specs=[HB] * 8,
        out_specs=[VM] * 5,
        scratch_shapes=[
            pltpu.SMEM((ROWS8,), jnp.int32),
            pltpu.SMEM((ROWS8,), jnp.int32),
            pltpu.VMEM(images.shape, BF),
            pltpu.VMEM(sigma2.shape, F32),
            pltpu.VMEM((BINS, LANES), F32),
            pltpu.VMEM((NGROUP, LANES), F32),
            pltpu.VMEM((BLOCK_COLS, BLOCK_COLS), BF),
            pltpu.VMEM((S_STEP * STEPS_A, 2 * ROT, LANES), F32),
            pltpu.VMEM((NGROUP, LANES), F32),
            pltpu.SemaphoreType.DMA((9,)),
        ],
        compiler_params=pltpu.CompilerParams(vmem_limit_bytes=20 * MIB),
        cost_estimate=cost(4.5),
        name="features_first",
    )(*in_hbm(
        ctf_group, defocus_bin, images, sigma2, jnp.asarray(ctf_lanes()),
        jnp.asarray(shell_expand()), jnp.asarray(pixel_perm(), BF), jnp.asarray(phase_lanes()),
    ))


def second_features(hi, lo, table, pix, slot):
    mt = np.stack(split(refs_transform()))
    back = np.stack([half for part in inverse_transform() for half in split(part)])
    return pl.pallas_call(
        second_kernel,
        out_shape=(
            jax.ShapeDtypeStruct(hi.shape, BF),
            jax.ShapeDtypeStruct(lo.shape, F8),
            jax.ShapeDtypeStruct(mt.shape, BF),
            jax.ShapeDtypeStruct(back.shape, BF),
        ),
        in_specs=[VM] * 5 + [HB] * 2,
        out_specs=[VM] * 4,
        scratch_shapes=[pltpu.SemaphoreType.DMA((2,))],
        input_output_aliases={0: 0, 1: 1},
        compiler_params=pltpu.CompilerParams(vmem_limit_bytes=16 * MIB),
        cost_estimate=cost(2.5),
        name="features_second",
    )(hi, lo, table, pix, slot, *in_hbm(jnp.asarray(mt), jnp.asarray(back)))


def nt(left, right):
    return lax.dot_general(left, right, (((1,), (1,)), ((), ())), preferred_element_type=F32)


def posterior_kernel(
    direct, r0_ref, r1_ref, r2_ref, r3_ref, s0_ref, s1_ref, s2_ref, s3_ref, fh_ref, fl_ref, mt_ref,
    out_ref, x_ref, d_ref, a_ref, e_ref, ca_ref, cb_ref, ct_ref, sa_ref, sb_ref, st_ref,
    pa_ref, pb_ref, pt_ref, q_ref, num_ref,
):
    lane = lax.broadcasted_iota(jnp.int32, (CLASSES, LANES), 1)
    lane8 = lax.broadcasted_iota(jnp.int32, (8, LANES), 1)
    row8 = lax.broadcasted_iota(jnp.int32, (8, LANES), 0)

    me = lax.axis_index("img") if direct else 0
    blank = jnp.zeros((KPAD - CLASSES, BLOCK_COLS), BF)
    for side, refs in enumerate(((r0_ref, r1_ref, r2_ref, r3_ref), (s0_ref, s1_ref, s2_ref, s3_ref))):
        for g, pair in enumerate(refs):
            for h in range(2):
                row = pl.multiple_of((me ^ (2 * g + 8 * h + side)) * KPAD, KPAD)
                x_ref[pl.ds(row, KPAD), :] = jnp.concatenate([pair[h], blank], axis=0)
    x = x_ref[...]
    d_ref[...] = nt(mt_ref[0], x) + nt(mt_ref[1], x)

    for t in range(BLOCKS // 2):
        cols = slice(t * LANES, (t + 1) * LANES)
        edge = jnp.zeros((8, LANES), F32)
        inner = jnp.zeros((8, LANES), F32)
        for q in range(FREQS):
            re = d_ref[q * 16 : q * 16 + 8, cols]
            if q in (0, ROT // 2):
                edge += re * re
            else:
                im = d_ref[q * 16 + 8 : q * 16 + 16, cols]
                inner += re * re + im * im
        power = -0.5 * (ROT * edge + (ROT // 2) * inner)
        power += pltpu.roll(power, 7, 0)
        power += pltpu.roll(power, 6, 0)
        power = jnp.where((row8 & (STEP - 1)) == 0, power, 0.0)
        d_ref[8:16, cols] = power + pltpu.roll(power, 1, 0)

    def operand(q):
        tile = jnp.concatenate(
            [
                d_ref[q * 16 + part * 8 : q * 16 + part * 8 + 8, t * LANES : (t + 1) * LANES]
                for part in range(2)
                for t in range(BLOCKS // 2)
            ],
            axis=0,
        )
        tile = tile.T
        even, odd = tile[:CLASSES], tile[KPAD : KPAD + CLASSES]
        real = jnp.where(lane < 64, even, pltpu.roll(odd, 64, 1))
        imag = jnp.where(lane < 64, pltpu.roll(even, 64, 1), odd)
        real_hi, imag_hi = real.astype(BF), imag.astype(BF)
        real_lo = (real - real_hi.astype(F32)).astype(BF)
        imag_lo = (imag - imag_hi.astype(F32)).astype(BF)
        for first, re, im in ((0, real_hi, imag_hi), (2 * CLASSES, real_lo, imag_lo)):
            a_ref[q, first : first + CLASSES, :LANES] = re
            a_ref[q, first : first + CLASSES, LANES:] = im
            a_ref[q, first + CLASSES : first + 2 * CLASSES, :LANES] = -im
            a_ref[q, first + CLASSES : first + 2 * CLASSES, LANES:] = re
        left = [jnp.concatenate([real, imag], axis=1), jnp.concatenate([-imag, real], axis=1)]
        e_ref[q] = jnp.concatenate(left, axis=0).astype(F8)

    tiles_k = CLASSES // 8

    def cross(q, rows):
        both = a_ref[q]
        first = nt(both, fh_ref[q, rows])
        return first[: 2 * CLASSES] + first[2 * CLASSES :] + nt(e_ref[q], fl_ref[q, rows])

    def cross_first(q):
        total = cross(q, slice(0, GROUP))
        if q + 1 < FREQS:
            operand(q + 1)
        ca_ref[2 * q] = total[:CLASSES]
        ca_ref[2 * q + 1] = total[CLASSES:]

    def cross_second(q):
        total = cross(q, slice(GROUP, ROWS))
        cb_ref[2 * q] = total[:CLASSES, : TAIL - GROUP]
        cb_ref[2 * q + 1] = total[CLASSES:, : TAIL - GROUP]
        last = total[:, TAIL - GROUP : TAIL - GROUP + TAIL_ROWS]
        last = jnp.concatenate([last, jnp.zeros((2 * CLASSES, LANES - TAIL_ROWS), F32)], axis=1)
        for part in range(2):
            packed = last[part * CLASSES : part * CLASSES + 8]
            for kt in range(1, tiles_k):
                row = part * CLASSES + kt * 8
                packed += pltpu.roll(last[row : row + 8], kt * TAIL_ROWS, 1)
            ct_ref[2 * q + part] = packed

    def tiles_of(c_ref, s_ref, p_ref):
        return [
            (c_ref, s_ref, p_ref, slice(row, row + 8), slice(col, col + LANES))
            for col in range(0, c_ref.shape[2], LANES)
            for row in range(0, c_ref.shape[1], 8)
        ]

    packed_live = ((lane8 & (TAIL_ROWS - 1)) < LIVE - TAIL) & (lane8 < tiles_k * TAIL_ROWS)

    def to_scores(where, top):
        c_ref, s_ref, _, rows, cols = where
        re = [c_ref[2 * q, rows, cols] for q in range(FREQS)]
        im = [None] + [c_ref[2 * q + 1, rows, cols] for q in range(1, FREQS - 1)] + [None]
        if c_ref is ct_ref:
            re[0] = jnp.where(packed_live, re[0], -1e30)
        x = inverse36(re, im)
        for r in range(ROT):
            s_ref[r, rows, cols] = x[r]
        while len(x) > 1:
            x = [jnp.maximum(*x[i : i + 2]) if i + 1 < len(x) else x[i] for i in range(0, len(x), 2)]
        return x[0] if top is None else jnp.maximum(top, x[0])

    def fold(v, op):
        for t in (4, 2, 1):
            v = op(v, pltpu.roll(v, t, 0))
        for t in (64, 32, 16, 8):
            v = op(v, pltpu.roll(v, t, 1))
        return v

    def to_posterior(where, top, total):
        _, s_ref, p_ref, rows, cols = where
        x = [jnp.exp(s_ref[r, rows, cols] - top) for r in range(ROT)]
        re, im = forward36(x)
        for q in range(FREQS):
            p_ref[2 * q, rows, cols] = re[q]
            if im[q] is not None:
                p_ref[2 * q + 1, rows, cols] = im[q]
        return re[0] if total is None else total + re[0]

    operand(0)
    for q in range(FREQS):
        cross_first(q)
        cross_second(q)
    tiles_a = tiles_of(ca_ref, sa_ref, pa_ref)
    tiles_b = tiles_of(cb_ref, sb_ref, pb_ref) + tiles_of(ct_ref, st_ref, pt_ref)
    top_a = total_a = top_b = total_b = None
    for where in tiles_b:
        top_b = to_scores(where, top_b)
    top_b = fold(top_b, jnp.maximum)
    for where in tiles_b:
        total_b = to_posterior(where, top_b, total_b)
    for where in tiles_a:
        top_a = to_scores(where, top_a)
    top_a = fold(top_a, jnp.maximum)
    for where in tiles_a:
        total_a = to_posterior(where, top_a, total_a)
    top = jnp.maximum(top_a, top_b)
    part_a, part_b = jnp.exp(top_a - top), jnp.exp(top_b - top)
    inverse = 1.0 / (part_a * fold(total_a, jnp.add) + part_b * fold(total_b, jnp.add))
    scale_a, scale_b = (part_a * inverse)[:1], (part_b * inverse)[:1]

    def scaled(q):
        for part in range(2):
            rows = slice(part * CLASSES, (part + 1) * CLASSES)
            if part == 1 and q in (0, ROT // 2):
                q_ref[q, rows, :] = jnp.zeros((CLASSES, COLS), BF)
                continue
            slot = 2 * q + part
            for col in range(0, GROUP, LANES):
                value = pa_ref[slot, :, col : col + LANES] * scale_a
                q_ref[q, rows, col : col + LANES] = value.astype(BF)
            q_ref[q, rows, GROUP:TAIL] = (pb_ref[slot] * scale_b).astype(BF)
            packed = jnp.where(packed_live, pt_ref[slot] * scale_b, 0.0)
            last = [packed] + [
                pltpu.roll(packed, LANES - kt * TAIL_ROWS, 1) for kt in range(1, tiles_k)
            ]
            last = jnp.where(lane < TAIL_ROWS, jnp.concatenate(last, axis=0), 0.0)
            q_ref[q, rows, TAIL:] = last.astype(BF)

    third = 2 * CLASSES // 3
    order = [4 * quad + slot for quad in range(QUADS) for slot in (3, 0, 1, 2)]
    order = [q for q in order if q < FREQS]
    extra = jnp.zeros((2 * CLASSES, LANES), F32)
    scaled(order[0])
    for n, q in enumerate(order):
        o = jnp.dot(q_ref[q, :, :ROWS], fh_ref[q], preferred_element_type=F32)
        if n + 1 < len(order):
            scaled(order[n + 1])
        real = o[:CLASSES, :LANES] + o[CLASSES:, LANES:]
        imag = o[:CLASSES, LANES:] - o[CLASSES:, :LANES]
        both = jnp.concatenate([real, imag], axis=0)
        quad, slot = q // 4, q % 4
        if slot == 3:
            extra = both
            continue
        if 4 * quad + 3 >= FREQS:
            extra = jnp.zeros((2 * CLASSES, LANES), F32)
        tile = [both, extra[slot * third : (slot + 1) * third]]
        num_ref[slot * QUADS + quad] = jnp.concatenate(tile, axis=0).T
    core, chip = me % 2, me // 2
    for half in range(2):
        side = (1 - core) if half == 0 else core
        for e in range(BLOCKS // 2):
            row = side * (LANES // 2) + (chip ^ (e // 2 + 4 * (e % 2))) * ROWS8
            row = pl.multiple_of(row, ROWS8)
            out_ref[half, e] = num_ref[:, pl.ds(row, 8), :].reshape(PAY, LANES).astype(BF)


def make_payload(direct, refs, feat_hi, feat_lo, mt):
    return pl.pallas_call(
        functools.partial(posterior_kernel, direct),
        out_shape=jax.ShapeDtypeStruct((2, BLOCKS // 2, PAY, LANES), BF),
        in_specs=[VM] * 11,
        out_specs=VM,
        scratch_shapes=[
            pltpu.VMEM((BLOCKS * KPAD, BLOCK_COLS), BF),
            pltpu.VMEM((FREQS * 16, BLOCKS * KPAD), F32),
            pltpu.VMEM((FREQS, 4 * CLASSES, 2 * LANES), BF),
            pltpu.VMEM((FREQS, 2 * CLASSES, 2 * LANES), F8),
            pltpu.VMEM((2 * FREQS, CLASSES, GROUP), F32),
            pltpu.VMEM((2 * FREQS, CLASSES, TAIL - GROUP), F32),
            pltpu.VMEM((2 * FREQS, 8, LANES), F32),
            pltpu.VMEM((ROT, CLASSES, GROUP), F32),
            pltpu.VMEM((ROT, CLASSES, TAIL - GROUP), F32),
            pltpu.VMEM((ROT, 8, LANES), F32),
            pltpu.VMEM((2 * FREQS, CLASSES, GROUP), F32),
            pltpu.VMEM((2 * FREQS, CLASSES, TAIL - GROUP), F32),
            pltpu.VMEM((2 * FREQS, 8, LANES), F32),
            pltpu.VMEM((FREQS, 2 * CLASSES, COLS), BF),
            pltpu.VMEM((TILES, LANES, LANES), F32),
        ],
        compiler_params=pltpu.CompilerParams(vmem_limit_bytes=28 * MIB),
        cost_estimate=cost(10.0),
        name="posterior",
    )(*refs, feat_hi, feat_lo, mt)


def final_kernel(keep_ref, got_ref, back_ref, out_ref):
    total = keep_ref[...] + got_ref[...].astype(F32)
    turned = total.T
    width = QUADS * ROWS8
    third = 2 * CLASSES // 3
    last = jnp.concatenate(
        [turned[2 * CLASSES :, slot * width : (slot + 1) * width] for slot in range(3)], axis=0
    )
    numer = jnp.zeros((CLASSES, BLOCK_COLS), F32)
    for part in range(2):
        rows = slice(part * CLASSES, (part + 1) * CLASSES)
        for value, first in ((turned[rows], 0), (last[rows], 3 * width)):
            span = slice(first, first + value.shape[1])
            hi = value.astype(BF)
            lo = (value - hi.astype(F32)).astype(BF)
            dot = functools.partial(jnp.dot, preferred_element_type=F32)
            table_hi, table_lo = back_ref[2 * part, span], back_ref[2 * part + 1, span]
            numer += dot(hi, table_hi) + dot(lo, table_hi) + dot(hi, table_lo)
    weights = turned[CLASSES : 2 * CLASSES]
    column = lax.broadcasted_iota(jnp.int32, (CLASSES, BLOCK_COLS), 1)
    first = weights[:, 0:1] + weights[:, 1:2]
    second = weights[:, STEP : STEP + 1] + weights[:, STEP + 1 : STEP + 2]
    out_ref[...] = numer / (jnp.where(column < ANG, first, second) + 1.0)


def finish(keep, got, back):
    return pl.pallas_call(
        final_kernel,
        out_shape=jax.ShapeDtypeStruct((CLASSES, BLOCK_COLS), F32),
        in_specs=[VM] * 3,
        out_specs=VM,
        compiler_params=pltpu.CompilerParams(vmem_limit_bytes=8 * MIB),
        cost_estimate=cost(1.0),
        name="finish",
    )(keep, got, back)


def swap(value, distance):
    pairs = [(i, i ^ distance) for i in range(lax.axis_size("img"))]
    return lax.ppermute(value, "img", pairs)


def reduce_direct(pay):
    pairs = pay[1].astype(F32) + swap(pay[0], 1).astype(F32)
    pairs = pairs.reshape((4, BLOCKS // 8) + pairs.shape[1:])
    parts = [swap(pairs[g].astype(BF), 2 * g) for g in (1, 2, 3)]
    total = pairs[0]
    for part in parts:
        total = total + part.astype(F32)
    return total[0], swap(total[1].astype(BF), 8)


def on_device(images, class_refs, sigma2, ctf_group, defocus_bin):
    devices = lax.axis_size("img")
    share = class_refs.shape[1]
    me = lax.axis_index("img")
    direct = devices == BLOCKS and share == BLOCK_COLS
    if direct:
        near = swap(class_refs, 8)
    else:
        whole = lax.all_gather(class_refs, "img", axis=1, tiled=True)
        blocks = whole.reshape(CLASSES, BLOCKS, BLOCK_COLS).transpose(1, 0, 2)
        refs = [jnp.stack([blocks[2 * g + s], blocks[2 * g + s + 8]]) for s in range(2) for g in range(4)]
    pay = None
    for first in range(0, images.shape[0], ROWS8):
        part = slice(first, first + ROWS8)
        hi, lo, pix, slot, table = first_features(
            images[part], sigma2, ctf_group[part], defocus_bin[part]
        )
        if direct and first == 0:
            near, hi = lax.optimization_barrier((near, hi))
            near = jnp.stack([class_refs, near])
            rest = [swap(near, 2 * g) for g in (1, 2, 3)]
        hi, lo, mt, back = second_features(hi, lo, table, pix, slot)
        if direct and first == 0:
            other = [swap(near, 1)]
            other[0], hi = lax.optimization_barrier((other[0], hi))
            for g in range(3):
                rest[g], hi = lax.optimization_barrier((rest[g], hi))
                other.append(swap(rest[g], 1))
            refs = [near] + rest + other
        one = make_payload(direct, refs, hi, lo, mt)
        pay = one if pay is None else pay + one
    if direct:
        return finish(*reduce_direct(pay), back)
    summed = lax.psum(pay.astype(F32), "img")
    start = me * share
    block = start // BLOCK_COLS
    chip = block // 2
    mine = summed[1 - block % 2, 2 * (chip % 4) + chip // 4]
    return lax.dynamic_slice_in_dim(
        finish(mine, jnp.zeros_like(mine, BF), back), start % BLOCK_COLS, share, 1
    )


def solution(mesh):
    in_specs = (
        P(("groups", "img"), None),
        P("groups", "img"),
        P("groups", None),
        P(("groups", "img")),
        P(("groups", "img")),
    )
    out_specs = P("groups", "img")
    return jax.shard_map(
        on_device, mesh=mesh, in_specs=in_specs, out_specs=out_specs, check_vma=False
    )
```

```python
import functools
import math

import jax
import jax.numpy as jnp
import numpy as np
from jax import lax
from jax.experimental import pallas as pl
from jax.experimental.pallas import tpu as pltpu
from jax.sharding import PartitionSpec as P

CLASSES = 48
ROT = 36
SHELLS = 16
ANG = 144
REACH = 3
SHIFTS = 49
BINS = 32
NGROUP = 16

STEP = ANG // ROT
CHANS = 2 * SHELLS
BLOCKS = CHANS // 2
BLOCK_COLS = 2 * ANG
LANES = CHANS * STEP
FREQS = ROT // 2 + 1
ROWS8 = 8
S_STEP = 4
S_PAD = -(-SHIFTS // S_STEP) * S_STEP
ROWS = S_PAD * ROWS8
LIVE = SHIFTS * ROWS8
COLS = 512
STEPS_A = 2
STEPS_B = 5
GROUP = 256
TAIL = 3 * LANES
TAIL_ROWS = 16
KPAD = 64
QUADS = (FREQS + 1) // 4
TILES = 3 * QUADS
PAY = TILES * ROWS8
BF = jnp.bfloat16
F8 = jnp.float8_e5m2
F32 = jnp.float32
MIB = 1024 * 1024


def block_order():
    return [m for m in range(0, BLOCKS, 2)] + [m for m in range(1, BLOCKS, 2)]


def lane_channel():
    chan, off = [], []
    for m in block_order():
        for cc in range(2):
            for d in range(STEP):
                chan.append(2 * m + cc)
                off.append(d)
    return np.array(chan), np.array(off)


def radius_of():
    return (np.arange(SHELLS, dtype=np.float64) + 1.0) / (2.0 * SHELLS)


def ctf_lanes():
    chan, _ = lane_channel()
    defocus = 1.0 + np.arange(BINS, dtype=np.float64) / BINS
    table = -np.sin(80.0 * defocus[:, None] * radius_of()[None, :] ** 2 + 0.1)
    return table[:, chan % SHELLS].astype(np.float32)


def shell_expand():
    chan, _ = lane_channel()
    return (np.arange(SHELLS)[:, None] == (chan % SHELLS)[None, :]).astype(np.float32)


def pixel_perm():
    table = np.zeros((BLOCK_COLS, BLOCK_COLS), np.float32)
    for b in range(ROT):
        for cc in range(2):
            for d in range(STEP):
                table[b * 8 + cc * STEP + d, cc * ANG + STEP * b + d] = 1.0
    return table


def phase_lanes():
    chan, off = lane_channel()
    shell = chan % SHELLS
    sign = np.where(chan < SHELLS, -1.0, 1.0)
    offsets = np.arange(2 * REACH + 1, dtype=np.float64) - REACH
    sx = np.repeat(offsets, 2 * REACH + 1)
    sy = np.tile(offsets, 2 * REACH + 1)
    angle = 2.0 * math.pi * (STEP * np.arange(ROT)[:, None] + off[None, :]) / ANG
    phase = (
        2.0
        * math.pi
        * radius_of()[shell][None, None, :]
        * (np.cos(angle)[None] * sx[:, None, None] + np.sin(angle)[None] * sy[:, None, None])
    )
    cos_t = np.zeros((S_PAD, ROT, LANES), np.float32)
    sin_t = np.zeros((S_PAD, ROT, LANES), np.float32)
    cos_t[:SHIFTS] = np.cos(phase)
    sin_t[:SHIFTS] = np.sin(phase) * sign[None, None, :]
    return np.concatenate([cos_t, sin_t], axis=1)


def refs_transform():
    table = np.zeros((FREQS, 2, 2, STEP, 2, ANG), np.float64)
    for q in range(FREQS):
        scale = (1.0 if q in (0, ROT // 2) else 2.0) / ROT
        for d in range(STEP):
            b = np.arange(ROT)
            turn = 2.0 * math.pi * ((q * b) % ROT) / ROT
            for cc in range(2):
                table[q, 0, cc, d, cc, STEP * b + d] = scale * np.cos(turn)
                if q not in (0, ROT // 2):
                    table[q, 1, cc, d, cc, STEP * b + d] = -scale * np.sin(turn)
    return table.reshape(FREQS * 16, BLOCK_COLS)


def inverse_transform():
    real = np.zeros((FREQS + 1, 2, STEP, 2, ANG), np.float64)
    imag = np.zeros((FREQS + 1, 2, STEP, 2, ANG), np.float64)
    b = np.arange(ROT)
    for q in range(FREQS):
        scale = (1.0 if q in (0, ROT // 2) else 2.0) / ROT
        turn = 2.0 * math.pi * ((q * b) % ROT) / ROT
        for cc in range(2):
            for d in range(STEP):
                real[q, cc, d, cc, STEP * b + d] = scale * np.cos(turn)
                if q not in (0, ROT // 2):
                    imag[q, cc, d, cc, STEP * b + d] = -scale * np.sin(turn)
    shape = (QUADS, 4, ROWS8, BLOCK_COLS)
    return [t.reshape(shape).transpose(1, 0, 2, 3).reshape(4 * QUADS * ROWS8, BLOCK_COLS) for t in (real, imag)]


def split(table):
    hi = table.astype(np.float32).astype(jnp.bfloat16)
    lo = (table - hi.astype(np.float64)).astype(np.float32).astype(jnp.bfloat16)
    return hi, lo


C1, C2 = math.cos(2 * math.pi / 9), math.cos(4 * math.pi / 9)
S1, S3, S4 = math.sin(2 * math.pi / 9), math.sin(6 * math.pi / 9), math.sin(8 * math.pi / 9)


def nine_cos(x0, s1, s2, s3, s4):
    u = s1 + s2 + s4
    v = x0 + s3
    base = x0 - 0.5 * s3
    a, b, c = s1 - s4, s2 - s4, s1 - s2
    p1 = C1 * a + C2 * b
    p2 = C2 * c - C1 * b
    return u + v, base + p1, base + p2, v - 0.5 * u, base - (p1 + p2)


def nine_sin(d1, d2, d3, d4):
    p, q, r = d1 + d2, d2 + d4, d1 - d4
    h = S3 * d3
    e1 = S1 * p + S4 * q
    e2 = S1 * r + S4 * p
    return e1 + h, e2 - h, S3 * (d1 - d2 + d4), (e2 - e1) + h


def nine_real(x):
    r = nine_cos(x[0], x[1] + x[8], x[2] + x[7], x[3] + x[6], x[4] + x[5])
    i = nine_sin(x[1] - x[8], x[2] - x[7], x[3] - x[6], x[4] - x[5])
    return r, (None,) + i


def crt(k1, k2):
    for k in range(ROT):
        if k % 4 == k1 and k % 9 == k2:
            return k
    return None


def forward36(x):
    re, im = [None] * FREQS, [None] * FREQS
    y0, y2, ya, yb = [], [], [], []
    for n2 in range(9):
        v = [x[(9 * n1 + 4 * n2) % ROT] for n1 in range(4)]
        t0, t1 = v[0] + v[2], v[1] + v[3]
        y0.append(t0 + t1)
        y2.append(t0 - t1)
        ya.append(v[0] - v[2])
        yb.append(v[3] - v[1])

    def put(k, real, imag):
        if k <= ROT // 2:
            re[k], im[k] = real, imag
        else:
            re[ROT - k], im[ROT - k] = real, -imag

    for k1, y in ((0, y0), (2, y2)):
        r, i = nine_real(y)
        k = crt(k1, 0)
        re[k] = r[0]
        for k2 in range(1, 5):
            k = crt(k1, k2)
            if k <= ROT // 2:
                re[k], im[k] = r[k2], -i[k2]
            else:
                re[ROT - k], im[ROT - k] = r[k2], i[k2]
    ra, ia = nine_real(ya)
    rb, ib = nine_real(yb)
    put(crt(1, 0), ra[0], rb[0])
    for k2 in range(1, 5):
        put(crt(1, k2), ra[k2] + ib[k2], rb[k2] - ia[k2])
        put(crt(1, 9 - k2), ra[k2] - ib[k2], rb[k2] + ia[k2])
    return re, im


def inverse36(re, im):
    def entry(k):
        if k <= ROT // 2:
            return re[k], im[k], 1
        return re[ROT - k], im[ROT - k], -1

    ys = []
    for k1 in (0, 2):
        real, imag = [entry(crt(k1, 0))[0]], [None]
        for k2 in range(1, 5):
            a, b, sign = entry(crt(k1, k2))
            real.append(a)
            imag.append(b if sign > 0 else -b)
        r = nine_cos(*real)
        i = (None,) + nine_sin(*imag[1:])
        y = [None] * 9
        y[0] = r[0]
        for n in range(1, 5):
            y[n], y[9 - n] = r[n] - i[n], r[n] + i[n]
        ys.append(y)
    xr, xi = [], []
    for k2 in range(9):
        a, b, sign = entry(crt(1, k2))
        xr.append(a)
        xi.append(b if sign > 0 else -b)
    rr, ir = nine_real(xr)
    ri, ii = nine_real(xi)
    ya, yb = [None] * 9, [None] * 9
    ya[0], yb[0] = rr[0], ri[0]
    for n in range(1, 5):
        ya[n], ya[9 - n] = rr[n] - ii[n], rr[n] + ii[n]
        yb[n], yb[9 - n] = ri[n] + ir[n], ri[n] - ir[n]
    x = [None] * ROT
    for n2 in range(9):
        t0, t1 = ys[0][n2] + ys[1][n2], ys[0][n2] - ys[1][n2]
        for n1, value in enumerate((t0 + ya[n2], t1 - yb[n2], t0 - ya[n2], t1 + yb[n2])):
            x[(9 * n1 + 4 * n2) % ROT] = value
    return x


def transform_steps(table_ref, pix_ref, slot_ref, fh_ref, fl_ref, first, count):
    slot = jnp.concatenate([slot_ref[...]] * 2, axis=0)
    nothing = jnp.zeros_like(slot)

    def step(i, _):
        parts = []
        for pair in range(S_STEP // 2):
            x = []
            for b in range(ROT):
                halves = []
                for h in range(2):
                    at = S_STEP * i + 2 * pair + h
                    c = table_ref[at, b : b + 1, :]
                    s = table_ref[at, ROT + b : ROT + b + 1, :]
                    halves.append(pix_ref[0, b] * c + pix_ref[1, b] * s)
                x.append(jnp.concatenate(halves, axis=0).astype(BF).astype(F32))
            re, im = forward36(x)
            im[0], im[ROT // 2] = slot, nothing
            row = pl.multiple_of((first + i) * S_STEP * ROWS8 + 16 * pair, 16)
            low = []
            for q in range(FREQS):
                for part, value in ((0, re[q]), (1, im[q])):
                    hi = value.astype(BF)
                    fh_ref[q, pl.ds(row, 16), part * LANES : (part + 1) * LANES] = hi
                    low.append(value - hi.astype(F32))
            parts.append(low)
        rows = pl.ds(pl.multiple_of((first + i) * S_STEP * ROWS8, S_STEP * ROWS8), S_STEP * ROWS8)
        for n, low in enumerate(zip(*parts)):
            cols = slice((n % 2) * LANES, (n % 2 + 1) * LANES)
            fl_ref[n // 2, rows, cols] = jnp.concatenate(low, axis=0).astype(F8)
        return 0

    lax.fori_loop(0, count, step, 0)


def first_kernel(
    grp_hbm, bin_hbm, img_hbm, sig_hbm, ctf_hbm, exp_hbm, perm_hbm, table_hbm,
    fh_ref, fl_ref, pix_ref, slot_ref, rest_ref,
    grp_ref, bin_ref, img_ref, sig_ref, ctf_ref, exp_ref, perm_ref, table_ref, noise_ref, sems,
):
    moves = [
        (grp_hbm, grp_ref), (bin_hbm, bin_ref), (img_hbm, img_ref), (sig_hbm, sig_ref),
        (ctf_hbm, ctf_ref), (exp_hbm, exp_ref), (perm_hbm, perm_ref),
        (table_hbm.at[pl.ds(0, S_STEP * STEPS_A)], table_ref),
        (table_hbm.at[pl.ds(S_STEP * STEPS_A, S_STEP * STEPS_B)], rest_ref),
    ]
    copies = [pltpu.make_async_copy(a, b, sems.at[i]) for i, (a, b) in enumerate(moves)]
    for copy in copies[:8]:
        copy.start()
    for copy in copies[:7]:
        copy.wait()
    copies[8].start()
    noise_ref[...] = jnp.dot(
        sig_ref[...], exp_ref[...], precision=lax.Precision.HIGHEST, preferred_element_type=F32
    )
    ctf = jnp.concatenate([ctf_ref[pl.ds(bin_ref[i], 1), :] for i in range(ROWS8)], axis=0)
    noise = jnp.concatenate([noise_ref[pl.ds(grp_ref[i], 1), :] for i in range(ROWS8)], axis=0)
    filt = ctf / noise
    weight = ctf * ctf / noise

    img = img_ref[...].astype(F32)
    stack = jnp.concatenate(
        [img[:, BLOCK_COLS * m : BLOCK_COLS * (m + 1)] for m in block_order()], axis=0
    ).astype(BF)
    turned = lax.dot_general(
        perm_ref[...], stack, (((1,), (1,)), ((), ())), preferred_element_type=F32
    )
    sub = lax.broadcasted_iota(jnp.int32, (ROWS8, LANES), 0)
    lane = lax.broadcasted_iota(jnp.int32, (ROWS8, LANES), 1)
    for b in range(ROT):
        y = turned[b * 8 : (b + 1) * 8]
        for t in (1, 2, 4):
            up = pltpu.roll(pltpu.roll(y, t, 0), LANES - t, 1)
            down = pltpu.roll(pltpu.roll(y, 8 - t, 0), t, 1)
            row_bit, lane_bit = (sub & t) != 0, (lane & t) != 0
            y = jnp.where(row_bit == lane_bit, y, jnp.where(row_bit, up, down))
        y = y * filt
        pix_ref[0, b] = y
        pix_ref[1, b] = jnp.where(
            (lane & 32) == 0, pltpu.roll(y, LANES - 32, 1), pltpu.roll(y, 32, 1)
        )

    off = lane & (STEP - 1)
    weight_hi = weight.astype(BF).astype(F32)
    slot_ref[...] = jnp.where(off == 0, weight_hi, jnp.where(off == 1, weight - weight_hi, 0.0))
    copies[7].wait()
    transform_steps(table_ref, pix_ref, slot_ref, fh_ref, fl_ref, 0, STEPS_A)
    copies[8].wait()


def second_kernel(
    fh_in, fl_in, table_ref, pix_ref, slot_ref, table_hbm, mt_hbm, back_hbm,
    fh_ref, fl_ref, mt_ref, back_ref, late_ref, sems,
):
    del fh_in, fl_in
    early = STEPS_A + STEPS_B
    late = table_hbm.at[pl.ds(S_STEP * early, S_PAD - S_STEP * early)]
    moves = [(late, late_ref), (mt_hbm, mt_ref), (back_hbm, back_ref)]
    copies = [pltpu.make_async_copy(a, b, sems.at[i]) for i, (a, b) in enumerate(moves)]
    for copy in copies:
        copy.start()
    transform_steps(table_ref, pix_ref, slot_ref, fh_ref, fl_ref, STEPS_A, STEPS_B)
    copies[0].wait()
    transform_steps(
        late_ref, pix_ref, slot_ref, fh_ref, fl_ref, early, S_PAD // S_STEP - early
    )
    for copy in copies[1:]:
        copy.wait()


VM = pl.BlockSpec(memory_space=pltpu.VMEM)
HB = pl.BlockSpec(memory_space=pltpu.HBM)


def in_hbm(*arrays):
    return [pltpu.with_memory_space_constraint(a, pltpu.HBM) for a in arrays]


def cost(micros):
    return pl.CostEstimate(flops=int(micros * 1e9), bytes_accessed=int(micros * 3e6), transcendentals=0)


def first_features(images, sigma2, ctf_group, defocus_bin):
    feat = (FREQS, ROWS, 2 * LANES)
    return pl.pallas_call(
        first_kernel,
        out_shape=(
            jax.ShapeDtypeStruct(feat, BF),
            jax.ShapeDtypeStruct(feat, F8),
            jax.ShapeDtypeStruct((2, ROT, ROWS8, LANES), F32),
            jax.ShapeDtypeStruct((ROWS8, LANES), F32),
            jax.ShapeDtypeStruct((S_STEP * STEPS_B, 2 * ROT, LANES), F32),
        ),
        in_specs=[HB] * 8,
        out_specs=[VM] * 5,
        scratch_shapes=[
            pltpu.SMEM((ROWS8,), jnp.int32),
            pltpu.SMEM((ROWS8,), jnp.int32),
            pltpu.VMEM(images.shape, BF),
            pltpu.VMEM(sigma2.shape, F32),
            pltpu.VMEM((BINS, LANES), F32),
            pltpu.VMEM((NGROUP, LANES), F32),
            pltpu.VMEM((BLOCK_COLS, BLOCK_COLS), BF),
            pltpu.VMEM((S_STEP * STEPS_A, 2 * ROT, LANES), F32),
            pltpu.VMEM((NGROUP, LANES), F32),
            pltpu.SemaphoreType.DMA((9,)),
        ],
        compiler_params=pltpu.CompilerParams(vmem_limit_bytes=20 * MIB),
        cost_estimate=cost(4.5),
        name="features_first",
    )(*in_hbm(
        ctf_group, defocus_bin, images, sigma2, jnp.asarray(ctf_lanes()),
        jnp.asarray(shell_expand()), jnp.asarray(pixel_perm(), BF), jnp.asarray(phase_lanes()),
    ))


def second_features(hi, lo, table, pix, slot):
    mt = np.stack(split(refs_transform()))
    back = np.stack([half for part in inverse_transform() for half in split(part)])
    return pl.pallas_call(
        second_kernel,
        out_shape=(
            jax.ShapeDtypeStruct(hi.shape, BF),
            jax.ShapeDtypeStruct(lo.shape, F8),
            jax.ShapeDtypeStruct(mt.shape, BF),
            jax.ShapeDtypeStruct(back.shape, BF),
        ),
        in_specs=[VM] * 5 + [HB] * 3,
        out_specs=[VM] * 4,
        scratch_shapes=[
            pltpu.VMEM((S_PAD - S_STEP * (STEPS_A + STEPS_B), 2 * ROT, LANES), F32),
            pltpu.SemaphoreType.DMA((3,)),
        ],
        input_output_aliases={0: 0, 1: 1},
        compiler_params=pltpu.CompilerParams(vmem_limit_bytes=16 * MIB),
        cost_estimate=cost(2.5),
        name="features_second",
    )(
        hi, lo, table, pix, slot,
        *in_hbm(jnp.asarray(phase_lanes()), jnp.asarray(mt), jnp.asarray(back)),
    )


def nt(left, right):
    return lax.dot_general(left, right, (((1,), (1,)), ((), ())), preferred_element_type=F32)


def posterior_kernel(
    direct, r0_ref, r1_ref, r2_ref, r3_ref, s0_ref, s1_ref, s2_ref, s3_ref, fh_ref, fl_ref, mt_ref,
    out_ref, x_ref, d_ref, a_ref, e_ref, ca_ref, cb_ref, ct_ref, sa_ref, sb_ref, st_ref,
    pa_ref, pb_ref, pt_ref, q_ref, num_ref,
):
    lane = lax.broadcasted_iota(jnp.int32, (CLASSES, LANES), 1)
    lane8 = lax.broadcasted_iota(jnp.int32, (8, LANES), 1)
    row8 = lax.broadcasted_iota(jnp.int32, (8, LANES), 0)

    me = lax.axis_index("img") if direct else 0
    blank = jnp.zeros((KPAD - CLASSES, BLOCK_COLS), BF)
    for side, refs in enumerate(((r0_ref, r1_ref, r2_ref, r3_ref), (s0_ref, s1_ref, s2_ref, s3_ref))):
        for g, pair in enumerate(refs):
            for h in range(2):
                row = pl.multiple_of((me ^ (2 * g + 8 * h + side)) * KPAD, KPAD)
                x_ref[pl.ds(row, KPAD), :] = jnp.concatenate([pair[h], blank], axis=0)
    x = x_ref[...]
    d_ref[...] = nt(mt_ref[0], x) + nt(mt_ref[1], x)

    for t in range(BLOCKS // 2):
        cols = slice(t * LANES, (t + 1) * LANES)
        edge = jnp.zeros((8, LANES), F32)
        inner = jnp.zeros((8, LANES), F32)
        for q in range(FREQS):
            re = d_ref[q * 16 : q * 16 + 8, cols]
            if q in (0, ROT // 2):
                edge += re * re
            else:
                im = d_ref[q * 16 + 8 : q * 16 + 16, cols]
                inner += re * re + im * im
        power = -0.5 * (ROT * edge + (ROT // 2) * inner)
        power += pltpu.roll(power, 7, 0)
        power += pltpu.roll(power, 6, 0)
        power = jnp.where((row8 & (STEP - 1)) == 0, power, 0.0)
        d_ref[8:16, cols] = power + pltpu.roll(power, 1, 0)

    def operand(q):
        tile = jnp.concatenate(
            [
                d_ref[q * 16 + part * 8 : q * 16 + part * 8 + 8, t * LANES : (t + 1) * LANES]
                for part in range(2)
                for t in range(BLOCKS // 2)
            ],
            axis=0,
        )
        tile = tile.T
        even, odd = tile[:CLASSES], tile[KPAD : KPAD + CLASSES]
        real = jnp.where(lane < 64, even, pltpu.roll(odd, 64, 1))
        imag = jnp.where(lane < 64, pltpu.roll(even, 64, 1), odd)
        real_hi, imag_hi = real.astype(BF), imag.astype(BF)
        real_lo = (real - real_hi.astype(F32)).astype(BF)
        imag_lo = (imag - imag_hi.astype(F32)).astype(BF)
        for first, re, im in ((0, real_hi, imag_hi), (2 * CLASSES, real_lo, imag_lo)):
            a_ref[q, first : first + CLASSES, :LANES] = re
            a_ref[q, first : first + CLASSES, LANES:] = im
            a_ref[q, first + CLASSES : first + 2 * CLASSES, :LANES] = -im
            a_ref[q, first + CLASSES : first + 2 * CLASSES, LANES:] = re
        left = [jnp.concatenate([real, imag], axis=1), jnp.concatenate([-imag, real], axis=1)]
        e_ref[q] = jnp.concatenate(left, axis=0).astype(F8)

    tiles_k = CLASSES // 8

    def cross(q, rows):
        both = a_ref[q]
        first = nt(both, fh_ref[q, rows])
        return first[: 2 * CLASSES] + first[2 * CLASSES :] + nt(e_ref[q], fl_ref[q, rows])

    def cross_first(q):
        total = cross(q, slice(0, GROUP))
        if q + 1 < FREQS:
            operand(q + 1)
        ca_ref[2 * q] = total[:CLASSES]
        ca_ref[2 * q + 1] = total[CLASSES:]

    def cross_second(q):
        total = cross(q, slice(GROUP, ROWS))
        cb_ref[2 * q] = total[:CLASSES, : TAIL - GROUP]
        cb_ref[2 * q + 1] = total[CLASSES:, : TAIL - GROUP]
        last = total[:, TAIL - GROUP : TAIL - GROUP + TAIL_ROWS]
        last = jnp.concatenate([last, jnp.zeros((2 * CLASSES, LANES - TAIL_ROWS), F32)], axis=1)
        for part in range(2):
            packed = last[part * CLASSES : part * CLASSES + 8]
            for kt in range(1, tiles_k):
                row = part * CLASSES + kt * 8
                packed += pltpu.roll(last[row : row + 8], kt * TAIL_ROWS, 1)
            ct_ref[2 * q + part] = packed

    def tiles_of(c_ref, s_ref, p_ref):
        return [
            (c_ref, s_ref, p_ref, slice(row, row + 8), slice(col, col + LANES))
            for col in range(0, c_ref.shape[2], LANES)
            for row in range(0, c_ref.shape[1], 8)
        ]

    packed_live = ((lane8 & (TAIL_ROWS - 1)) < LIVE - TAIL) & (lane8 < tiles_k * TAIL_ROWS)

    def to_scores(where, top):
        c_ref, s_ref, _, rows, cols = where
        re = [c_ref[2 * q, rows, cols] for q in range(FREQS)]
        im = [None] + [c_ref[2 * q + 1, rows, cols] for q in range(1, FREQS - 1)] + [None]
        if c_ref is ct_ref:
            re[0] = jnp.where(packed_live, re[0], -1e30)
        x = inverse36(re, im)
        for r in range(ROT):
            s_ref[r, rows, cols] = x[r]
        while len(x) > 1:
            x = [jnp.maximum(*x[i : i + 2]) if i + 1 < len(x) else x[i] for i in range(0, len(x), 2)]
        return x[0] if top is None else jnp.maximum(top, x[0])

    def fold(v, op):
        for t in (4, 2, 1):
            v = op(v, pltpu.roll(v, t, 0))
        for t in (64, 32, 16, 8):
            v = op(v, pltpu.roll(v, t, 1))
        return v

    def to_posterior(where, top, total):
        _, s_ref, p_ref, rows, cols = where
        x = [jnp.exp(s_ref[r, rows, cols] - top) for r in range(ROT)]
        re, im = forward36(x)
        for q in range(FREQS):
            p_ref[2 * q, rows, cols] = re[q]
            if im[q] is not None:
                p_ref[2 * q + 1, rows, cols] = im[q]
        return re[0] if total is None else total + re[0]

    operand(0)
    for q in range(FREQS):
        cross_first(q)
        cross_second(q)
    tiles_a = tiles_of(ca_ref, sa_ref, pa_ref)
    tiles_b = tiles_of(cb_ref, sb_ref, pb_ref) + tiles_of(ct_ref, st_ref, pt_ref)
    top_a = total_a = top_b = total_b = None
    for where in tiles_b:
        top_b = to_scores(where, top_b)
    top_b = fold(top_b, jnp.maximum)
    for where in tiles_b:
        total_b = to_posterior(where, top_b, total_b)
    for where in tiles_a:
        top_a = to_scores(where, top_a)
    top_a = fold(top_a, jnp.maximum)
    for where in tiles_a:
        total_a = to_posterior(where, top_a, total_a)
    top = jnp.maximum(top_a, top_b)
    part_a, part_b = jnp.exp(top_a - top), jnp.exp(top_b - top)
    inverse = 1.0 / (part_a * fold(total_a, jnp.add) + part_b * fold(total_b, jnp.add))
    scale_a, scale_b = (part_a * inverse)[:1], (part_b * inverse)[:1]

    def scaled(q):
        for part in range(2):
            rows = slice(part * CLASSES, (part + 1) * CLASSES)
            if part == 1 and q in (0, ROT // 2):
                q_ref[q, rows, :] = jnp.zeros((CLASSES, COLS), BF)
                continue
            slot = 2 * q + part
            for col in range(0, GROUP, LANES):
                value = pa_ref[slot, :, col : col + LANES] * scale_a
                q_ref[q, rows, col : col + LANES] = value.astype(BF)
            q_ref[q, rows, GROUP:TAIL] = (pb_ref[slot] * scale_b).astype(BF)
            packed = jnp.where(packed_live, pt_ref[slot] * scale_b, 0.0)
            last = [packed] + [
                pltpu.roll(packed, LANES - kt * TAIL_ROWS, 1) for kt in range(1, tiles_k)
            ]
            last = jnp.where(lane < TAIL_ROWS, jnp.concatenate(last, axis=0), 0.0)
            q_ref[q, rows, TAIL:] = last.astype(BF)

    third = 2 * CLASSES // 3
    order = [4 * quad + slot for quad in range(QUADS) for slot in (3, 0, 1, 2)]
    order = [q for q in order if q < FREQS]
    extra = jnp.zeros((2 * CLASSES, LANES), F32)
    scaled(order[0])
    for n, q in enumerate(order):
        o = jnp.dot(q_ref[q, :, :ROWS], fh_ref[q], preferred_element_type=F32)
        if n + 1 < len(order):
            scaled(order[n + 1])
        real = o[:CLASSES, :LANES] + o[CLASSES:, LANES:]
        imag = o[:CLASSES, LANES:] - o[CLASSES:, :LANES]
        both = jnp.concatenate([real, imag], axis=0)
        quad, slot = q // 4, q % 4
        if slot == 3:
            extra = both
            continue
        if 4 * quad + 3 >= FREQS:
            extra = jnp.zeros((2 * CLASSES, LANES), F32)
        tile = [both, extra[slot * third : (slot + 1) * third]]
        num_ref[slot * QUADS + quad] = jnp.concatenate(tile, axis=0).T
    core, chip = me % 2, me // 2
    for half in range(2):
        side = (1 - core) if half == 0 else core
        for e in range(BLOCKS // 2):
            row = side * (LANES // 2) + (chip ^ (e // 2 + 4 * (e % 2))) * ROWS8
            row = pl.multiple_of(row, ROWS8)
            out_ref[half, e] = num_ref[:, pl.ds(row, 8), :].reshape(PAY, LANES).astype(BF)


def make_payload(direct, refs, feat_hi, feat_lo, mt):
    return pl.pallas_call(
        functools.partial(posterior_kernel, direct),
        out_shape=jax.ShapeDtypeStruct((2, BLOCKS // 2, PAY, LANES), BF),
        in_specs=[VM] * 11,
        out_specs=VM,
        scratch_shapes=[
            pltpu.VMEM((BLOCKS * KPAD, BLOCK_COLS), BF),
            pltpu.VMEM((FREQS * 16, BLOCKS * KPAD), F32),
            pltpu.VMEM((FREQS, 4 * CLASSES, 2 * LANES), BF),
            pltpu.VMEM((FREQS, 2 * CLASSES, 2 * LANES), F8),
            pltpu.VMEM((2 * FREQS, CLASSES, GROUP), F32),
            pltpu.VMEM((2 * FREQS, CLASSES, TAIL - GROUP), F32),
            pltpu.VMEM((2 * FREQS, 8, LANES), F32),
            pltpu.VMEM((ROT, CLASSES, GROUP), F32),
            pltpu.VMEM((ROT, CLASSES, TAIL - GROUP), F32),
            pltpu.VMEM((ROT, 8, LANES), F32),
            pltpu.VMEM((2 * FREQS, CLASSES, GROUP), F32),
            pltpu.VMEM((2 * FREQS, CLASSES, TAIL - GROUP), F32),
            pltpu.VMEM((2 * FREQS, 8, LANES), F32),
            pltpu.VMEM((FREQS, 2 * CLASSES, COLS), BF),
            pltpu.VMEM((TILES, LANES, LANES), F32),
        ],
        compiler_params=pltpu.CompilerParams(vmem_limit_bytes=28 * MIB),
        cost_estimate=cost(10.0),
        name="posterior",
    )(*refs, feat_hi, feat_lo, mt)


def final_kernel(keep_ref, got_ref, back_ref, out_ref):
    total = keep_ref[...] + got_ref[...].astype(F32)
    turned = total.T
    width = QUADS * ROWS8
    third = 2 * CLASSES // 3
    last = jnp.concatenate(
        [turned[2 * CLASSES :, slot * width : (slot + 1) * width] for slot in range(3)], axis=0
    )
    numer = jnp.zeros((CLASSES, BLOCK_COLS), F32)
    for part in range(2):
        rows = slice(part * CLASSES, (part + 1) * CLASSES)
        for value, first in ((turned[rows], 0), (last[rows], 3 * width)):
            span = slice(first, first + value.shape[1])
            hi = value.astype(BF)
            lo = (value - hi.astype(F32)).astype(BF)
            dot = functools.partial(jnp.dot, preferred_element_type=F32)
            table_hi, table_lo = back_ref[2 * part, span], back_ref[2 * part + 1, span]
            numer += dot(hi, table_hi) + dot(lo, table_hi) + dot(hi, table_lo)
    weights = turned[CLASSES : 2 * CLASSES]
    column = lax.broadcasted_iota(jnp.int32, (CLASSES, BLOCK_COLS), 1)
    first = weights[:, 0:1] + weights[:, 1:2]
    second = weights[:, STEP : STEP + 1] + weights[:, STEP + 1 : STEP + 2]
    out_ref[...] = numer / (jnp.where(column < ANG, first, second) + 1.0)


def finish(keep, got, back):
    return pl.pallas_call(
        final_kernel,
        out_shape=jax.ShapeDtypeStruct((CLASSES, BLOCK_COLS), F32),
        in_specs=[VM] * 3,
        out_specs=VM,
        compiler_params=pltpu.CompilerParams(vmem_limit_bytes=8 * MIB),
        cost_estimate=cost(1.0),
        name="finish",
    )(keep, got, back)


def swap(value, distance):
    pairs = [(i, i ^ distance) for i in range(lax.axis_size("img"))]
    return lax.ppermute(value, "img", pairs)


def reduce_direct(pay):
    pairs = pay[1].astype(F32) + swap(pay[0], 1).astype(F32)
    pairs = pairs.reshape((4, BLOCKS // 8) + pairs.shape[1:])
    parts = [swap(pairs[g].astype(BF), 2 * g) for g in (1, 2, 3)]
    total = pairs[0]
    for part in parts:
        total = total + part.astype(F32)
    return total[0], swap(total[1].astype(BF), 8)


def on_device(images, class_refs, sigma2, ctf_group, defocus_bin):
    devices = lax.axis_size("img")
    share = class_refs.shape[1]
    me = lax.axis_index("img")
    direct = devices == BLOCKS and share == BLOCK_COLS
    if direct:
        near = swap(class_refs, 8)
    else:
        whole = lax.all_gather(class_refs, "img", axis=1, tiled=True)
        blocks = whole.reshape(CLASSES, BLOCKS, BLOCK_COLS).transpose(1, 0, 2)
        refs = [jnp.stack([blocks[2 * g + s], blocks[2 * g + s + 8]]) for s in range(2) for g in range(4)]
    pay = None
    for first in range(0, images.shape[0], ROWS8):
        part = slice(first, first + ROWS8)
        hi, lo, pix, slot, table = first_features(
            images[part], sigma2, ctf_group[part], defocus_bin[part]
        )
        if direct and first == 0:
            near, hi = lax.optimization_barrier((near, hi))
            near = jnp.stack([class_refs, near])
            rest = [swap(near, 2 * g) for g in (1, 2, 3)]
        hi, lo, mt, back = second_features(hi, lo, table, pix, slot)
        if direct and first == 0:
            other = [swap(near, 1)]
            other[0], hi = lax.optimization_barrier((other[0], hi))
            for g in range(3):
                rest[g], hi = lax.optimization_barrier((rest[g], hi))
                other.append(swap(rest[g], 1))
            refs = [near] + rest + other
        one = make_payload(direct, refs, hi, lo, mt)
        pay = one if pay is None else pay + one
    if direct:
        return finish(*reduce_direct(pay), back)
    summed = lax.psum(pay.astype(F32), "img")
    start = me * share
    block = start // BLOCK_COLS
    chip = block // 2
    mine = summed[1 - block % 2, 2 * (chip % 4) + chip // 4]
    return lax.dynamic_slice_in_dim(
        finish(mine, jnp.zeros_like(mine, BF), back), start % BLOCK_COLS, share, 1
    )


def solution(mesh):
    in_specs = (
        P(("groups", "img"), None),
        P("groups", "img"),
        P("groups", None),
        P(("groups", "img")),
        P(("groups", "img")),
    )
    out_specs = P("groups", "img")
    return jax.shard_map(
        on_device, mesh=mesh, in_specs=in_specs, out_specs=out_specs, check_vma=False
    )
```

```python
import functools
import math

import jax
import jax.numpy as jnp
import numpy as np
from jax import lax
from jax.experimental import pallas as pl
from jax.experimental.pallas import tpu as pltpu
from jax.sharding import PartitionSpec as P

CLASSES = 48
ROT = 36
SHELLS = 16
ANG = 144
REACH = 3
SHIFTS = 49
BINS = 32
NGROUP = 16

STEP = ANG // ROT
CHANS = 2 * SHELLS
BLOCKS = CHANS // 2
BLOCK_COLS = 2 * ANG
LANES = CHANS * STEP
FREQS = ROT // 2 + 1
ROWS8 = 8
S_STEP = 4
S_PAD = -(-SHIFTS // S_STEP) * S_STEP
ROWS = S_PAD * ROWS8
LIVE = SHIFTS * ROWS8
COLS = 512
STEPS_A = 2
STEPS_B = 5
GROUP = 256
TAIL = 3 * LANES
TAIL_ROWS = 16
KPAD = 64
QUADS = (FREQS + 1) // 4
TILES = 3 * QUADS
PAY = TILES * ROWS8
BF = jnp.bfloat16
F8 = jnp.float8_e5m2
F32 = jnp.float32
MIB = 1024 * 1024


def block_order():
    return [m for m in range(0, BLOCKS, 2)] + [m for m in range(1, BLOCKS, 2)]


def lane_channel():
    chan, off = [], []
    for m in block_order():
        for cc in range(2):
            for d in range(STEP):
                chan.append(2 * m + cc)
                off.append(d)
    return np.array(chan), np.array(off)


def radius_of():
    return (np.arange(SHELLS, dtype=np.float64) + 1.0) / (2.0 * SHELLS)


def ctf_lanes():
    chan, _ = lane_channel()
    defocus = 1.0 + np.arange(BINS, dtype=np.float64) / BINS
    table = -np.sin(80.0 * defocus[:, None] * radius_of()[None, :] ** 2 + 0.1)
    return table[:, chan % SHELLS].astype(np.float32)


def shell_expand():
    chan, _ = lane_channel()
    return (np.arange(SHELLS)[:, None] == (chan % SHELLS)[None, :]).astype(np.float32)


def pixel_perm():
    table = np.zeros((BLOCK_COLS, BLOCK_COLS), np.float32)
    for b in range(ROT):
        for cc in range(2):
            for d in range(STEP):
                table[b * 8 + cc * STEP + d, cc * ANG + STEP * b + d] = 1.0
    return table


def phase_lanes():
    chan, off = lane_channel()
    shell = chan % SHELLS
    sign = np.where(chan < SHELLS, -1.0, 1.0)
    offsets = np.arange(2 * REACH + 1, dtype=np.float64) - REACH
    sx = np.repeat(offsets, 2 * REACH + 1)
    sy = np.tile(offsets, 2 * REACH + 1)
    angle = 2.0 * math.pi * (STEP * np.arange(ROT)[:, None] + off[None, :]) / ANG
    phase = (
        2.0
        * math.pi
        * radius_of()[shell][None, None, :]
        * (np.cos(angle)[None] * sx[:, None, None] + np.sin(angle)[None] * sy[:, None, None])
    )
    cos_t = np.zeros((S_PAD, ROT, LANES), np.float32)
    sin_t = np.zeros((S_PAD, ROT, LANES), np.float32)
    cos_t[:SHIFTS] = np.cos(phase)
    sin_t[:SHIFTS] = np.sin(phase) * sign[None, None, :]
    return np.concatenate([cos_t, sin_t], axis=1)


def refs_transform():
    table = np.zeros((FREQS, 2, 2, STEP, 2, ANG), np.float64)
    for q in range(FREQS):
        scale = (1.0 if q in (0, ROT // 2) else 2.0) / ROT
        for d in range(STEP):
            b = np.arange(ROT)
            turn = 2.0 * math.pi * ((q * b) % ROT) / ROT
            for cc in range(2):
                table[q, 0, cc, d, cc, STEP * b + d] = scale * np.cos(turn)
                if q not in (0, ROT // 2):
                    table[q, 1, cc, d, cc, STEP * b + d] = -scale * np.sin(turn)
    return table.reshape(FREQS * 16, BLOCK_COLS)


def inverse_transform():
    real = np.zeros((FREQS + 1, 2, STEP, 2, ANG), np.float64)
    imag = np.zeros((FREQS + 1, 2, STEP, 2, ANG), np.float64)
    b = np.arange(ROT)
    for q in range(FREQS):
        scale = (1.0 if q in (0, ROT // 2) else 2.0) / ROT
        turn = 2.0 * math.pi * ((q * b) % ROT) / ROT
        for cc in range(2):
            for d in range(STEP):
                real[q, cc, d, cc, STEP * b + d] = scale * np.cos(turn)
                if q not in (0, ROT // 2):
                    imag[q, cc, d, cc, STEP * b + d] = -scale * np.sin(turn)
    rows = []
    for slots in (slice(0, 3), slice(3, 4)):
        for t in (real, imag):
            part = t.reshape(QUADS, 4, ROWS8, BLOCK_COLS)[:, slots].transpose(1, 0, 2, 3).reshape(-1, BLOCK_COLS)
            rows.append(np.pad(part, ((0, LANES - len(part)), (0, 0))))
    return np.concatenate(rows)


def split(table):
    hi = table.astype(np.float32).astype(jnp.bfloat16)
    lo = (table - hi.astype(np.float64)).astype(np.float32).astype(jnp.bfloat16)
    return hi, lo


C1, C2 = math.cos(2 * math.pi / 9), math.cos(4 * math.pi / 9)
S1, S3, S4 = math.sin(2 * math.pi / 9), math.sin(6 * math.pi / 9), math.sin(8 * math.pi / 9)


def nine_cos(x0, s1, s2, s3, s4):
    u = s1 + s2 + s4
    v = x0 + s3
    base = x0 - 0.5 * s3
    a, b, c = s1 - s4, s2 - s4, s1 - s2
    p1 = C1 * a + C2 * b
    p2 = C2 * c - C1 * b
    return u + v, base + p1, base + p2, v - 0.5 * u, base - (p1 + p2)


def nine_sin(d1, d2, d3, d4):
    p, q, r = d1 + d2, d2 + d4, d1 - d4
    h = S3 * d3
    e1 = S1 * p + S4 * q
    e2 = S1 * r + S4 * p
    return e1 + h, e2 - h, S3 * (d1 - d2 + d4), (e2 - e1) + h


def nine_real(x):
    r = nine_cos(x[0], x[1] + x[8], x[2] + x[7], x[3] + x[6], x[4] + x[5])
    i = nine_sin(x[1] - x[8], x[2] - x[7], x[3] - x[6], x[4] - x[5])
    return r, (None,) + i


def crt(k1, k2):
    for k in range(ROT):
        if k % 4 == k1 and k % 9 == k2:
            return k
    return None


def forward36(x):
    re, im = [None] * FREQS, [None] * FREQS
    y0, y2, ya, yb = [], [], [], []
    for n2 in range(9):
        v = [x[(9 * n1 + 4 * n2) % ROT] for n1 in range(4)]
        t0, t1 = v[0] + v[2], v[1] + v[3]
        y0.append(t0 + t1)
        y2.append(t0 - t1)
        ya.append(v[0] - v[2])
        yb.append(v[3] - v[1])

    def put(k, real, imag):
        if k <= ROT // 2:
            re[k], im[k] = real, imag
        else:
            re[ROT - k], im[ROT - k] = real, -imag

    for k1, y in ((0, y0), (2, y2)):
        r, i = nine_real(y)
        k = crt(k1, 0)
        re[k] = r[0]
        for k2 in range(1, 5):
            k = crt(k1, k2)
            if k <= ROT // 2:
                re[k], im[k] = r[k2], -i[k2]
            else:
                re[ROT - k], im[ROT - k] = r[k2], i[k2]
    ra, ia = nine_real(ya)
    rb, ib = nine_real(yb)
    put(crt(1, 0), ra[0], rb[0])
    for k2 in range(1, 5):
        put(crt(1, k2), ra[k2] + ib[k2], rb[k2] - ia[k2])
        put(crt(1, 9 - k2), ra[k2] - ib[k2], rb[k2] + ia[k2])
    return re, im


def inverse36(re, im):
    def entry(k):
        if k <= ROT // 2:
            return re[k], im[k], 1
        return re[ROT - k], im[ROT - k], -1

    ys = []
    for k1 in (0, 2):
        real, imag = [entry(crt(k1, 0))[0]], [None]
        for k2 in range(1, 5):
            a, b, sign = entry(crt(k1, k2))
            real.append(a)
            imag.append(b if sign > 0 else -b)
        r = nine_cos(*real)
        i = (None,) + nine_sin(*imag[1:])
        y = [None] * 9
        y[0] = r[0]
        for n in range(1, 5):
            y[n], y[9 - n] = r[n] - i[n], r[n] + i[n]
        ys.append(y)
    xr, xi = [], []
    for k2 in range(9):
        a, b, sign = entry(crt(1, k2))
        xr.append(a)
        xi.append(b if sign > 0 else -b)
    rr, ir = nine_real(xr)
    ri, ii = nine_real(xi)
    ya, yb = [None] * 9, [None] * 9
    ya[0], yb[0] = rr[0], ri[0]
    for n in range(1, 5):
        ya[n], ya[9 - n] = rr[n] - ii[n], rr[n] + ii[n]
        yb[n], yb[9 - n] = ri[n] + ir[n], ri[n] - ir[n]
    x = [None] * ROT
    for n2 in range(9):
        t0, t1 = ys[0][n2] + ys[1][n2], ys[0][n2] - ys[1][n2]
        for n1, value in enumerate((t0 + ya[n2], t1 - yb[n2], t0 - ya[n2], t1 + yb[n2])):
            x[(9 * n1 + 4 * n2) % ROT] = value
    return x


def transform_steps(table_ref, pix_ref, slot_ref, fh_ref, fl_ref, first, count):
    slot = jnp.concatenate([slot_ref[...]] * 2, axis=0)
    nothing = jnp.zeros_like(slot)

    def step(i, _):
        parts = []
        for pair in range(S_STEP // 2):
            x = []
            for b in range(ROT):
                halves = []
                for h in range(2):
                    at = S_STEP * i + 2 * pair + h
                    c = table_ref[at, b : b + 1, :]
                    s = table_ref[at, ROT + b : ROT + b + 1, :]
                    halves.append(pix_ref[0, b] * c + pix_ref[1, b] * s)
                x.append(jnp.concatenate(halves, axis=0).astype(BF).astype(F32))
            re, im = forward36(x)
            im[0], im[ROT // 2] = slot, nothing
            row = pl.multiple_of((first + i) * S_STEP * ROWS8 + 16 * pair, 16)
            low = []
            for q in range(FREQS):
                for part, value in ((0, re[q]), (1, im[q])):
                    hi = value.astype(BF)
                    fh_ref[q, pl.ds(row, 16), part * LANES : (part + 1) * LANES] = hi
                    low.append(value - hi.astype(F32))
            parts.append(low)
        rows = pl.ds(pl.multiple_of((first + i) * S_STEP * ROWS8, S_STEP * ROWS8), S_STEP * ROWS8)
        for n, low in enumerate(zip(*parts)):
            cols = slice((n % 2) * LANES, (n % 2 + 1) * LANES)
            fl_ref[n // 2, rows, cols] = jnp.concatenate(low, axis=0).astype(F8)
        return 0

    lax.fori_loop(0, count, step, 0)


def first_kernel(
    grp_hbm, bin_hbm, img_hbm, sig_hbm, ctf_hbm, exp_hbm, perm_hbm, table_hbm,
    fh_ref, fl_ref, pix_ref, slot_ref, rest_ref,
    grp_ref, bin_ref, img_ref, sig_ref, ctf_ref, exp_ref, perm_ref, table_ref, noise_ref, sems,
):
    moves = [
        (grp_hbm, grp_ref), (bin_hbm, bin_ref), (img_hbm, img_ref), (sig_hbm, sig_ref),
        (ctf_hbm, ctf_ref), (exp_hbm, exp_ref), (perm_hbm, perm_ref),
        (table_hbm.at[pl.ds(0, S_STEP * STEPS_A)], table_ref),
        (table_hbm.at[pl.ds(S_STEP * STEPS_A, S_STEP * STEPS_B)], rest_ref),
    ]
    copies = [pltpu.make_async_copy(a, b, sems.at[i]) for i, (a, b) in enumerate(moves)]
    for copy in copies[:8]:
        copy.start()
    for copy in copies[:7]:
        copy.wait()
    copies[8].start()
    noise_ref[...] = jnp.dot(
        sig_ref[...], exp_ref[...], precision=lax.Precision.HIGHEST, preferred_element_type=F32
    )
    ctf = jnp.concatenate([ctf_ref[pl.ds(bin_ref[i], 1), :] for i in range(ROWS8)], axis=0)
    noise = jnp.concatenate([noise_ref[pl.ds(grp_ref[i], 1), :] for i in range(ROWS8)], axis=0)
    filt = ctf / noise
    weight = ctf * ctf / noise

    img = img_ref[...].astype(F32)
    stack = jnp.concatenate(
        [img[:, BLOCK_COLS * m : BLOCK_COLS * (m + 1)] for m in block_order()], axis=0
    ).astype(BF)
    turned = lax.dot_general(
        perm_ref[...], stack, (((1,), (1,)), ((), ())), preferred_element_type=F32
    )
    sub = lax.broadcasted_iota(jnp.int32, (ROWS8, LANES), 0)
    lane = lax.broadcasted_iota(jnp.int32, (ROWS8, LANES), 1)
    for b in range(ROT):
        y = turned[b * 8 : (b + 1) * 8]
        for t in (1, 2, 4):
            up = pltpu.roll(pltpu.roll(y, t, 0), LANES - t, 1)
            down = pltpu.roll(pltpu.roll(y, 8 - t, 0), t, 1)
            row_bit, lane_bit = (sub & t) != 0, (lane & t) != 0
            y = jnp.where(row_bit == lane_bit, y, jnp.where(row_bit, up, down))
        y = y * filt
        pix_ref[0, b] = y
        pix_ref[1, b] = jnp.where(
            (lane & 32) == 0, pltpu.roll(y, LANES - 32, 1), pltpu.roll(y, 32, 1)
        )

    off = lane & (STEP - 1)
    weight_hi = weight.astype(BF).astype(F32)
    slot_ref[...] = jnp.where(off == 0, weight_hi, jnp.where(off == 1, weight - weight_hi, 0.0))
    copies[7].wait()
    transform_steps(table_ref, pix_ref, slot_ref, fh_ref, fl_ref, 0, STEPS_A)
    copies[8].wait()


def second_kernel(
    fh_in, fl_in, table_ref, pix_ref, slot_ref, table_hbm, mt_hbm, back_hbm,
    fh_ref, fl_ref, mt_ref, back_ref, late_ref, sems,
):
    del fh_in, fl_in
    early = STEPS_A + STEPS_B
    late = table_hbm.at[pl.ds(S_STEP * early, S_PAD - S_STEP * early)]
    moves = [(late, late_ref), (mt_hbm, mt_ref), (back_hbm, back_ref)]
    copies = [pltpu.make_async_copy(a, b, sems.at[i]) for i, (a, b) in enumerate(moves)]
    for copy in copies:
        copy.start()
    transform_steps(table_ref, pix_ref, slot_ref, fh_ref, fl_ref, STEPS_A, STEPS_B)
    copies[0].wait()
    transform_steps(
        late_ref, pix_ref, slot_ref, fh_ref, fl_ref, early, S_PAD // S_STEP - early
    )
    for copy in copies[1:]:
        copy.wait()


VM = pl.BlockSpec(memory_space=pltpu.VMEM)
HB = pl.BlockSpec(memory_space=pltpu.HBM)


def in_hbm(*arrays):
    return [pltpu.with_memory_space_constraint(a, pltpu.HBM) for a in arrays]


def cost(micros):
    return pl.CostEstimate(flops=int(micros * 1e9), bytes_accessed=int(micros * 3e6), transcendentals=0)


def first_features(images, sigma2, ctf_group, defocus_bin):
    feat = (FREQS, ROWS, 2 * LANES)
    return pl.pallas_call(
        first_kernel,
        out_shape=(
            jax.ShapeDtypeStruct(feat, BF),
            jax.ShapeDtypeStruct(feat, F8),
            jax.ShapeDtypeStruct((2, ROT, ROWS8, LANES), F32),
            jax.ShapeDtypeStruct((ROWS8, LANES), F32),
            jax.ShapeDtypeStruct((S_STEP * STEPS_B, 2 * ROT, LANES), F32),
        ),
        in_specs=[HB] * 8,
        out_specs=[VM] * 5,
        scratch_shapes=[
            pltpu.SMEM((ROWS8,), jnp.int32),
            pltpu.SMEM((ROWS8,), jnp.int32),
            pltpu.VMEM(images.shape, BF),
            pltpu.VMEM(sigma2.shape, F32),
            pltpu.VMEM((BINS, LANES), F32),
            pltpu.VMEM((NGROUP, LANES), F32),
            pltpu.VMEM((BLOCK_COLS, BLOCK_COLS), BF),
            pltpu.VMEM((S_STEP * STEPS_A, 2 * ROT, LANES), F32),
            pltpu.VMEM((NGROUP, LANES), F32),
            pltpu.SemaphoreType.DMA((9,)),
        ],
        compiler_params=pltpu.CompilerParams(vmem_limit_bytes=20 * MIB),
        cost_estimate=cost(4.5),
        name="features_first",
    )(*in_hbm(
        ctf_group, defocus_bin, images, sigma2, jnp.asarray(ctf_lanes()),
        jnp.asarray(shell_expand()), jnp.asarray(pixel_perm(), BF), jnp.asarray(phase_lanes()),
    ))


def second_features(hi, lo, table, pix, slot):
    mt = np.stack(split(refs_transform()))
    back = np.stack(split(inverse_transform()))
    return pl.pallas_call(
        second_kernel,
        out_shape=(
            jax.ShapeDtypeStruct(hi.shape, BF),
            jax.ShapeDtypeStruct(lo.shape, F8),
            jax.ShapeDtypeStruct(mt.shape, BF),
            jax.ShapeDtypeStruct(back.shape, BF),
        ),
        in_specs=[VM] * 5 + [HB] * 3,
        out_specs=[VM] * 4,
        scratch_shapes=[
            pltpu.VMEM((S_PAD - S_STEP * (STEPS_A + STEPS_B), 2 * ROT, LANES), F32),
            pltpu.SemaphoreType.DMA((3,)),
        ],
        input_output_aliases={0: 0, 1: 1},
        compiler_params=pltpu.CompilerParams(vmem_limit_bytes=16 * MIB),
        cost_estimate=cost(2.5),
        name="features_second",
    )(
        hi, lo, table, pix, slot,
        *in_hbm(jnp.asarray(phase_lanes()), jnp.asarray(mt), jnp.asarray(back)),
    )


def nt(left, right):
    return lax.dot_general(left, right, (((1,), (1,)), ((), ())), preferred_element_type=F32)


def posterior_kernel(
    direct, r0_ref, r1_ref, r2_ref, r3_ref, s0_ref, s1_ref, s2_ref, s3_ref, fh_ref, fl_ref, mt_ref,
    out_ref, x_ref, d_ref, a_ref, e_ref, ca_ref, cb_ref, ct_ref, sa_ref, sb_ref, st_ref,
    pa_ref, pb_ref, pt_ref, q_ref, num_ref,
):
    lane = lax.broadcasted_iota(jnp.int32, (CLASSES, LANES), 1)
    lane8 = lax.broadcasted_iota(jnp.int32, (8, LANES), 1)
    row8 = lax.broadcasted_iota(jnp.int32, (8, LANES), 0)

    me = lax.axis_index("img") if direct else 0
    blank = jnp.zeros((KPAD - CLASSES, BLOCK_COLS), BF)
    for side, refs in enumerate(((r0_ref, r1_ref, r2_ref, r3_ref), (s0_ref, s1_ref, s2_ref, s3_ref))):
        for g, pair in enumerate(refs):
            for h in range(2):
                row = pl.multiple_of((me ^ (2 * g + 8 * h + side)) * KPAD, KPAD)
                x_ref[pl.ds(row, KPAD), :] = jnp.concatenate([pair[h], blank], axis=0)
    x = x_ref[...]
    d_ref[...] = nt(mt_ref[0], x) + nt(mt_ref[1], x)

    for t in range(BLOCKS // 2):
        cols = slice(t * LANES, (t + 1) * LANES)
        edge = jnp.zeros((8, LANES), F32)
        inner = jnp.zeros((8, LANES), F32)
        for q in range(FREQS):
            re = d_ref[q * 16 : q * 16 + 8, cols]
            if q in (0, ROT // 2):
                edge += re * re
            else:
                im = d_ref[q * 16 + 8 : q * 16 + 16, cols]
                inner += re * re + im * im
        power = -0.5 * (ROT * edge + (ROT // 2) * inner)
        power += pltpu.roll(power, 7, 0)
        power += pltpu.roll(power, 6, 0)
        power = jnp.where((row8 & (STEP - 1)) == 0, power, 0.0)
        d_ref[8:16, cols] = power + pltpu.roll(power, 1, 0)

    def operand(q):
        tile = jnp.concatenate(
            [
                d_ref[q * 16 + part * 8 : q * 16 + part * 8 + 8, t * LANES : (t + 1) * LANES]
                for part in range(2)
                for t in range(BLOCKS // 2)
            ],
            axis=0,
        )
        tile = tile.T
        even, odd = tile[:CLASSES], tile[KPAD : KPAD + CLASSES]
        real = jnp.where(lane < 64, even, pltpu.roll(odd, 64, 1))
        imag = jnp.where(lane < 64, pltpu.roll(even, 64, 1), odd)
        real_hi, imag_hi = real.astype(BF), imag.astype(BF)
        real_lo = (real - real_hi.astype(F32)).astype(BF)
        imag_lo = (imag - imag_hi.astype(F32)).astype(BF)
        for first, re, im in ((0, real_hi, imag_hi), (2 * CLASSES, real_lo, imag_lo)):
            a_ref[q, first : first + CLASSES, :LANES] = re
            a_ref[q, first : first + CLASSES, LANES:] = im
            a_ref[q, first + CLASSES : first + 2 * CLASSES, :LANES] = -im
            a_ref[q, first + CLASSES : first + 2 * CLASSES, LANES:] = re
        left = [jnp.concatenate([real, imag], axis=1), jnp.concatenate([-imag, real], axis=1)]
        e_ref[q] = jnp.concatenate(left, axis=0).astype(F8)

    tiles_k = CLASSES // 8

    def cross(q, rows):
        both = a_ref[q]
        first = nt(both, fh_ref[q, rows])
        return first[: 2 * CLASSES] + first[2 * CLASSES :] + nt(e_ref[q], fl_ref[q, rows])

    def cross_first(q):
        total = cross(q, slice(0, GROUP))
        if q + 1 < FREQS:
            operand(q + 1)
        ca_ref[2 * q] = total[:CLASSES]
        ca_ref[2 * q + 1] = total[CLASSES:]

    def cross_second(q):
        total = cross(q, slice(GROUP, ROWS))
        cb_ref[2 * q] = total[:CLASSES, : TAIL - GROUP]
        cb_ref[2 * q + 1] = total[CLASSES:, : TAIL - GROUP]
        last = total[:, TAIL - GROUP : TAIL - GROUP + TAIL_ROWS]
        last = jnp.concatenate([last, jnp.zeros((2 * CLASSES, LANES - TAIL_ROWS), F32)], axis=1)
        for part in range(2):
            packed = last[part * CLASSES : part * CLASSES + 8]
            for kt in range(1, tiles_k):
                row = part * CLASSES + kt * 8
                packed += pltpu.roll(last[row : row + 8], kt * TAIL_ROWS, 1)
            ct_ref[2 * q + part] = packed

    def tiles_of(c_ref, s_ref, p_ref):
        return [
            (c_ref, s_ref, p_ref, slice(row, row + 8), slice(col, col + LANES))
            for col in range(0, c_ref.shape[2], LANES)
            for row in range(0, c_ref.shape[1], 8)
        ]

    packed_live = ((lane8 & (TAIL_ROWS - 1)) < LIVE - TAIL) & (lane8 < tiles_k * TAIL_ROWS)

    def to_scores(where, top):
        c_ref, s_ref, _, rows, cols = where
        re = [c_ref[2 * q, rows, cols] for q in range(FREQS)]
        im = [None] + [c_ref[2 * q + 1, rows, cols] for q in range(1, FREQS - 1)] + [None]
        if c_ref is ct_ref:
            re[0] = jnp.where(packed_live, re[0], -1e30)
        x = inverse36(re, im)
        for r in range(ROT):
            s_ref[r, rows, cols] = x[r]
        while len(x) > 1:
            x = [jnp.maximum(*x[i : i + 2]) if i + 1 < len(x) else x[i] for i in range(0, len(x), 2)]
        return x[0] if top is None else jnp.maximum(top, x[0])

    def fold(v, op):
        for t in (4, 2, 1):
            v = op(v, pltpu.roll(v, t, 0))
        for t in (64, 32, 16, 8):
            v = op(v, pltpu.roll(v, t, 1))
        return v

    def to_posterior(where, top, total):
        _, s_ref, p_ref, rows, cols = where
        x = [jnp.exp(s_ref[r, rows, cols] - top) for r in range(ROT)]
        re, im = forward36(x)
        for q in range(FREQS):
            p_ref[2 * q, rows, cols] = re[q]
            if im[q] is not None:
                p_ref[2 * q + 1, rows, cols] = im[q]
        return re[0] if total is None else total + re[0]

    operand(0)
    for q in range(FREQS):
        cross_first(q)
        cross_second(q)
    tiles_a = tiles_of(ca_ref, sa_ref, pa_ref)
    tiles_b = tiles_of(cb_ref, sb_ref, pb_ref) + tiles_of(ct_ref, st_ref, pt_ref)
    top_a = total_a = top_b = total_b = None
    for where in tiles_b:
        top_b = to_scores(where, top_b)
    top_b = fold(top_b, jnp.maximum)
    for where in tiles_b:
        total_b = to_posterior(where, top_b, total_b)
    for where in tiles_a:
        top_a = to_scores(where, top_a)
    top_a = fold(top_a, jnp.maximum)
    for where in tiles_a:
        total_a = to_posterior(where, top_a, total_a)
    top = jnp.maximum(top_a, top_b)
    part_a, part_b = jnp.exp(top_a - top), jnp.exp(top_b - top)
    inverse = 1.0 / (part_a * fold(total_a, jnp.add) + part_b * fold(total_b, jnp.add))
    scale_a, scale_b = (part_a * inverse)[:1], (part_b * inverse)[:1]

    def scaled(q):
        for part in range(2):
            rows = slice(part * CLASSES, (part + 1) * CLASSES)
            if part == 1 and q in (0, ROT // 2):
                q_ref[q, rows, :] = jnp.zeros((CLASSES, COLS), BF)
                continue
            slot = 2 * q + part
            for col in range(0, GROUP, LANES):
                value = pa_ref[slot, :, col : col + LANES] * scale_a
                q_ref[q, rows, col : col + LANES] = value.astype(BF)
            q_ref[q, rows, GROUP:TAIL] = (pb_ref[slot] * scale_b).astype(BF)
            packed = jnp.where(packed_live, pt_ref[slot] * scale_b, 0.0)
            last = [packed] + [
                pltpu.roll(packed, LANES - kt * TAIL_ROWS, 1) for kt in range(1, tiles_k)
            ]
            last = jnp.where(lane < TAIL_ROWS, jnp.concatenate(last, axis=0), 0.0)
            q_ref[q, rows, TAIL:] = last.astype(BF)

    third = 2 * CLASSES // 3
    order = [4 * quad + slot for quad in range(QUADS) for slot in (3, 0, 1, 2)]
    order = [q for q in order if q < FREQS]
    extra = jnp.zeros((2 * CLASSES, LANES), F32)
    scaled(order[0])
    for n, q in enumerate(order):
        o = jnp.dot(q_ref[q, :, :ROWS], fh_ref[q], preferred_element_type=F32)
        if n + 1 < len(order):
            scaled(order[n + 1])
        real = o[:CLASSES, :LANES] + o[CLASSES:, LANES:]
        imag = o[:CLASSES, LANES:] - o[CLASSES:, :LANES]
        both = jnp.concatenate([real, imag], axis=0)
        quad, slot = q // 4, q % 4
        if slot == 3:
            extra = both
            continue
        if 4 * quad + 3 >= FREQS:
            extra = jnp.zeros((2 * CLASSES, LANES), F32)
        tile = [both, extra[slot * third : (slot + 1) * third]]
        num_ref[slot * QUADS + quad] = jnp.concatenate(tile, axis=0).T
    core, chip = me % 2, me // 2
    for half in range(2):
        side = (1 - core) if half == 0 else core
        for e in range(BLOCKS // 2):
            row = side * (LANES // 2) + (chip ^ (e // 2 + 4 * (e % 2))) * ROWS8
            row = pl.multiple_of(row, ROWS8)
            out_ref[half, e] = num_ref[:, pl.ds(row, 8), :].reshape(PAY, LANES).astype(BF)


def make_payload(direct, refs, feat_hi, feat_lo, mt):
    return pl.pallas_call(
        functools.partial(posterior_kernel, direct),
        out_shape=jax.ShapeDtypeStruct((2, BLOCKS // 2, PAY, LANES), BF),
        in_specs=[VM] * 11,
        out_specs=VM,
        scratch_shapes=[
            pltpu.VMEM((BLOCKS * KPAD, BLOCK_COLS), BF),
            pltpu.VMEM((FREQS * 16, BLOCKS * KPAD), F32),
            pltpu.VMEM((FREQS, 4 * CLASSES, 2 * LANES), BF),
            pltpu.VMEM((FREQS, 2 * CLASSES, 2 * LANES), F8),
            pltpu.VMEM((2 * FREQS, CLASSES, GROUP), F32),
            pltpu.VMEM((2 * FREQS, CLASSES, TAIL - GROUP), F32),
            pltpu.VMEM((2 * FREQS, 8, LANES), F32),
            pltpu.VMEM((ROT, CLASSES, GROUP), F32),
            pltpu.VMEM((ROT, CLASSES, TAIL - GROUP), F32),
            pltpu.VMEM((ROT, 8, LANES), F32),
            pltpu.VMEM((2 * FREQS, CLASSES, GROUP), F32),
            pltpu.VMEM((2 * FREQS, CLASSES, TAIL - GROUP), F32),
            pltpu.VMEM((2 * FREQS, 8, LANES), F32),
            pltpu.VMEM((FREQS, 2 * CLASSES, COLS), BF),
            pltpu.VMEM((TILES, LANES, LANES), F32),
        ],
        compiler_params=pltpu.CompilerParams(vmem_limit_bytes=28 * MIB),
        cost_estimate=cost(10.0),
        name="posterior",
    )(*refs, feat_hi, feat_lo, mt)


def final_kernel(keep_ref, got_ref, back_ref, out_ref):
    total = keep_ref[...] + got_ref[...].astype(F32)
    total = jnp.concatenate([total, jnp.zeros((LANES - PAY, LANES), F32)], axis=0)
    turned = total.T
    width = QUADS * ROWS8
    rest = turned[2 * CLASSES :]
    last = [rest] + [pltpu.roll(rest, LANES - slot * width, 1) for slot in (1, 2)]
    last = jnp.concatenate(last, axis=0)
    column = lax.broadcasted_iota(jnp.int32, last.shape, 1)
    last = jnp.where(column < width, last, 0.0)
    parts = [v[rows] for v in (turned, last) for rows in (slice(0, CLASSES), slice(CLASSES, 2 * CLASSES))]
    value = jnp.concatenate(parts, axis=1)
    hi = value.astype(BF)
    lo = (value - hi.astype(F32)).astype(BF)
    dot = functools.partial(jnp.dot, preferred_element_type=F32)
    both = dot(jnp.concatenate([hi, lo], axis=0), back_ref[0])
    numer = both[:CLASSES] + both[CLASSES:] + dot(hi, back_ref[1])
    weights = turned[CLASSES : 2 * CLASSES]
    column = lax.broadcasted_iota(jnp.int32, (CLASSES, BLOCK_COLS), 1)
    first = weights[:, 0:1] + weights[:, 1:2]
    second = weights[:, STEP : STEP + 1] + weights[:, STEP + 1 : STEP + 2]
    out_ref[...] = numer / (jnp.where(column < ANG, first, second) + 1.0)


def finish(keep, got, back):
    return pl.pallas_call(
        final_kernel,
        out_shape=jax.ShapeDtypeStruct((CLASSES, BLOCK_COLS), F32),
        in_specs=[VM] * 3,
        out_specs=VM,
        compiler_params=pltpu.CompilerParams(vmem_limit_bytes=8 * MIB),
        cost_estimate=cost(1.0),
        name="finish",
    )(keep, got, back)


def swap(value, distance):
    pairs = [(i, i ^ distance) for i in range(lax.axis_size("img"))]
    return lax.ppermute(value, "img", pairs)


def reduce_direct(pay):
    pairs = pay[1].astype(F32) + swap(pay[0], 1).astype(F32)
    pairs = pairs.reshape((4, BLOCKS // 8) + pairs.shape[1:])
    parts = [swap(pairs[g].astype(BF), 2 * g) for g in (1, 2, 3)]
    total = pairs[0]
    for part in parts:
        total = total + part.astype(F32)
    return total[0], swap(total[1].astype(BF), 8)


def on_device(images, class_refs, sigma2, ctf_group, defocus_bin):
    devices = lax.axis_size("img")
    share = class_refs.shape[1]
    me = lax.axis_index("img")
    direct = devices == BLOCKS and share == BLOCK_COLS
    if direct:
        near = swap(class_refs, 8)
    else:
        whole = lax.all_gather(class_refs, "img", axis=1, tiled=True)
        blocks = whole.reshape(CLASSES, BLOCKS, BLOCK_COLS).transpose(1, 0, 2)
        refs = [jnp.stack([blocks[2 * g + s], blocks[2 * g + s + 8]]) for s in range(2) for g in range(4)]
    pay = None
    for first in range(0, images.shape[0], ROWS8):
        part = slice(first, first + ROWS8)
        hi, lo, pix, slot, table = first_features(
            images[part], sigma2, ctf_group[part], defocus_bin[part]
        )
        if direct and first == 0:
            near, hi = lax.optimization_barrier((near, hi))
            near = jnp.stack([class_refs, near])
            rest = [swap(near, 2 * g) for g in (1, 2, 3)]
        hi, lo, mt, back = second_features(hi, lo, table, pix, slot)
        if direct and first == 0:
            other = [swap(near, 1)]
            other[0], hi = lax.optimization_barrier((other[0], hi))
            for g in range(3):
                rest[g], hi = lax.optimization_barrier((rest[g], hi))
                other.append(swap(rest[g], 1))
            refs = [near] + rest + other
        one = make_payload(direct, refs, hi, lo, mt)
        pay = one if pay is None else pay + one
    if direct:
        return finish(*reduce_direct(pay), back)
    summed = lax.psum(pay.astype(F32), "img")
    start = me * share
    block = start // BLOCK_COLS
    chip = block // 2
    mine = summed[1 - block % 2, 2 * (chip % 4) + chip // 4]
    return lax.dynamic_slice_in_dim(
        finish(mine, jnp.zeros_like(mine, BF), back), start % BLOCK_COLS, share, 1
    )


def solution(mesh):
    in_specs = (
        P(("groups", "img"), None),
        P("groups", "img"),
        P("groups", None),
        P(("groups", "img")),
        P(("groups", "img")),
    )
    out_specs = P("groups", "img")
    return jax.shard_map(
        on_device, mesh=mesh, in_specs=in_specs, out_specs=out_specs, check_vma=False
    )
```
